512 devices in a mesh: board: 32 (over z, y_lo), depth: 4 (over y_hi, core), hand: 4 (over x).
Axes of the slice: x: 4, y: 4 (y_hi: 2, y_lo: 2; y = y_hi * 2 + y_lo), z: 16, core: 2. Of those that a mesh axis runs over, the one named last changes fastest.
Arguments:
- reach: bfloat16 [256, 1536, 1024], P('board', 'hand', 'depth'), may hold values from 0 to 1
- payoff: bfloat16 [1024, 1024], P('depth'), may hold values from -2.670288e-05 to 2.670288e-05
- board_cards: int32 [256, 5], P('board'), may hold values from 0 to 51, as said below
- hand_rank: int32 [256, 1326], P('board'), may hold values from 0 to 7461
- logits: float32 [1536, 1024], P('hand', 'depth'), may hold values from -8 to 310, as said below
- action_counts: int32 [4, 64], replicated, may hold values from 2 to 4
- parent_seq: int32 [4, 64], replicated, may hold values from 0 to 253, as said below
Outputs:
- log_policy: float32 [1536, 1024], P('hand', 'depth')
- parent_values: float32 [1536, 1024], P('hand', 'depth')
The draws below stay inside these ranges and needn't reach their ends.
Inputs may be any that keep to these rules, and one draw needn't show every extreme that they name: `board_cards`: each row holds five different cards. `logits`: entries are finite; in some draws a few scores are very large. `parent_seq`: each entry names a legal action slot of the level above: its remainder modulo 4 is 0 or 1.
All inputs are finite; a program needn't handle non-finite values.
Results may differ from the reference program's by a relative error of at most 0.0003.
Values may be sent and summed in bfloat16 or wider, within the bound.
A program may use at most 64 MiB of HBM per device.

```python
import jax
import jax.numpy as jnp
import numpy as np
from jax import lax

CARDS = 52
HANDS = 1326
HP = 1536
SEQ_LEV = 256
ACT = 4
NINFO = 64
LEVELS = 4
SX = 1024
OPP_SEQ = 1024
RANK_CLASSES = 7462
BOARDS = 256


def draw_board_cards(key, part):
    key = jax.random.fold_in(key, 7)
    rows_key, first_key = jax.random.split(key)
    keys = jax.random.split(rows_key, BOARDS)
    picked = jax.vmap(lambda single: jax.random.permutation(single, CARDS)[:5])(keys).astype(jnp.int32)
    middle = (1 + jax.random.permutation(first_key, CARDS - 2)[:3]).astype(jnp.int32)
    opening = jnp.concatenate([jnp.zeros((1,), jnp.int32), middle, jnp.full((1,), CARDS - 1, jnp.int32)])
    return picked.at[0].set(opening)


def draw_logits(key, part):
    key = jax.random.fold_in(key, 5)
    first_key = jax.random.fold_in(key, 0)
    base = jnp.clip(jax.random.normal(first_key, (HP, SX), jnp.float32) * 1.5, -8.0, 8.0)
    return base


def draw_parent_seq(key, part):
    key = jax.random.fold_in(key, 11)
    info_key, slot_key = jax.random.split(key)
    points = SEQ_LEV // ACT
    info = jax.random.randint(info_key, (LEVELS, points), 0, points)
    slot = jax.random.randint(slot_key, (LEVELS, points), 0, 2)
    flat = jnp.arange(LEVELS * points, dtype=jnp.int32).reshape(LEVELS, points)
    info = jnp.where(flat == 0, 0, jnp.where(flat == LEVELS * points - 1, points - 1, info))
    slot = jnp.where(flat == 0, 0, jnp.where(flat == LEVELS * points - 1, 1, slot))
    return (info * ACT + slot).astype(jnp.int32)


def with_ends(array, stream_key, least, high):
    shape = array.shape
    place = [jax.random.randint(jax.random.fold_in(stream_key, axis), (), 0, shape[axis]) for axis in range(len(shape))]
    array = array.at[tuple(place)].set(least)
    longest = shape.index(max(shape))
    place[longest] = (place[longest] + 1) % shape[longest]
    return array.at[tuple(place)].set(high)


def shard_levels(stream_key, dims, pieces, smallest, largest):
    gain, own = 1.0, jax.random.fold_in(stream_key, 6)
    for position, shards_of in pieces:
        draws = jnp.exp(jax.random.uniform(jax.random.fold_in(own, position), (shards_of,), jnp.float32, smallest / len(pieces), largest / len(pieces)))
        gain = gain * jnp.repeat(draws, dims[position] // shards_of).reshape([-1 if axis == position else 1 for axis in range(len(dims))])
    return gain


def normal_values(own_key, dims, spread, bound, pieces=(), kind=jnp.bfloat16):
    result = spread * jax.random.normal(own_key, dims, jnp.float32)
    if pieces:
        result = result * shard_levels(own_key, dims, pieces, -0.22, 0.18)
    return jnp.clip(result, -bound, bound).astype(kind)


def setup_inputs(seed: int = 0) -> dict:
    key_of = jax.random.split(jax.random.key(seed), 8)
    return {
        "reach": jnp.clip(1.0 * jax.random.uniform(key_of[0], (BOARDS, HP, OPP_SEQ), jnp.float32) ** shard_levels(key_of[0], (BOARDS, HP, OPP_SEQ), ((0, 32), (1, 4), (2, 4)), -0.2, 0.2), 0.0, 1.0).astype(jnp.bfloat16),
        "payoff": normal_values(key_of[1], (OPP_SEQ, SX), (OPP_SEQ * BOARDS * HANDS * HANDS // 8) ** -0.5, 2.6702880859375e-05, ((0, 4),)),
        "board_cards": draw_board_cards(jax.random.fold_in(key_of[7], 71), 0),
        "hand_rank": with_ends(jax.random.randint(key_of[3], (BOARDS, HANDS), 0, RANK_CLASSES), jax.random.fold_in(key_of[3], 1), 0, RANK_CLASSES - 1).astype(jnp.int32),
        "logits": draw_logits(jax.random.fold_in(key_of[7], 71), 0),
        "action_counts": with_ends(jax.random.randint(key_of[5], (LEVELS, NINFO), 2, 5), jax.random.fold_in(key_of[5], 1), 2, 4).astype(jnp.int32),
        "parent_seq": draw_parent_seq(jax.random.fold_in(key_of[7], 71), 0),
    }


def hand_table(slots):
    first, second = np.triu_indices(CARDS, 1)
    pad = slots - first.shape[0]
    first = np.concatenate([first, np.full(pad, -1)])
    second = np.concatenate([second, np.full(pad, -2)])
    return jnp.asarray(first, jnp.int32), jnp.asarray(second, jnp.int32)


def hand_valid(cards, first, second, real):
    hit_first = jnp.any(first[None, :, None] == cards[:, None, :], axis=2)
    hit_second = jnp.any(second[None, :, None] == cards[:, None, :], axis=2)
    return real[None, :] & jnp.logical_not(hit_first) & jnp.logical_not(hit_second)


def showdown_block(valid_rows, valid_cols, rank_rows, rank_cols, first_rows, second_rows, first_cols, second_cols):
    apart = (first_rows[:, None] != first_cols[None, :]) & (first_rows[:, None] != second_cols[None, :])
    apart = apart & (second_rows[:, None] != first_cols[None, :]) & (second_rows[:, None] != second_cols[None, :])
    signs = jnp.sign(rank_rows[:, :, None] - rank_cols[:, None, :]).astype(jnp.float32)
    live = valid_rows[:, :, None] & valid_cols[:, None, :] & apart[None]
    return jnp.where(live, signs, jnp.float32(0.0)).astype(jnp.bfloat16)


def prox_level(scores, counts, parents):
    rows = scores.shape[0]
    levels_seq = scores.shape[1]
    grouped = scores.reshape(rows, levels_seq // ACT, ACT)
    legal = jnp.arange(ACT, dtype=jnp.int32)[None, :] < counts[:, None]
    masked = jnp.where(legal[None], grouped, -jnp.inf)
    top = jnp.max(masked, axis=2, keepdims=True)
    total = jnp.sum(jnp.exp(masked - top), axis=2, keepdims=True)
    value = top + jnp.log(total)
    policy = jnp.where(legal[None], grouped - value, jnp.float32(0.0)).reshape(rows, levels_seq)
    owner = (parents[:, None] == jnp.arange(levels_seq, dtype=jnp.int32)[None, :]).astype(scores.dtype)
    passed = jnp.dot(value[:, :, 0], owner, precision=lax.Precision.HIGHEST)
    return policy, passed


def reference(reach, payoff, board_cards, hand_rank, logits, action_counts, parent_seq):
    first, second = hand_table(HP)
    real = jnp.arange(HP, dtype=jnp.int32) < HANDS
    ranks = jnp.pad(hand_rank, ((0, 0), (0, HP - HANDS)))
    payoff_wide = payoff.astype(jnp.float32)

    def one_board(total, inputs):
        cards, rank, reach_b = inputs
        valid = hand_valid(cards[None], first, second, real)
        block = showdown_block(valid, valid, rank[None], rank[None], first, second, first, second)[0]
        counter = jnp.dot(block, reach_b, preferred_element_type=jnp.float32)
        return total + jnp.dot(counter, payoff_wide, precision=lax.Precision.HIGHEST), None

    gradient, _ = lax.scan(one_board, jnp.zeros((HP, SX), jnp.float32), (board_cards, ranks, reach))
    incoming = jnp.zeros((HP, SEQ_LEV), jnp.float32)
    policies = []
    values = []
    for level in reversed(range(LEVELS)):
        cols = slice(level * SEQ_LEV, (level + 1) * SEQ_LEV)
        scores = logits[:, cols] + gradient[:, cols] + incoming
        policy, passed = prox_level(scores, action_counts[level], parent_seq[level])
        policies.insert(0, policy)
        values.insert(0, passed)
        incoming = passed
    return jnp.concatenate(policies, axis=1), jnp.concatenate(values, axis=1)
```

```python
import jax
import jax.numpy as jnp
import numpy as np
from jax import lax
from jax.experimental import pallas as pl
from jax.experimental.pallas import tpu as pltpu
from jax.sharding import PartitionSpec as P

CARDS = 52
HANDS = 1326
ACT = 4
NZ = 16
NX = 4
NL = 4
NJ = 8
HX = 384
HP = NX * HX
HJ = HX // NJ
HZ = HJ // NZ
SL = 256
SX = NL * SL
NB = 8
BOUND = float(NB * HX)
SCALE = 32767.0 / BOUND
MESH = pl.DeviceIdType.MESH
NAN = float("nan")


def hand_cards():
    first, second = np.triu_indices(CARDS, 1)
    table = np.full((8, HP), -1.0, np.float32)
    table[0, :HANDS] = first
    table[1, :HANDS] = second
    onehot = np.zeros((HP, 128), np.float32)
    onehot[np.arange(HANDS), first] = 1.0
    onehot[np.arange(HANDS), second] = 1.0
    return table, onehot


def dot_t(a, b):
    return lax.dot_general(a, b, (((1,), (1,)), ((), ())), preferred_element_type=jnp.float32)


def group_reduce(x, op):
    lane = lax.broadcasted_iota(jnp.int32, x.shape, 1)
    near = jnp.where(lane % 2 == 0, pltpu.roll(x, 127, 1), pltpu.roll(x, 1, 1))
    x = op(x, near)
    far = jnp.where(lane % 4 < 2, pltpu.roll(x, 126, 1), pltpu.roll(x, 2, 1))
    return op(x, far)


def group_value(scores, legal):
    parts = []
    for half in range(2):
        cols = slice(half * 128, half * 128 + 128)
        masked = jnp.where(legal[:, cols] > 0.0, scores[:, cols], -jnp.inf)
        top = group_reduce(masked, jnp.maximum)
        total = group_reduce(jnp.exp(masked - top), jnp.add)
        parts.append(top + jnp.log(total))
    return jnp.concatenate(parts, axis=1)


def hand_down(value, owner_t):
    a = value.astype(jnp.bfloat16)
    rest = value - a.astype(jnp.float32)
    b = rest.astype(jnp.bfloat16)
    c = (rest - b.astype(jnp.float32)).astype(jnp.bfloat16)
    return dot_t(a, owner_t) + dot_t(b, owner_t) + dot_t(c, owner_t)


def kernel(
    reach,
    payoff,
    cards,
    rank,
    logits,
    counts,
    parents,
    table,
    onehot,
    policy,
    passed,
    ranks,
    ranks_t,
    out1,
    in1,
    out2,
    in2,
    rows8,
    logit8,
    pay,
    logit_rows,
    logit_tiles,
    out3,
    in3,
    out4,
    in4,
    legal,
    owners,
    send1,
    recv1,
    send2,
    recv2,
    send3,
    recv3,
    send4,
    recv4,
    send_p,
    recv_p,
    send_l,
    recv_l,
):
    board = lax.axis_index("board")
    depth = lax.axis_index("depth")
    x = lax.axis_index("hand")
    z = board // 2
    y_lo = board % 2
    j = y_lo * NL + depth

    def device(to_z, to_j, to_x):
        return (to_z * 2 + to_j // NL, to_j % NL, to_x)

    def copy(src, dst, send, recv, to):
        return pltpu.make_async_remote_copy(
            src_ref=src, dst_ref=dst, send_sem=send, recv_sem=recv, device_id=to, device_id_type=MESH
        )

    barrier = pltpu.get_barrier_semaphore()

    @pl.loop(1, NX * NJ)
    def _(step):
        other = (x * NJ + j + step) % (NX * NJ)
        pl.semaphore_signal(barrier, inc=1, device_id=device(z, other % NJ, other // NJ), device_id_type=MESH)

    @pl.loop(1, NZ)
    def _(step):
        pl.semaphore_signal(barrier, inc=1, device_id=device((z + step) % NZ, j, x), device_id_type=MESH)

    ranks[...] = jnp.full((NB, HP), NAN, jnp.float32)
    ranks[:, :HANDS] = rank[...].astype(jnp.float32)
    first = table[0:1, :]
    second = table[1:2, :]
    hit = first < 0.0
    for card in range(5):
        one = cards[:, card : card + 1].astype(jnp.float32)
        hit = hit | (first == one) | (second == one)
    ranks[...] = jnp.where(hit, NAN, ranks[...])
    ranks_t[...] = ranks[...].T

    own = pl.ds(pl.multiple_of(x * HX, HX), HX)

    def partial(to_x):
        rows = pl.ds(pl.multiple_of(to_x * HX, HX), HX)
        shared = dot_t(onehot[rows, :], onehot[own, :])
        apart = jnp.where(shared > 0.0, 0.0, 1.0)
        minus = -apart
        total = jnp.zeros((HX, SL), jnp.float32)
        for pair in range(NB // 2):
            sides = []
            for b in (2 * pair, 2 * pair + 1):
                mine = ranks_t[rows, b : b + 1]
                theirs = ranks[b : b + 1, own]
                sign = jnp.where(theirs < mine, apart, jnp.where(theirs > mine, minus, 0.0))
                sides.append(sign.astype(jnp.bfloat16))
            total += jnp.dot(
                jnp.concatenate(sides, axis=1),
                reach[2 * HX * pair : 2 * HX * (pair + 1), :],
                preferred_element_type=jnp.float32,
            )
        return jnp.round(total * SCALE).astype(jnp.int32).astype(jnp.int16)

    out1[0] = partial((x + 2) % NX).reshape(NJ, HJ, SL)
    pl.semaphore_wait(barrier, NX * NJ - 1 + NZ - 1)

    me1 = depth * NJ + x * 2 + y_lo

    def send_chunk(i):
        to_x = (x + 2 + i) % NX

        @pl.loop(0, NJ)
        def _(to_j):
            copy(
                out1.at[i, to_j], in1.at[me1], send1.at[i, to_j], recv1.at[me1], device(z, to_j, to_x)
            ).start()

    send_chunk(0)

    for i in (1, 3):
        out1[i] = partial((x + 2 + i) % NX).reshape(NJ, HJ, SL)
        send_chunk(i)
    out1[2] = partial(x).reshape(NJ, HJ, SL)

    @pl.loop(1, NJ)
    def _(step):
        to_j = (j + step) % NJ
        copy(out1.at[2, to_j], in1.at[me1], send1.at[2, to_j], recv1.at[me1], device(z, to_j, x)).start()

    in1[me1] = out1[2, j]

    def depth_peer(step):
        return (depth + step) % NL

    for step in range(1, NL):
        to = y_lo * NL + depth_peer(step)
        copy(
            logits.at[pl.ds(pl.multiple_of(to * HJ, HJ), HJ)],
            logit_rows.at[depth],
            send_l.at[step],
            recv_l.at[depth],
            device(z, to, x),
        ).start()
    logit_rows[depth] = logits[pl.ds(pl.multiple_of(j * HJ, HJ), HJ), :]
    pay[depth] = payoff[...]
    across = depth_peer(2)
    beside = depth + 1 - 2 * (depth % 2)
    opposite = across + 1 - 2 * (across % 2)
    pay_across = copy(payoff, pay.at[depth], send_p.at[0], recv_p.at[depth], device(z, y_lo * NL + across, x))
    pay_across.start()
    pay_beside = copy(payoff, pay.at[depth], send_p.at[1], recv_p.at[depth], device(z, y_lo * NL + beside, x))
    pay_beside.start()

    spread = (
        lax.broadcasted_iota(jnp.int32, (SL // ACT, SL), 0)
        == lax.broadcasted_iota(jnp.int32, (SL // ACT, SL), 1) // ACT
    ).astype(jnp.bfloat16)
    lane = lax.broadcasted_iota(jnp.int32, (NL, SL), 1) % ACT
    counts_wide = jnp.dot(
        counts[...].astype(jnp.float32).astype(jnp.bfloat16), spread, preferred_element_type=jnp.float32
    )
    parents_wide = jnp.dot(
        parents[...].astype(jnp.float32).astype(jnp.bfloat16), spread, preferred_element_type=jnp.float32
    )
    legal[...] = jnp.where(lane.astype(jnp.float32) < counts_wide, 1.0, 0.0)
    parents_wide = jnp.where(lane == 0, parents_wide, -1.0)
    seq = lax.broadcasted_iota(jnp.int32, (SL, SL), 0).astype(jnp.float32)
    for level in range(NL):
        owners[level] = jnp.where(seq == parents_wide[level : level + 1, :], 1.0, 0.0).astype(jnp.bfloat16)

    @pl.loop(1, NX * NJ)
    def _(step):
        slot = (me1 + step) % (NX * NJ)
        copy(in1.at[slot], in1.at[slot], send1.at[0, 0], recv1.at[slot], device(z, (j + 1) % NJ, x)).wait_recv()

    for block in range(NL):
        total = in1[block * NJ].astype(jnp.int32)
        for source in range(1, NJ):
            total += in1[block * NJ + source].astype(jnp.int32)
        total = total.astype(jnp.float32)
        out2[:, 2 * block, :] = total[:, :128]
        out2[:, 2 * block + 1, :] = total[:, 128:]

    @pl.loop(1, NZ)
    def _(step):
        to_z = (z + step) % NZ
        copy(
            out2.at[pl.ds(to_z * HZ, HZ)], in2.at[z], send2.at[step], recv2.at[z], device(to_z, j, x)
        ).start()

    in2[z] = out2[pl.ds(z * HZ, HZ)]

    copy(payoff, pay.at[across], send_p.at[0], recv_p.at[across], device(z, (j + 1) % NJ, x)).wait_recv()
    pay_on = copy(
        pay.at[across], pay.at[across], send_p.at[2], recv_p.at[across], device(z, y_lo * NL + beside, x)
    )
    pay_on.start()
    copy(payoff, pay.at[beside], send_p.at[0], recv_p.at[beside], device(z, (j + 1) % NJ, x)).wait_recv()
    copy(payoff, pay.at[opposite], send_p.at[0], recv_p.at[opposite], device(z, (j + 1) % NJ, x)).wait_recv()

    rows8[...] = jnp.zeros((8, SX), jnp.float32)
    logit8[...] = jnp.zeros((8, SX), jnp.float32)
    for step in range(1, NL):
        slot = depth_peer(step)
        copy(
            logit_rows.at[slot], logit_rows.at[slot], send_l.at[0], recv_l.at[slot], device(z, (j + 1) % NJ, x)
        ).wait_recv()
    for group in range(8):
        logit_tiles[:, group, :] = logit_rows[group // 2, :, (group % 2) * 128 : (group % 2) * 128 + 128]
    for group in range(8):
        logit8[0:HZ, group * 128 : (group + 1) * 128] = logit_tiles[pl.ds(z * HZ, HZ), group, :]

    @pl.loop(1, NZ)
    def _(step):
        slot = (z + step) % NZ
        copy(in2.at[slot], in2.at[slot], send2.at[0], recv2.at[slot], device(slot, j, x)).wait_recv()

    total = in2[0]
    for source in range(1, NZ):
        total += in2[source]
    in2[0] = total
    for group in range(8):
        rows8[0:HZ, group * 128 : (group + 1) * 128] = in2[0, :, group, :]
    counter = rows8[...]
    high = counter.astype(jnp.bfloat16).astype(jnp.float32)
    both = jnp.concatenate([high, counter - high], axis=0).astype(jnp.bfloat16)
    gradient = jnp.dot(both[:, :SL], pay[0], preferred_element_type=jnp.float32)
    for block in range(1, NL):
        gradient += jnp.dot(
            both[:, block * SL : (block + 1) * SL], pay[block], preferred_element_type=jnp.float32
        )
    gradient = (gradient[:8] + gradient[8:]) * (1.0 / SCALE)

    incoming = jnp.zeros((8, SL), jnp.float32)
    for level in range(NL - 1, -1, -1):
        cols = slice(level * SL, (level + 1) * SL)
        shift = gradient[:, cols] + incoming
        out3[:, 2 * level, :] = shift[:HZ, :128]
        out3[:, 2 * level + 1, :] = shift[:HZ, 128:]
        if level:
            value = group_value(logit8[:, cols] + shift, legal[level : level + 1, :])
            incoming = hand_down(value, owners[level])

    @pl.loop(1, NZ)
    def _(step):
        to_z = (z + step) % NZ
        copy(out3, in3.at[z], send3.at[step], recv3.at[z], device(to_z, j, x)).start()

    in3[z] = out3[...]

    @pl.loop(1, NZ)
    def _(step):
        slot = (z + step) % NZ
        copy(in3.at[slot], in3.at[slot], send3.at[0], recv3.at[slot], device(slot, j, x)).wait_recv()

    shifts = in3[...].reshape(HJ, 8, 128)
    for level in range(NL):
        out4[level, :, :128] = shifts[:, 2 * level, :]
        out4[level, :, 128:] = shifts[:, 2 * level + 1, :]

    @pl.loop(1, NJ)
    def _(step):
        to_j = (j + step) % NJ
        copy(out4.at[to_j % NL], in4.at[j], send4.at[step], recv4.at[j], device(z, to_j, x)).start()

    in4[j] = out4[depth]

    @pl.loop(1, NJ)
    def _(step):
        slot = (j + step) % NJ
        copy(in4.at[slot], in4.at[slot], send4.at[0], recv4.at[slot], device(z, slot, x)).wait_recv()

    scores = logits[...] + in4[...].reshape(HX, SL)
    can = legal[pl.ds(depth, 1), :]
    value = group_value(scores, can)
    policy[...] = jnp.where(can > 0.0, scores - value, 0.0)
    passed[...] = hand_down(value, owners[depth])

    for i in (0, 1, 3):

        @pl.loop(0, NJ)
        def _(to_j):
            copy(
                out1.at[i, to_j], in1.at[me1], send1.at[i, to_j], recv1.at[me1], device(z, (j + 1) % NJ, x)
            ).wait_send()

    @pl.loop(1, NJ)
    def _(step):
        to_j = (j + step) % NJ
        copy(out1.at[2, to_j], in1.at[me1], send1.at[2, to_j], recv1.at[me1], device(z, to_j, x)).wait_send()
        copy(out4.at[to_j % NL], in4.at[j], send4.at[step], recv4.at[j], device(z, to_j, x)).wait_send()

    @pl.loop(1, NZ)
    def _(step):
        to_z = (z + step) % NZ
        copy(
            out2.at[pl.ds(to_z * HZ, HZ)], in2.at[z], send2.at[step], recv2.at[z], device(to_z, j, x)
        ).wait_send()
        copy(out3, in3.at[z], send3.at[step], recv3.at[z], device(to_z, j, x)).wait_send()

    for step in range(1, NL):
        to = y_lo * NL + depth_peer(step)
        copy(
            logits.at[pl.ds(pl.multiple_of(to * HJ, HJ), HJ)],
            logit_rows.at[depth],
            send_l.at[step],
            recv_l.at[depth],
            device(z, to, x),
        ).wait_send()
    pay_across.wait_send()
    pay_beside.wait_send()
    pay_on.wait_send()


def local(reach, payoff, board_cards, hand_rank, logits, action_counts, parent_seq):
    table, onehot = hand_cards()
    vmem = pl.BlockSpec(memory_space=pltpu.VMEM)
    dma = pltpu.SemaphoreType.DMA
    f32, bf16, i16 = jnp.float32, jnp.bfloat16, jnp.int16
    return pl.pallas_call(
        kernel,
        name="prox",
        out_shape=(jax.ShapeDtypeStruct((HX, SL), f32), jax.ShapeDtypeStruct((HX, SL), f32)),
        in_specs=[vmem] * 9,
        out_specs=(vmem, vmem),
        scratch_shapes=[
            pltpu.VMEM((NB, HP), f32),
            pltpu.VMEM((HP, NB), f32),
            pltpu.VMEM((NX, NJ, HJ, SL), i16),
            pltpu.VMEM((NL * NJ, HJ, SL), i16),
            pltpu.VMEM((HJ, 8, 128), f32),
            pltpu.VMEM((NZ, HZ, 8, 128), f32),
            pltpu.VMEM((8, SX), f32),
            pltpu.VMEM((8, SX), f32),
            pltpu.VMEM((NL, SL, SX), bf16),
            pltpu.VMEM((NL, HJ, SL), f32),
            pltpu.VMEM((HJ, 8, 128), f32),
            pltpu.VMEM((HZ, 8, 128), f32),
            pltpu.VMEM((NZ, HZ, 8, 128), f32),
            pltpu.VMEM((NL, HJ, SL), f32),
            pltpu.VMEM((NJ, HJ, SL), f32),
            pltpu.VMEM((NL, SL), f32),
            pltpu.VMEM((NL, SL, SL), bf16),
            dma((NX, NJ)),
            dma((NL * NJ,)),
            dma((NZ,)),
            dma((NZ,)),
            dma((NZ,)),
            dma((NZ,)),
            dma((NJ,)),
            dma((NJ,)),
            dma((3,)),
            dma((NL,)),
            dma((NL,)),
            dma((NL,)),
        ],
        compiler_params=pltpu.CompilerParams(
            collective_id=0, has_side_effects=True, vmem_limit_bytes=48 * 1024 * 1024
        ),
    )(
        reach.reshape(NB * HX, SL),
        payoff,
        board_cards,
        hand_rank,
        logits,
        action_counts,
        parent_seq,
        jnp.asarray(table),
        jnp.asarray(onehot, jnp.bfloat16),
    )


def solution(mesh):
    return jax.shard_map(
        local,
        mesh=mesh,
        in_specs=(
            P("board", "hand", "depth"),
            P("depth", None),
            P("board", None),
            P("board", None),
            P("hand", "depth"),
            P(),
            P(),
        ),
        out_specs=(P("hand", "depth"), P("hand", "depth")),
        check_vma=False,
    )
```

```python
import jax
import jax.numpy as jnp
import numpy as np
from jax import lax
from jax.experimental import pallas as pl
from jax.experimental.pallas import tpu as pltpu
from jax.sharding import PartitionSpec as P

CARDS = 52
HANDS = 1326
ACT = 4
NZ = 16
NX = 4
NL = 4
NJ = 8
HX = 384
HP = NX * HX
HJ = HX // NJ
HZ = HJ // NZ
SL = 256
SX = NL * SL
NB = 8
BOUND = float(NB * HX)
SCALE = 32767.0 / BOUND
MESH = pl.DeviceIdType.MESH
NEAR = (1, -1, 2, -2)
UP = (3, 4, 6, 7, 8)
DOWN = (-3, -4, -6, -7)
HUB = 5
PEERS = (1, -1, 2, -2, 3, -3, 5, -5)
PLACES = (0, 1, -1, 2, -2, 5, -5, 3, 4, 6, 7, 8, -3, -4, -6, -7)
EARLY = 7
NAN = float("nan")


def hand_cards():
    first, second = np.triu_indices(CARDS, 1)
    table = np.full((8, HP), -1.0, np.float32)
    table[0, :HANDS] = first
    table[1, :HANDS] = second
    onehot = np.zeros((HP, 128), np.float32)
    onehot[np.arange(HANDS), first] = 1.0
    onehot[np.arange(HANDS), second] = 1.0
    return table, onehot


def dot_t(a, b):
    return lax.dot_general(a, b, (((1,), (1,)), ((), ())), preferred_element_type=jnp.float32)


def group_reduce(x, op):
    lane = lax.broadcasted_iota(jnp.int32, x.shape, 1)
    near = jnp.where(lane % 2 == 0, pltpu.roll(x, 127, 1), pltpu.roll(x, 1, 1))
    x = op(x, near)
    far = jnp.where(lane % 4 < 2, pltpu.roll(x, 126, 1), pltpu.roll(x, 2, 1))
    return op(x, far)


def group_value(scores, legal):
    parts = []
    for half in range(2):
        cols = slice(half * 128, half * 128 + 128)
        masked = jnp.where(legal[:, cols] > 0.0, scores[:, cols], -jnp.inf)
        top = group_reduce(masked, jnp.maximum)
        total = group_reduce(jnp.exp(masked - top), jnp.add)
        parts.append(top + jnp.log(total))
    return jnp.concatenate(parts, axis=1)


def hand_down(value, owner_t):
    a = value.astype(jnp.bfloat16)
    rest = value - a.astype(jnp.float32)
    b = rest.astype(jnp.bfloat16)
    c = (rest - b.astype(jnp.float32)).astype(jnp.bfloat16)
    return dot_t(a, owner_t) + dot_t(b, owner_t) + dot_t(c, owner_t)


def kernel(
    reach_hbm,
    payoff,
    cards_hbm,
    rank_hbm,
    logits_hbm,
    counts_hbm,
    parents_hbm,
    table_hbm,
    onehot_hbm,
    policy,
    passed,
    reach,
    cards,
    rank,
    logits,
    counts,
    parents,
    table,
    onehot,
    load,
    ranks,
    ranks_t,
    out1,
    in1,
    out2,
    in2,
    rows8,
    logit8,
    pay,
    logit_rows,
    logit_tiles,
    mid2,
    in3,
    in4,
    shifts,
    legal,
    owners,
    send1,
    recv1,
    send2,
    recv2,
    send3,
    recv3,
    send4,
    recv4,
    send_p,
    recv_p,
    send_l,
    recv_l,
):
    board = lax.axis_index("board")
    depth = lax.axis_index("depth")
    x = lax.axis_index("hand")
    z = board // 2
    y_lo = board % 2
    j = y_lo * NL + depth

    def device(to_z, to_j, to_x):
        return (to_z * 2 + to_j // NL, to_j % NL, to_x)

    def along(dz):
        return (z + dz + NZ) % NZ

    def copy(src, dst, send, recv, to):
        return pltpu.make_async_remote_copy(
            src_ref=src, dst_ref=dst, send_sem=send, recv_sem=recv, device_id=to, device_id_type=MESH
        )

    loads = [
        pltpu.make_async_copy(src, dst, load.at[i])
        for i, (src, dst) in enumerate(
            [
                (rank_hbm, rank),
                (cards_hbm, cards),
                (table_hbm, table),
                (onehot_hbm, onehot),
                (reach_hbm, reach),
                (payoff, pay.at[depth]),
                (logits_hbm, logits),
                (counts_hbm, counts),
                (parents_hbm, parents),
            ]
        )
    ]
    for one in loads:
        one.start()

    barrier = pltpu.get_barrier_semaphore()

    @pl.loop(1, NX * NJ)
    def _(step):
        other = (x * NJ + j + step) % (NX * NJ)
        pl.semaphore_signal(barrier, inc=1, device_id=device(z, other % NJ, other // NJ), device_id_type=MESH)

    for dz in PEERS:
        pl.semaphore_signal(barrier, inc=1, device_id=device(along(dz), j, x), device_id_type=MESH)

    for one in loads[:3]:
        one.wait()

    ranks[...] = jnp.full((NB, HP), NAN, jnp.float32)
    ranks[:, :HANDS] = rank[...].astype(jnp.float32)
    first = table[0:1, :]
    second = table[1:2, :]
    hit = first < 0.0
    for card in range(5):
        one = cards[:, card : card + 1].astype(jnp.float32)
        hit = hit | (first == one) | (second == one)
    ranks[...] = jnp.where(hit, NAN, ranks[...])
    ranks_t[...] = ranks[...].T

    own = pl.ds(pl.multiple_of(x * HX, HX), HX)

    loads[3].wait()
    loads[4].wait()

    def partial(to_x):
        rows = pl.ds(pl.multiple_of(to_x * HX, HX), HX)
        shared = dot_t(onehot[rows, :], onehot[own, :])
        apart = jnp.where(shared > 0.0, 0.0, 1.0)
        minus = -apart
        total = jnp.zeros((HX, SL), jnp.float32)
        for pair in range(NB // 2):
            sides = []
            for b in (2 * pair, 2 * pair + 1):
                mine = ranks_t[rows, b : b + 1]
                theirs = ranks[b : b + 1, own]
                sign = jnp.where(theirs < mine, apart, jnp.where(theirs > mine, minus, 0.0))
                sides.append(sign.astype(jnp.bfloat16))
            total += jnp.dot(
                jnp.concatenate(sides, axis=1),
                reach[2 * HX * pair : 2 * HX * (pair + 1), :],
                preferred_element_type=jnp.float32,
            )
        return jnp.round(total * SCALE).astype(jnp.int32).astype(jnp.int16)

    @pl.loop(0, NX)
    def _(i):
        out1[i] = partial(i).reshape(NJ, HJ, SL)

    pl.semaphore_wait(barrier, NX * NJ - 1 + len(PEERS))

    me1 = depth * NJ + x * 2 + y_lo

    def row_copy(step):
        turn = step // NX
        to_y_lo = (y_lo + (turn // 2 + 1) // 2) % 2
        to_y_hi = (depth // 2 + 1 - turn // 4) % 2
        to_core = (depth + 1 - turn % 2) % 2
        to_j = to_y_lo * NL + to_y_hi * 2 + to_core
        hop = step % NX
        to_x = (x + 2 + hop + hop * (hop - 1) // 2) % NX
        return copy(
            out1.at[to_x, to_j], in1.at[me1], send1.at[step], recv1.at[me1], device(z, to_j, to_x)
        )

    @pl.loop(0, NX * NJ - 1)
    def _(step):
        row_copy(step).start()

    in1[me1] = out1[x, j]

    for one in loads[5:]:
        one.wait()

    def depth_peer(step):
        return (depth + step) % NL

    for step in range(1, NL):
        to = y_lo * NL + depth_peer(step)
        copy(
            logits.at[pl.ds(pl.multiple_of(to * HJ, HJ), HJ)],
            logit_rows.at[depth],
            send_l.at[step],
            recv_l.at[depth],
            device(z, to, x),
        ).start()
    logit_rows[depth] = logits[pl.ds(pl.multiple_of(j * HJ, HJ), HJ), :]
    across = depth_peer(2)
    beside = depth + 1 - 2 * (depth % 2)
    opposite = across + 1 - 2 * (across % 2)
    pay_across = copy(pay.at[depth], pay.at[depth], send_p.at[0], recv_p.at[depth], device(z, y_lo * NL + across, x))
    pay_across.start()
    pay_beside = copy(pay.at[depth], pay.at[depth], send_p.at[1], recv_p.at[depth], device(z, y_lo * NL + beside, x))
    pay_beside.start()

    spread = (
        lax.broadcasted_iota(jnp.int32, (SL // ACT, SL), 0)
        == lax.broadcasted_iota(jnp.int32, (SL // ACT, SL), 1) // ACT
    ).astype(jnp.bfloat16)
    lane = lax.broadcasted_iota(jnp.int32, (NL, SL), 1) % ACT
    counts_wide = jnp.dot(
        counts[...].astype(jnp.float32).astype(jnp.bfloat16), spread, preferred_element_type=jnp.float32
    )
    parents_wide = jnp.dot(
        parents[...].astype(jnp.float32).astype(jnp.bfloat16), spread, preferred_element_type=jnp.float32
    )
    legal[...] = jnp.where(lane.astype(jnp.float32) < counts_wide, 1.0, 0.0)
    parents_wide = jnp.where(lane == 0, parents_wide, -1.0)
    seq = lax.broadcasted_iota(jnp.int32, (SL, SL), 0).astype(jnp.float32)
    for level in range(NL):
        owners[level] = jnp.where(seq == parents_wide[level : level + 1, :], 1.0, 0.0).astype(jnp.bfloat16)

    @pl.loop(1, NX * NJ)
    def _(step):
        slot = (me1 + step) % (NX * NJ)
        copy(in1.at[slot], in1.at[slot], send1.at[0], recv1.at[slot], device(z, (j + 1) % NJ, x)).wait_recv()

    for block in range(NL):
        total = in1[block * NJ].astype(jnp.int32)
        for source in range(1, NJ):
            total += in1[block * NJ + source].astype(jnp.int32)
        total = total.astype(jnp.float32)
        out2[:, 2 * block, :] = total[:, :128]
        out2[:, 2 * block + 1, :] = total[:, 128:]

    def block2(dz):
        return out2.at[pl.ds(along(dz) * HZ, HZ)]

    sums = []
    for i, k in enumerate(UP):
        sums.append((block2(-k), i, HUB - k))
    for i, k in enumerate(DOWN):
        sums.append((block2(-k), len(UP) + i, -HUB - k))
    for i, dz in enumerate(NEAR):
        sums.append((block2(dz), len(UP) + len(DOWN) + i, dz))

    def copy2(src, slot, dz):
        return copy(src, in2.at[slot], send2.at[slot], recv2.at[slot], device(along(dz), j, x))

    for src, slot, dz in sums:
        copy2(src, slot, dz).start()

    def wait2(slots):
        total = None
        for slot in slots:
            copy2(in2.at[slot], slot, 1).wait_recv()
        for slot in slots:
            total = in2[slot] if total is None else total + in2[slot]
        return total

    n_up, n_far = len(UP), len(UP) + len(DOWN)
    n_all = n_far + len(NEAR)
    mid2[0] = wait2(range(n_up)) + out2[pl.ds(along(-HUB) * HZ, HZ)]
    copy2(mid2.at[0], n_all, -HUB).start()
    mid2[1] = wait2(range(n_up, n_far)) + out2[pl.ds(along(HUB) * HZ, HZ)]
    copy2(mid2.at[1], n_all + 1, HUB).start()

    copy(pay.at[depth], pay.at[across], send_p.at[0], recv_p.at[across], device(z, (j + 1) % NJ, x)).wait_recv()
    pay_on = copy(
        pay.at[across], pay.at[across], send_p.at[2], recv_p.at[across], device(z, y_lo * NL + beside, x)
    )
    pay_on.start()
    copy(pay.at[depth], pay.at[beside], send_p.at[0], recv_p.at[beside], device(z, (j + 1) % NJ, x)).wait_recv()
    copy(pay.at[depth], pay.at[opposite], send_p.at[0], recv_p.at[opposite], device(z, (j + 1) % NJ, x)).wait_recv()

    rows8[...] = jnp.zeros((8, SX), jnp.float32)
    logit8[...] = jnp.zeros((8, SX), jnp.float32)
    for step in range(1, NL):
        slot = depth_peer(step)
        copy(
            logit_rows.at[slot], logit_rows.at[slot], send_l.at[0], recv_l.at[slot], device(z, (j + 1) % NJ, x)
        ).wait_recv()
    for group in range(8):
        logit_tiles[:, group, :] = logit_rows[group // 2, :, (group % 2) * 128 : (group % 2) * 128 + 128]
    for group in range(8):
        logit8[0:HZ, group * 128 : (group + 1) * 128] = logit_tiles[pl.ds(z * HZ, HZ), group, :]

    mid2[2] = wait2(range(n_far, n_all + 2)) + out2[pl.ds(z * HZ, HZ)]
    for group in range(8):
        rows8[0:HZ, group * 128 : (group + 1) * 128] = mid2[2, :, group, :]
    counter = rows8[...]
    high = counter.astype(jnp.bfloat16).astype(jnp.float32)
    both = jnp.concatenate([high, counter - high], axis=0).astype(jnp.bfloat16)
    gradient = jnp.dot(both[:, :SL], pay[0], preferred_element_type=jnp.float32)
    for block in range(1, NL):
        gradient += jnp.dot(
            both[:, block * SL : (block + 1) * SL], pay[block], preferred_element_type=jnp.float32
        )
    gradient = (gradient[:8] + gradient[8:]) * (1.0 / SCALE)

    incoming = jnp.zeros((8, SL), jnp.float32)
    for level in range(NL - 1, -1, -1):
        cols = slice(level * SL, (level + 1) * SL)
        shift = gradient[:, cols] + incoming
        in3[0, level, :, 0, :] = shift[:HZ, :128]
        in3[0, level, :, 1, :] = shift[:HZ, 128:]
        if level:
            value = group_value(logit8[:, cols] + shift, legal[level : level + 1, :])
            incoming = hand_down(value, owners[level])

    def copy3(source, dz):
        slot = PLACES.index(source)
        there = PLACES.index((source - dz + 7) % NZ - 7)
        return copy(in3.at[slot], in3.at[there], send3.at[there], recv3.at[there], device(along(dz), j, x))

    def wait3(source):
        slot = PLACES.index(source)
        copy(in3.at[slot], in3.at[slot], send3.at[slot], recv3.at[slot], device(along(1), j, x)).wait_recv()

    straight = [copy3(0, dz) for dz in (HUB, -HUB) + NEAR]
    onward = [copy3(-HUB, k - HUB) for k in UP]
    onward_down = [copy3(HUB, k + HUB) for k in DOWN]
    for one in straight:
        one.start()
    wait3(-HUB)
    for one in onward:
        one.start()
    wait3(HUB)
    for one in onward_down:
        one.start()

    def copy4(step, part):
        slots = pl.ds(0, EARLY) if part == 0 else pl.ds(EARLY, NZ - EARLY)
        to_j = (j + step) % NJ
        return copy(
            in3.at[slots, to_j % NL],
            in4.at[j, slots],
            send4.at[part, step],
            recv4.at[part, j],
            device(z, to_j, x),
        )

    for source in NEAR:
        wait3(source)

    @pl.loop(1, NJ)
    def _(step):
        copy4(step, 0).start()

    for source in PLACES[EARLY:]:
        wait3(source)

    @pl.loop(1, NJ)
    def _(step):
        copy4(step, 1).start()

    def place(from_j, block, slots):
        for slot in slots:
            rows = pl.ds((from_j * NZ + along(PLACES[slot])) * HZ, HZ)
            shifts[rows] = block(slot)

    place(j, lambda slot: in3[slot, depth], range(NZ))

    for part, slots in enumerate((range(EARLY), range(EARLY, NZ))):
        whole = pl.ds(slots[0], len(slots))

        @pl.loop(1, NJ)
        def _(step):
            slot = (j + step) % NJ
            copy(
                in4.at[slot, whole],
                in4.at[slot, whole],
                send4.at[part, 0],
                recv4.at[part, slot],
                device(z, slot, x),
            ).wait_recv()
            place(slot, lambda one: in4[slot, one], slots)

    scores = logits[...] + jnp.concatenate([shifts[:, 0, :], shifts[:, 1, :]], axis=1)
    can = legal[pl.ds(depth, 1), :]
    value = group_value(scores, can)
    policy[...] = jnp.where(can > 0.0, scores - value, 0.0)
    passed[...] = hand_down(value, owners[depth])

    @pl.loop(0, NX * NJ - 1)
    def _(step):
        row_copy(step).wait_send()

    for src, slot, dz in sums:
        copy2(src, slot, dz).wait_send()
    copy2(mid2.at[0], n_all, -HUB).wait_send()
    copy2(mid2.at[1], n_all + 1, HUB).wait_send()
    for one in straight + onward + onward_down:
        one.wait_send()

    @pl.loop(1, NJ)
    def _(step):
        copy4(step, 0).wait_send()
        copy4(step, 1).wait_send()

    for step in range(1, NL):
        to = y_lo * NL + depth_peer(step)
        copy(
            logits.at[pl.ds(pl.multiple_of(to * HJ, HJ), HJ)],
            logit_rows.at[depth],
            send_l.at[step],
            recv_l.at[depth],
            device(z, to, x),
        ).wait_send()
    pay_across.wait_send()
    pay_beside.wait_send()
    pay_on.wait_send()


def local(reach, payoff, board_cards, hand_rank, logits, action_counts, parent_seq):
    table, onehot = hand_cards()
    vmem = pl.BlockSpec(memory_space=pltpu.VMEM)
    dma = pltpu.SemaphoreType.DMA
    f32, bf16, i16 = jnp.float32, jnp.bfloat16, jnp.int16
    return pl.pallas_call(
        kernel,
        name="prox",
        out_shape=(jax.ShapeDtypeStruct((HX, SL), f32), jax.ShapeDtypeStruct((HX, SL), f32)),
        in_specs=[pl.BlockSpec(memory_space=pl.ANY)] * 9,
        out_specs=(vmem, vmem),
        scratch_shapes=[
            pltpu.VMEM((NB * HX, SL), bf16),
            pltpu.VMEM((NB, 5), jnp.int32),
            pltpu.VMEM((NB, HANDS), jnp.int32),
            pltpu.VMEM((HX, SL), f32),
            pltpu.VMEM((NL, SL // ACT), jnp.int32),
            pltpu.VMEM((NL, SL // ACT), jnp.int32),
            pltpu.VMEM((8, HP), f32),
            pltpu.VMEM((HP, 128), bf16),
            dma((9,)),
            pltpu.VMEM((NB, HP), f32),
            pltpu.VMEM((HP, NB), f32),
            pltpu.VMEM((NX, NJ, HJ, SL), i16),
            pltpu.VMEM((NL * NJ, HJ, SL), i16),
            pltpu.VMEM((HJ, 8, 128), f32),
            pltpu.VMEM((NZ, HZ, 8, 128), f32),
            pltpu.VMEM((8, SX), f32),
            pltpu.VMEM((8, SX), f32),
            pltpu.VMEM((NL, SL, SX), bf16),
            pltpu.VMEM((NL, HJ, SL), f32),
            pltpu.VMEM((HJ, 8, 128), f32),
            pltpu.VMEM((3, HZ, 8, 128), f32),
            pltpu.VMEM((NZ, NL, HZ, 2, 128), f32),
            pltpu.VMEM((NJ, NZ, HZ, 2, 128), f32),
            pltpu.VMEM((HX, 2, 128), f32),
            pltpu.VMEM((NL, SL), f32),
            pltpu.VMEM((NL, SL, SL), bf16),
            dma((NX * NJ,)),
            dma((NL * NJ,)),
            dma((NZ,)),
            dma((NZ,)),
            dma((NZ,)),
            dma((NZ,)),
            dma((2, NJ)),
            dma((2, NJ)),
            dma((3,)),
            dma((NL,)),
            dma((NL,)),
            dma((NL,)),
        ],
        compiler_params=pltpu.CompilerParams(
            collective_id=0, has_side_effects=True, vmem_limit_bytes=60 * 1024 * 1024
        ),
    )(
        reach.reshape(NB * HX, SL),
        payoff,
        board_cards,
        hand_rank,
        logits,
        action_counts,
        parent_seq,
        jnp.asarray(table),
        jnp.asarray(onehot, jnp.bfloat16),
    )


def solution(mesh):
    return jax.shard_map(
        local,
        mesh=mesh,
        in_specs=(
            P("board", "hand", "depth"),
            P("depth", None),
            P("board", None),
            P("board", None),
            P("hand", "depth"),
            P(),
            P(),
        ),
        out_specs=(P("hand", "depth"), P("hand", "depth")),
        check_vma=False,
    )
```

```python
import jax
import jax.numpy as jnp
import numpy as np
from jax import lax
from jax.experimental import pallas as pl
from jax.experimental.pallas import tpu as pltpu
from jax.sharding import PartitionSpec as P

CARDS = 52
HANDS = 1326
ACT = 4
NZ = 16
NX = 4
NL = 4
NJ = 8
HX = 384
HP = NX * HX
HY = HX // 2
HZ = HY // NZ
HD = HZ // NL
PAD = 16
SL = 256
SX = NL * SL
NB = 8
BOUND = float(NB * HX)
SCALE = 32767.0 / BOUND
LIVE = 45 * 44 // 2
BOUND_PLANE = float(2 * NB * LIVE)
SCALE_PLANE = 32700.0 / BOUND_PLANE
MESH = pl.DeviceIdType.MESH
NEAR = (1, -1, 2, -2)
UP = (3, 4, 6, 7, 8)
DOWN = (-3, -4, -6, -7)
HUB = 5
FAR_FIRST = (8, 7, -7, 6, -6, 5, -5, 4, -4, 3, -3, 2, -2, 1, -1)
GREET = (1, -1, 3, -3, 4, -4)
PASS_ON = (3, -3, 4, -4)
PLACES = (0, 1, -1, 2, -2, 5, -5, 3, 4, 6, 7, 8, -3, -4, -6, -7)
EARLY = 7
OWNERS = ((1, 2), (0, 2), (1, 1), (1, 3), (0, 1), (0, 3), (1, 0))
NAN = float("nan")


def hand_cards():
    first, second = np.triu_indices(CARDS, 1)
    table = np.full((8, HP), -1.0, np.float32)
    table[0, :HANDS] = first
    table[1, :HANDS] = second
    onehot = np.zeros((HP, 128), np.float32)
    onehot[np.arange(HANDS), first] = 1.0
    onehot[np.arange(HANDS), second] = 1.0
    return table, onehot


def dot_t(a, b):
    return lax.dot_general(a, b, (((1,), (1,)), ((), ())), preferred_element_type=jnp.float32)


def group_reduce(x, op):
    lane = lax.broadcasted_iota(jnp.int32, x.shape, 1)
    near = jnp.where(lane % 2 == 0, pltpu.roll(x, 127, 1), pltpu.roll(x, 1, 1))
    x = op(x, near)
    far = jnp.where(lane % 4 < 2, pltpu.roll(x, 126, 1), pltpu.roll(x, 2, 1))
    return op(x, far)


def group_value(scores, legal):
    parts = []
    for half in range(2):
        cols = slice(half * 128, half * 128 + 128)
        masked = jnp.where(legal[:, cols] > 0.0, scores[:, cols], -jnp.inf)
        top = group_reduce(masked, jnp.maximum)
        total = group_reduce(jnp.exp(masked - top), jnp.add)
        parts.append(top + jnp.log(total))
    return jnp.concatenate(parts, axis=1)


def hand_down(value, owner_t):
    a = value.astype(jnp.bfloat16)
    rest = value - a.astype(jnp.float32)
    b = rest.astype(jnp.bfloat16)
    c = (rest - b.astype(jnp.float32)).astype(jnp.bfloat16)
    return dot_t(a, owner_t) + dot_t(b, owner_t) + dot_t(c, owner_t)


def kernel(
    reach_hbm,
    payoff,
    cards_hbm,
    rank_hbm,
    logits_hbm,
    counts_hbm,
    parents_hbm,
    table_hbm,
    onehot_hbm,
    policy,
    passed,
    reach,
    cards,
    rank,
    logits,
    counts,
    parents,
    table,
    onehot,
    load,
    ranks,
    ranks_t,
    out1,
    in1,
    out2,
    in2,
    rows8,
    logit8,
    pay,
    logit_tiles,
    logit_rows,
    total2,
    out5,
    in5,
    in3,
    in4,
    shifts,
    legal,
    owners,
    send1,
    recv1,
    send2,
    recv2,
    send3,
    recv3,
    send4,
    recv4,
    send5,
    recv5,
    send_l,
    recv_l,
    know,
):
    board = lax.axis_index("board")
    depth = lax.axis_index("depth")
    x = lax.axis_index("hand")
    z = board // 2
    y_lo = board % 2
    j = y_lo * NL + depth

    def device(to_z, to_j, to_x):
        return (to_z * 2 + to_j // NL, to_j % NL, to_x)

    def along(dz):
        return (z + dz + NZ) % NZ

    def copy(src, dst, send, recv, to):
        return pltpu.make_async_remote_copy(
            src_ref=src, dst_ref=dst, send_sem=send, recv_sem=recv, device_id=to, device_id_type=MESH
        )

    loads = [
        pltpu.make_async_copy(src, dst, load.at[i])
        for i, (src, dst) in enumerate(
            [
                (rank_hbm, rank),
                (cards_hbm, cards),
                (table_hbm, table),
                (onehot_hbm, onehot),
                (reach_hbm, reach),
                (payoff, pay),
                (logits_hbm, logits),
                (counts_hbm, counts),
                (parents_hbm, parents),
            ]
        )
    ]
    for one in loads:
        one.start()

    def owner(other, hop):
        return (y_lo + other) % 2 * NL + depth, (x + hop) % NX

    barrier = pltpu.get_barrier_semaphore()
    for other, hop in OWNERS:
        to_j, to_x = owner(other, hop)
        pl.semaphore_signal(barrier, inc=1, device_id=device(z, to_j, to_x), device_id_type=MESH)
    for other in range(2):
        for step in range(1, NL):
            to_j = (y_lo + other) % 2 * NL + (depth + step) % NL
            pl.semaphore_signal(barrier, inc=1, device_id=device(z, to_j, x), device_id_type=MESH)
    for dz in GREET:
        pl.semaphore_signal(barrier, inc=1, device_id=device(along(dz), j, x), device_id_type=MESH)

    for one in loads[:3]:
        one.wait()

    ranks[...] = jnp.full((NB, HP), NAN, jnp.float32)
    ranks[:, :HANDS] = rank[...].astype(jnp.float32)
    first = table[0:1, :]
    second = table[1:2, :]
    hit = first < 0.0
    for card in range(5):
        one = cards[:, card : card + 1].astype(jnp.float32)
        hit = hit | (first == one) | (second == one)
    ranks[...] = jnp.where(hit, NAN, ranks[...])
    ranks_t[...] = ranks[...].T

    own = pl.ds(pl.multiple_of(x * HX, HX), HX)

    loads[3].wait()
    loads[4].wait()

    def partial(to_x):
        rows = pl.ds(pl.multiple_of(to_x * HX, HX), HX)
        shared = dot_t(onehot[rows, :], onehot[own, :])
        apart = jnp.where(shared > 0.0, 0.0, 1.0)
        minus = -apart
        total = jnp.zeros((HX, SL), jnp.float32)
        for pair in range(NB // 2):
            sides = []
            for b in (2 * pair, 2 * pair + 1):
                mine = ranks_t[rows, b : b + 1]
                theirs = ranks[b : b + 1, own]
                sign = jnp.where(theirs < mine, apart, jnp.where(theirs > mine, minus, 0.0))
                sides.append(sign.astype(jnp.bfloat16))
            total += jnp.dot(
                jnp.concatenate(sides, axis=1),
                reach[2 * HX * pair : 2 * HX * (pair + 1), :],
                preferred_element_type=jnp.float32,
            )
        return jnp.round(total * SCALE).astype(jnp.int32).astype(jnp.int16)

    @pl.loop(0, NX)
    def _(i):
        out1[i] = partial(i).reshape(2, HY, SL)

    pl.semaphore_wait(barrier, len(OWNERS) + 2 * (NL - 1) + len(GREET))
    for dz in PASS_ON:
        pl.semaphore_signal(know, inc=1, device_id=device(along(dz), j, x), device_id_type=MESH)

    me1 = x * 2 + y_lo

    def copy1(i):
        to_j, to_x = owner(*OWNERS[i])
        return copy(
            out1.at[to_x, to_j // NL], in1.at[me1], send1.at[i], recv1.at[me1], device(z, to_j, to_x)
        )

    for i in range(len(OWNERS)):
        copy1(i).start()
    in1[me1] = out1[x, y_lo]

    for one in loads[5:]:
        one.wait()

    for half in range(2):
        logit_tiles[:, half, :] = logits[:, half * 128 : half * 128 + 128]

    def depth_peer(step):
        return (depth + step) % NL

    def copy_l(step):
        to = depth_peer(step)
        rows = pl.ds(y_lo * HY + z * HZ + to * HD, HD)
        return copy(
            logit_tiles.at[rows],
            logit_rows.at[depth],
            send_l.at[step],
            recv_l.at[depth],
            device(z, y_lo * NL + to, x),
        )

    for step in range(1, NL):
        copy_l(step).start()
    logit_rows[depth] = logit_tiles[pl.ds(y_lo * HY + z * HZ + depth * HD, HD)]

    spread = (
        lax.broadcasted_iota(jnp.int32, (SL // ACT, SL), 0)
        == lax.broadcasted_iota(jnp.int32, (SL // ACT, SL), 1) // ACT
    ).astype(jnp.bfloat16)
    lane = lax.broadcasted_iota(jnp.int32, (NL, SL), 1) % ACT
    counts_wide = jnp.dot(
        counts[...].astype(jnp.float32).astype(jnp.bfloat16), spread, preferred_element_type=jnp.float32
    )
    parents_wide = jnp.dot(
        parents[...].astype(jnp.float32).astype(jnp.bfloat16), spread, preferred_element_type=jnp.float32
    )
    legal[...] = jnp.where(lane.astype(jnp.float32) < counts_wide, 1.0, 0.0)
    parents_wide = jnp.where(lane == 0, parents_wide, -1.0)
    seq = lax.broadcasted_iota(jnp.int32, (SL, SL), 0).astype(jnp.float32)
    for level in range(NL):
        owners[level] = jnp.where(seq == parents_wide[level : level + 1, :], 1.0, 0.0).astype(jnp.bfloat16)

    for i in range(len(OWNERS)):
        slot = (me1 + 1 + i) % NJ
        copy(in1.at[slot], in1.at[slot], send1.at[0], recv1.at[slot], device(z, j, (x + 1) % NX)).wait_recv()

    total = in1[0].astype(jnp.int32)
    for source in range(1, NJ):
        total += in1[source].astype(jnp.int32)
    total2[:HY, :] = total.astype(jnp.float32) * (SCALE_PLANE / SCALE)
    total2[HY:, :] = jnp.zeros((8, SL), jnp.float32)
    for to_z in range(NZ):
        rows = jnp.round(total2[to_z * HZ : to_z * HZ + PAD, :])
        out2[to_z] = rows.astype(jnp.int32).astype(jnp.int16)

    pl.semaphore_wait(know, len(PASS_ON))

    def copy2(i):
        dz = FAR_FIRST[i]
        return copy(
            out2.at[along(dz)], in2.at[i], send2.at[i], recv2.at[i], device(along(dz), j, x)
        )

    for i in range(NZ - 1):
        copy2(i).start()

    rows8[...] = jnp.zeros((8, SX), jnp.float32)
    logit8[...] = jnp.zeros((8, SX), jnp.float32)
    for step in range(1, NL):
        slot = depth_peer(step)
        copy(
            logit_rows.at[slot], logit_rows.at[slot], send_l.at[0], recv_l.at[slot], device(z, j, (x + 1) % NX)
        ).wait_recv()
    for group in range(8):
        logit8[0:HD, group * 128 : (group + 1) * 128] = logit_rows[group // 2, :, group % 2, :]

    for i in range(NZ - 1):
        copy2(i).wait_recv()
    total = out2[z].astype(jnp.int32)
    for i in range(NZ - 1):
        total += in2[i].astype(jnp.int32)
    counter = total.astype(jnp.float32)
    high = counter.astype(jnp.bfloat16).astype(jnp.float32)
    both = jnp.concatenate([high, counter - high], axis=0).astype(jnp.bfloat16)
    partial_gradient = jnp.dot(both, pay[...], preferred_element_type=jnp.float32)
    partial_gradient = (partial_gradient[:PAD] + partial_gradient[PAD:]) * (1.0 / SCALE_PLANE)
    for group in range(8):
        out5[:, group, :] = partial_gradient[:HZ, group * 128 : (group + 1) * 128]

    def copy5(step):
        to = depth_peer(step)
        return copy(
            out5.at[pl.ds(to * HD, HD)],
            in5.at[step],
            send5.at[step],
            recv5.at[step],
            device(z, y_lo * NL + to, x),
        )

    for step in range(1, NL):
        copy5(step).start()
    for step in range(1, NL):
        copy5(step).wait_recv()
    total = out5[pl.ds(depth * HD, HD)] + in5[1] + in5[2] + in5[3]
    in5[0] = total
    for group in range(8):
        rows8[0:HD, group * 128 : (group + 1) * 128] = in5[0, :, group, :]
    gradient = rows8[...]

    incoming = jnp.zeros((8, SL), jnp.float32)
    for level in range(NL - 1, -1, -1):
        cols = slice(level * SL, (level + 1) * SL)
        shift = gradient[:, cols] + incoming
        in3[0, level, :, 0, :] = shift[:HD, :128]
        in3[0, level, :, 1, :] = shift[:HD, 128:]
        if level:
            value = group_value(logit8[:, cols] + shift, legal[level : level + 1, :])
            incoming = hand_down(value, owners[level])

    def copy3(source, dz):
        slot = PLACES.index(source)
        there = PLACES.index((source - dz + 7) % NZ - 7)
        return copy(in3.at[slot], in3.at[there], send3.at[there], recv3.at[there], device(along(dz), j, x))

    def wait3(source):
        slot = PLACES.index(source)
        copy(in3.at[slot], in3.at[slot], send3.at[slot], recv3.at[slot], device(along(1), j, x)).wait_recv()

    straight = [copy3(0, dz) for dz in (HUB, -HUB) + NEAR]
    onward = [copy3(-HUB, k - HUB) for k in UP]
    onward_down = [copy3(HUB, k + HUB) for k in DOWN]
    for one in straight:
        one.start()
    wait3(-HUB)
    for one in onward:
        one.start()
    wait3(HUB)
    for one in onward_down:
        one.start()

    def copy4(step, part):
        slots = pl.ds(0, EARLY) if part == 0 else pl.ds(EARLY, NZ - EARLY)
        to_j = (j + step) % NJ
        return copy(
            in3.at[slots, to_j % NL],
            in4.at[j, slots],
            send4.at[part, step],
            recv4.at[part, j],
            device(z, to_j, x),
        )

    for source in NEAR:
        wait3(source)

    @pl.loop(1, NJ)
    def _(step):
        copy4(step, 0).start()

    for source in PLACES[EARLY:]:
        wait3(source)

    @pl.loop(1, NJ)
    def _(step):
        copy4(step, 1).start()

    def place(from_j, block, slots):
        for slot in slots:
            rows = pl.ds(from_j // NL * HY + along(PLACES[slot]) * HZ + from_j % NL * HD, HD)
            shifts[rows] = block(slot)

    place(j, lambda slot: in3[slot, depth], range(NZ))

    for part, slots in enumerate((range(EARLY), range(EARLY, NZ))):
        whole = pl.ds(slots[0], len(slots))

        @pl.loop(1, NJ)
        def _(step):
            slot = (j + step) % NJ
            copy(
                in4.at[slot, whole],
                in4.at[slot, whole],
                send4.at[part, 0],
                recv4.at[part, slot],
                device(z, slot, x),
            ).wait_recv()
            place(slot, lambda one: in4[slot, one], slots)

    scores = logits[...] + jnp.concatenate([shifts[:, 0, :], shifts[:, 1, :]], axis=1)
    can = legal[pl.ds(depth, 1), :]
    value = group_value(scores, can)
    policy[...] = jnp.where(can > 0.0, scores - value, 0.0)
    passed[...] = hand_down(value, owners[depth])

    for i in range(len(OWNERS)):
        copy1(i).wait_send()
    for i in range(NZ - 1):
        copy2(i).wait_send()
    for step in range(1, NL):
        copy5(step).wait_send()
        copy_l(step).wait_send()
    for one in straight + onward + onward_down:
        one.wait_send()

    @pl.loop(1, NJ)
    def _(step):
        copy4(step, 0).wait_send()
        copy4(step, 1).wait_send()


def local(reach, payoff, board_cards, hand_rank, logits, action_counts, parent_seq):
    table, onehot = hand_cards()
    vmem = pl.BlockSpec(memory_space=pltpu.VMEM)
    dma = pltpu.SemaphoreType.DMA
    f32, bf16, i16 = jnp.float32, jnp.bfloat16, jnp.int16
    return pl.pallas_call(
        kernel,
        name="prox",
        out_shape=(jax.ShapeDtypeStruct((HX, SL), f32), jax.ShapeDtypeStruct((HX, SL), f32)),
        in_specs=[pl.BlockSpec(memory_space=pl.ANY)] * 9,
        out_specs=(vmem, vmem),
        scratch_shapes=[
            pltpu.VMEM((NB * HX, SL), bf16),
            pltpu.VMEM((NB, 5), jnp.int32),
            pltpu.VMEM((NB, HANDS), jnp.int32),
            pltpu.VMEM((HX, SL), f32),
            pltpu.VMEM((NL, SL // ACT), jnp.int32),
            pltpu.VMEM((NL, SL // ACT), jnp.int32),
            pltpu.VMEM((8, HP), f32),
            pltpu.VMEM((HP, 128), bf16),
            dma((9,)),
            pltpu.VMEM((NB, HP), f32),
            pltpu.VMEM((HP, NB), f32),
            pltpu.VMEM((NX, 2, HY, SL), i16),
            pltpu.VMEM((NJ, HY, SL), i16),
            pltpu.VMEM((NZ, PAD, SL), i16),
            pltpu.VMEM((NZ - 1, PAD, SL), i16),
            pltpu.VMEM((8, SX), f32),
            pltpu.VMEM((8, SX), f32),
            pltpu.VMEM((SL, SX), bf16),
            pltpu.VMEM((HX, 2, 128), f32),
            pltpu.VMEM((NL, HD, 2, 128), f32),
            pltpu.VMEM((HY + 8, SL), f32),
            pltpu.VMEM((HZ, 8, 128), f32),
            pltpu.VMEM((NL, HD, 8, 128), f32),
            pltpu.VMEM((NZ, NL, HD, 2, 128), f32),
            pltpu.VMEM((NJ, NZ, HD, 2, 128), f32),
            pltpu.VMEM((HX, 2, 128), f32),
            pltpu.VMEM((NL, SL), f32),
            pltpu.VMEM((NL, SL, SL), bf16),
            dma((len(OWNERS),)),
            dma((NJ,)),
            dma((NZ - 1,)),
            dma((NZ - 1,)),
            dma((NZ,)),
            dma((NZ,)),
            dma((2, NJ)),
            dma((2, NJ)),
            dma((NL,)),
            dma((NL,)),
            dma((NL,)),
            dma((NL,)),
            pltpu.SemaphoreType.REGULAR,
        ],
        compiler_params=pltpu.CompilerParams(
            collective_id=0, has_side_effects=True, vmem_limit_bytes=60 * 1024 * 1024
        ),
    )(
        reach.reshape(NB * HX, SL),
        payoff,
        board_cards,
        hand_rank,
        logits,
        action_counts,
        parent_seq,
        jnp.asarray(table),
        jnp.asarray(onehot, jnp.bfloat16),
    )


def solution(mesh):
    return jax.shard_map(
        local,
        mesh=mesh,
        in_specs=(
            P("board", "hand", "depth"),
            P("depth", None),
            P("board", None),
            P("board", None),
            P("hand", "depth"),
            P(),
            P(),
        ),
        out_specs=(P("hand", "depth"), P("hand", "depth")),
        check_vma=False,
    )
```

```python
import jax
import jax.numpy as jnp
import numpy as np
from jax import lax
from jax.experimental import pallas as pl
from jax.experimental.pallas import tpu as pltpu
from jax.sharding import PartitionSpec as P

CARDS = 52
HANDS = 1326
ACT = 4
NZ = 16
NX = 4
NL = 4
NJ = 8
HX = 384
HP = NX * HX
HY = HX // 2
HZ = HY // NZ
HD = HZ // NL
PAD = 16
SL = 256
SX = NL * SL
NB = 8
BOUND = float(NB * HX)
SCALE = 32767.0 / BOUND
LIVE = 45 * 44 // 2
BOUND_PLANE = float(2 * NB * LIVE)
SCALE_PLANE = 32700.0 / BOUND_PLANE
MESH = pl.DeviceIdType.MESH
NEAR = (1, -1, 2, -2)
UP = (3, 4, 6, 7, 8)
DOWN = (-3, -4, -6, -7)
HUB = 5
FAR_FIRST = (8, 7, -7, 6, -6, 5, -5, 4, -4, 3, -3, 2, -2, 1, -1)
GREET = (1, -1, 2, -2)
PLACES = (0, 1, -1, 2, -2, 5, -5, -3, -4, -6, -7, 3, 4, 6, 7, 8)
PARTS = ((0, 7), (7, 11), (11, 16))
ROW_PEERS = 2 * NX - 1
NAN = float("nan")


def hand_cards():
    first, second = np.triu_indices(CARDS, 1)
    table = np.full((8, HP), -1.0, np.float32)
    table[0, :HANDS] = first
    table[1, :HANDS] = second
    onehot = np.zeros((HP, 128), np.float32)
    onehot[np.arange(HANDS), first] = 1.0
    onehot[np.arange(HANDS), second] = 1.0
    return table, onehot


def dot_t(a, b):
    return lax.dot_general(a, b, (((1,), (1,)), ((), ())), preferred_element_type=jnp.float32)


def group_reduce(x, op):
    lane = lax.broadcasted_iota(jnp.int32, x.shape, 1)
    near = jnp.where(lane % 2 == 0, pltpu.roll(x, 127, 1), pltpu.roll(x, 1, 1))
    x = op(x, near)
    far = jnp.where(lane % 4 < 2, pltpu.roll(x, 126, 1), pltpu.roll(x, 2, 1))
    return op(x, far)


def group_value(scores, legal):
    parts = []
    for half in range(2):
        cols = slice(half * 128, half * 128 + 128)
        masked = jnp.where(legal[:, cols] > 0.0, scores[:, cols], -jnp.inf)
        top = group_reduce(masked, jnp.maximum)
        total = group_reduce(jnp.exp(masked - top), jnp.add)
        parts.append(top + jnp.log(total))
    return jnp.concatenate(parts, axis=1)


def hand_down(value, owner_t):
    a = value.astype(jnp.bfloat16)
    rest = value - a.astype(jnp.float32)
    b = rest.astype(jnp.bfloat16)
    c = (rest - b.astype(jnp.float32)).astype(jnp.bfloat16)
    return dot_t(a, owner_t) + dot_t(b, owner_t) + dot_t(c, owner_t)


def kernel(
    reach_hbm,
    payoff,
    cards_hbm,
    rank_hbm,
    logits_hbm,
    counts_hbm,
    parents_hbm,
    table_hbm,
    onehot_hbm,
    policy,
    passed,
    reach,
    cards,
    rank,
    logits,
    counts,
    parents,
    table,
    onehot,
    load,
    ranks,
    ranks_t,
    out1,
    in1,
    out2,
    in2,
    rows8,
    logit8,
    pay,
    logit_tiles,
    logit_rows,
    total2,
    out5,
    in5,
    in3,
    in4,
    shifts,
    legal,
    owners,
    send1,
    recv1,
    send2,
    recv2,
    send3,
    recv3,
    send4,
    recv4,
    send5,
    recv5,
    send_l,
    recv_l,
    know,
):
    board = lax.axis_index("board")
    depth = lax.axis_index("depth")
    x = lax.axis_index("hand")
    z = board // 2
    y_lo = board % 2
    j = y_lo * NL + depth

    def device(to_z, to_j, to_x):
        return (to_z * 2 + to_j // NL, to_j % NL, to_x)

    def along(dz):
        return (z + dz + NZ) % NZ

    def copy(src, dst, send, recv, to):
        return pltpu.make_async_remote_copy(
            src_ref=src, dst_ref=dst, send_sem=send, recv_sem=recv, device_id=to, device_id_type=MESH
        )

    loads = [
        pltpu.make_async_copy(src, dst, load.at[i])
        for i, (src, dst) in enumerate(
            [
                (rank_hbm, rank),
                (cards_hbm, cards),
                (table_hbm, table),
                (onehot_hbm, onehot),
                (reach_hbm, reach),
                (payoff, pay),
                (logits_hbm, logits),
                (counts_hbm, counts),
                (parents_hbm, parents),
            ]
        )
    ]
    for one in loads:
        one.start()

    def hop_x(i):
        return (x + 2 + i + i * (i - 1) // 2) % NX

    barrier = pltpu.get_barrier_semaphore()
    for i in range(NX):
        for other in range(1 if i == NX - 1 else 0, 2):
            to_j = (y_lo + other) % 2 * NL + depth
            pl.semaphore_signal(barrier, inc=1, device_id=device(z, to_j, hop_x(i)), device_id_type=MESH)
    for other in range(2):
        for step in range(1, NL):
            to_j = (y_lo + other) % 2 * NL + (depth + step) % NL
            pl.semaphore_signal(barrier, inc=1, device_id=device(z, to_j, x), device_id_type=MESH)
    for dz in GREET:
        pl.semaphore_signal(barrier, inc=1, device_id=device(along(dz), j, x), device_id_type=MESH)

    for one in loads[:3]:
        one.wait()

    ranks[...] = jnp.full((NB, HP), NAN, jnp.float32)
    ranks[:, :HANDS] = rank[...].astype(jnp.float32)
    first = table[0:1, :]
    second = table[1:2, :]
    hit = first < 0.0
    for card in range(5):
        one = cards[:, card : card + 1].astype(jnp.float32)
        hit = hit | (first == one) | (second == one)
    ranks[...] = jnp.where(hit, NAN, ranks[...])
    ranks_t[...] = ranks[...].T

    own = pl.ds(pl.multiple_of(x * HX, HX), HX)

    loads[3].wait()
    loads[4].wait()

    def partial(to_x):
        rows = pl.ds(pl.multiple_of(to_x * HX, HX), HX)
        shared = dot_t(onehot[rows, :], onehot[own, :])
        apart = jnp.where(shared > 0.0, 0.0, 1.0)
        minus = -apart
        total = jnp.zeros((HX, SL), jnp.float32)
        for pair in range(NB // 2):
            sides = []
            for b in (2 * pair, 2 * pair + 1):
                mine = ranks_t[rows, b : b + 1]
                theirs = ranks[b : b + 1, own]
                sign = jnp.where(theirs < mine, apart, jnp.where(theirs > mine, minus, 0.0))
                sides.append(sign.astype(jnp.bfloat16))
            total += jnp.dot(
                jnp.concatenate(sides, axis=1),
                reach[2 * HX * pair : 2 * HX * (pair + 1), :],
                preferred_element_type=jnp.float32,
            )
        return jnp.round(total * SCALE).astype(jnp.int32).astype(jnp.int16)

    me1 = x * 2 + y_lo

    def copy1(i, other):
        to_x, to_y = hop_x(i), (y_lo + other) % 2
        return copy(
            out1.at[to_x, to_y],
            in1.at[me1],
            send1.at[i, other],
            recv1.at[me1],
            device(z, to_y * NL + depth, to_x),
        )

    @pl.loop(0, NX)
    def _(i):
        to_x = hop_x(i)
        out1[to_x] = partial(to_x).reshape(2, HY, SL)

        @pl.when(i == 0)
        def _():
            pl.semaphore_wait(barrier, ROW_PEERS + 2 * (NL - 1) + len(GREET))
            for dz in (2, -2):
                pl.semaphore_signal(
                    know.at[0], inc=1, device_id=device(along(dz), j, x), device_id_type=MESH
                )

        copy1(i, 1).start()

        @pl.when(i < NX - 1)
        def _():
            copy1(i, 0).start()

    pl.semaphore_wait(know.at[0], 2)
    for dz in (4, -4):
        pl.semaphore_signal(know.at[1], inc=1, device_id=device(along(dz), j, x), device_id_type=MESH)
    in1[me1] = out1[x, y_lo]

    for one in loads[5:]:
        one.wait()

    for half in range(2):
        logit_tiles[:, half, :] = logits[:, half * 128 : half * 128 + 128]

    def depth_peer(step):
        return (depth + step) % NL

    def copy_l(step):
        to = depth_peer(step)
        rows = pl.ds(y_lo * HY + z * HZ + to * HD, HD)
        return copy(
            logit_tiles.at[rows],
            logit_rows.at[depth],
            send_l.at[step],
            recv_l.at[depth],
            device(z, y_lo * NL + to, x),
        )

    for step in range(1, NL):
        copy_l(step).start()
    logit_rows[depth] = logit_tiles[pl.ds(y_lo * HY + z * HZ + depth * HD, HD)]

    spread = (
        lax.broadcasted_iota(jnp.int32, (SL // ACT, SL), 0)
        == lax.broadcasted_iota(jnp.int32, (SL // ACT, SL), 1) // ACT
    ).astype(jnp.bfloat16)
    lane = lax.broadcasted_iota(jnp.int32, (NL, SL), 1) % ACT
    counts_wide = jnp.dot(
        counts[...].astype(jnp.float32).astype(jnp.bfloat16), spread, preferred_element_type=jnp.float32
    )
    parents_wide = jnp.dot(
        parents[...].astype(jnp.float32).astype(jnp.bfloat16), spread, preferred_element_type=jnp.float32
    )
    legal[...] = jnp.where(lane.astype(jnp.float32) < counts_wide, 1.0, 0.0)
    parents_wide = jnp.where(lane == 0, parents_wide, -1.0)
    seq = lax.broadcasted_iota(jnp.int32, (SL, SL), 0).astype(jnp.float32)
    for level in range(NL):
        owners[level] = jnp.where(seq == parents_wide[level : level + 1, :], 1.0, 0.0).astype(jnp.bfloat16)

    for i in range(ROW_PEERS):
        slot = (me1 + 1 + i) % NJ
        copy(in1.at[slot], in1.at[slot], send1.at[0, 0], recv1.at[slot], device(z, j, (x + 1) % NX)).wait_recv()

    total = in1[0].astype(jnp.int32)
    for source in range(1, NJ):
        total += in1[source].astype(jnp.int32)
    total2[:HY, :] = total.astype(jnp.float32) * (SCALE_PLANE / SCALE)
    total2[HY:, :] = jnp.zeros((8, SL), jnp.float32)
    for to_z in range(NZ):
        rows = jnp.round(total2[to_z * HZ : to_z * HZ + PAD, :])
        out2[to_z] = rows.astype(jnp.int32).astype(jnp.int16)

    pl.semaphore_wait(know.at[1], 2)

    def copy2(i):
        dz = FAR_FIRST[i]
        return copy(
            out2.at[along(dz)], in2.at[i], send2.at[i], recv2.at[i], device(along(dz), j, x)
        )

    for i in range(NZ - 1):
        copy2(i).start()

    rows8[...] = jnp.zeros((8, SX), jnp.float32)
    logit8[...] = jnp.zeros((8, SX), jnp.float32)
    for step in range(1, NL):
        slot = depth_peer(step)
        copy(
            logit_rows.at[slot], logit_rows.at[slot], send_l.at[0], recv_l.at[slot], device(z, j, (x + 1) % NX)
        ).wait_recv()
    for group in range(8):
        logit8[0:HD, group * 128 : (group + 1) * 128] = logit_rows[group // 2, :, group % 2, :]

    for i in range(NZ - 1):
        copy2(i).wait_recv()
    total = out2[z].astype(jnp.int32)
    for i in range(NZ - 1):
        total += in2[i].astype(jnp.int32)
    counter = total.astype(jnp.float32)
    high = counter.astype(jnp.bfloat16).astype(jnp.float32)
    both = jnp.concatenate([high, counter - high], axis=0).astype(jnp.bfloat16)
    partial_gradient = jnp.dot(both, pay[...], preferred_element_type=jnp.float32)
    partial_gradient = (partial_gradient[:PAD] + partial_gradient[PAD:]) * (1.0 / SCALE_PLANE)
    for group in range(8):
        out5[:, group, :] = partial_gradient[:HZ, group * 128 : (group + 1) * 128]

    def copy5(step):
        to = depth_peer(step)
        return copy(
            out5.at[pl.ds(to * HD, HD)],
            in5.at[step],
            send5.at[step],
            recv5.at[step],
            device(z, y_lo * NL + to, x),
        )

    for step in (2, 1, 3):
        copy5(step).start()
    for step in range(1, NL):
        copy5(step).wait_recv()
    total = out5[pl.ds(depth * HD, HD)] + in5[1] + in5[2] + in5[3]
    in5[0] = total
    for group in range(8):
        rows8[0:HD, group * 128 : (group + 1) * 128] = in5[0, :, group, :]
    gradient = rows8[...]

    incoming = jnp.zeros((8, SL), jnp.float32)
    for level in range(NL - 1, -1, -1):
        cols = slice(level * SL, (level + 1) * SL)
        shift = gradient[:, cols] + incoming
        in3[0, level, :, 0, :] = shift[:HD, :128]
        in3[0, level, :, 1, :] = shift[:HD, 128:]
        if level:
            value = group_value(logit8[:, cols] + shift, legal[level : level + 1, :])
            incoming = hand_down(value, owners[level])

    def copy3(source, dz):
        slot = PLACES.index(source)
        there = PLACES.index((source - dz + 7) % NZ - 7)
        return copy(in3.at[slot], in3.at[there], send3.at[there], recv3.at[there], device(along(dz), j, x))

    def wait3(source):
        slot = PLACES.index(source)
        copy(in3.at[slot], in3.at[slot], send3.at[slot], recv3.at[slot], device(along(1), j, x)).wait_recv()

    straight = [copy3(0, dz) for dz in (HUB, -HUB) + NEAR]
    onward = [copy3(-HUB, k - HUB) for k in UP]
    onward_down = [copy3(HUB, k + HUB) for k in DOWN]
    for one in straight:
        one.start()
    wait3(-HUB)
    for one in onward:
        one.start()
    wait3(HUB)
    for one in onward_down:
        one.start()

    def copy4(step, part):
        slots = pl.ds(PARTS[part][0], PARTS[part][1] - PARTS[part][0])
        to_j = (j + step) % NJ
        return copy(
            in3.at[slots, to_j % NL],
            in4.at[j, slots],
            send4.at[part, step],
            recv4.at[part, j],
            device(z, to_j, x),
        )

    for part, (begin, end) in enumerate(PARTS):
        for slot in range(begin, end):
            if PLACES[slot] not in (0, HUB, -HUB):
                wait3(PLACES[slot])

        @pl.loop(1, NJ)
        def _(step):
            copy4(step, part).start()

    def place(from_j, block, slots):
        for slot in slots:
            rows = pl.ds(from_j // NL * HY + along(PLACES[slot]) * HZ + from_j % NL * HD, HD)
            shifts[rows] = block(slot)

    place(j, lambda slot: in3[slot, depth], range(NZ))

    for part, (begin, end) in enumerate(PARTS):
        whole = pl.ds(begin, end - begin)

        @pl.loop(1, NJ)
        def _(step):
            slot = (j + step) % NJ
            copy(
                in4.at[slot, whole],
                in4.at[slot, whole],
                send4.at[part, 0],
                recv4.at[part, slot],
                device(z, slot, x),
            ).wait_recv()
            place(slot, lambda one: in4[slot, one], range(begin, end))

    scores = logits[...] + jnp.concatenate([shifts[:, 0, :], shifts[:, 1, :]], axis=1)
    can = legal[pl.ds(depth, 1), :]
    value = group_value(scores, can)
    policy[...] = jnp.where(can > 0.0, scores - value, 0.0)
    passed[...] = hand_down(value, owners[depth])

    for i in range(NX):
        for other in range(1 if i == NX - 1 else 0, 2):
            copy1(i, other).wait_send()
    for i in range(NZ - 1):
        copy2(i).wait_send()
    for step in range(1, NL):
        copy5(step).wait_send()
        copy_l(step).wait_send()
    for one in straight + onward + onward_down:
        one.wait_send()

    @pl.loop(1, NJ)
    def _(step):
        for part in range(len(PARTS)):
            copy4(step, part).wait_send()


def local(reach, payoff, board_cards, hand_rank, logits, action_counts, parent_seq):
    table, onehot = hand_cards()
    vmem = pl.BlockSpec(memory_space=pltpu.VMEM)
    dma = pltpu.SemaphoreType.DMA
    f32, bf16, i16 = jnp.float32, jnp.bfloat16, jnp.int16
    return pl.pallas_call(
        kernel,
        name="prox",
        out_shape=(jax.ShapeDtypeStruct((HX, SL), f32), jax.ShapeDtypeStruct((HX, SL), f32)),
        in_specs=[pl.BlockSpec(memory_space=pl.ANY)] * 9,
        out_specs=(vmem, vmem),
        scratch_shapes=[
            pltpu.VMEM((NB * HX, SL), bf16),
            pltpu.VMEM((NB, 5), jnp.int32),
            pltpu.VMEM((NB, HANDS), jnp.int32),
            pltpu.VMEM((HX, SL), f32),
            pltpu.VMEM((NL, SL // ACT), jnp.int32),
            pltpu.VMEM((NL, SL // ACT), jnp.int32),
            pltpu.VMEM((8, HP), f32),
            pltpu.VMEM((HP, 128), bf16),
            dma((9,)),
            pltpu.VMEM((NB, HP), f32),
            pltpu.VMEM((HP, NB), f32),
            pltpu.VMEM((NX, 2, HY, SL), i16),
            pltpu.VMEM((NJ, HY, SL), i16),
            pltpu.VMEM((NZ, PAD, SL), i16),
            pltpu.VMEM((NZ - 1, PAD, SL), i16),
            pltpu.VMEM((8, SX), f32),
            pltpu.VMEM((8, SX), f32),
            pltpu.VMEM((SL, SX), bf16),
            pltpu.VMEM((HX, 2, 128), f32),
            pltpu.VMEM((NL, HD, 2, 128), f32),
            pltpu.VMEM((HY + 8, SL), f32),
            pltpu.VMEM((HZ, 8, 128), f32),
            pltpu.VMEM((NL, HD, 8, 128), f32),
            pltpu.VMEM((NZ, NL, HD, 2, 128), f32),
            pltpu.VMEM((NJ, NZ, HD, 2, 128), f32),
            pltpu.VMEM((HX, 2, 128), f32),
            pltpu.VMEM((NL, SL), f32),
            pltpu.VMEM((NL, SL, SL), bf16),
            dma((NX, 2)),
            dma((NJ,)),
            dma((NZ - 1,)),
            dma((NZ - 1,)),
            dma((NZ,)),
            dma((NZ,)),
            dma((len(PARTS), NJ)),
            dma((len(PARTS), NJ)),
            dma((NL,)),
            dma((NL,)),
            dma((NL,)),
            dma((NL,)),
            pltpu.SemaphoreType.REGULAR((2,)),
        ],
        compiler_params=pltpu.CompilerParams(
            collective_id=0, has_side_effects=True, vmem_limit_bytes=32 * 1024 * 1024
        ),
    )(
        *[
            pltpu.with_memory_space_constraint(operand, pltpu.HBM)
            for operand in (
                reach.reshape(NB * HX, SL),
                payoff,
                board_cards,
                hand_rank,
                logits,
                action_counts,
                parent_seq,
                jnp.asarray(table),
                jnp.asarray(onehot, jnp.bfloat16),
            )
        ]
    )


def solution(mesh):
    return jax.shard_map(
        local,
        mesh=mesh,
        in_specs=(
            P("board", "hand", "depth"),
            P("depth", None),
            P("board", None),
            P("board", None),
            P("hand", "depth"),
            P(),
            P(),
        ),
        out_specs=(P("hand", "depth"), P("hand", "depth")),
        check_vma=False,
    )
```

```python
import jax
import jax.numpy as jnp
import numpy as np
from jax import lax
from jax.experimental import pallas as pl
from jax.experimental.pallas import tpu as pltpu
from jax.sharding import PartitionSpec as P

CARDS = 52
HANDS = 1326
ACT = 4
NZ = 16
NX = 4
NL = 4
NJ = 8
HX = 384
HP = NX * HX
HY = HX // 2
HZ = HY // NZ
PAD = 16
SL = 256
SX = NL * SL
NB = 8
BOUND = float(NB * HX)
SCALE = 32767.0 / BOUND
LIVE = 45 * 44 // 2
BOUND_PLANE = float(2 * NB * LIVE)
SCALE_PLANE = 32700.0 / BOUND_PLANE
MESH = pl.DeviceIdType.MESH
NEAR = (1, -1, 2, -2)
UP = (3, 4, 6, 7, 8)
DOWN = (-3, -4, -6, -7)
HUB = 5
FAR_FIRST = (8, 7, -7, 6, -6, 5, -5, 4, -4, 3, -3, 2, -2, 1, -1)
GREET = (1, -1, 2, -2)
PLACES = (0, 1, -1, 2, -2, 5, -5, -3, -4, -6, -7, 3, 4, 6, 7, 8)
PARTS = ((0, 7), (7, 11), (11, 16))
ROW_PEERS = 2 * NX - 1
CHUNKS = 3
NAN = float("nan")


def hand_cards():
    first, second = np.triu_indices(CARDS, 1)
    table = np.full((8, HP), -1.0, np.float32)
    table[0, :HANDS] = first
    table[1, :HANDS] = second
    onehot = np.zeros((HP, 128), np.float32)
    onehot[np.arange(HANDS), first] = 1.0
    onehot[np.arange(HANDS), second] = 1.0
    return table, onehot


def dot_t(a, b):
    return lax.dot_general(a, b, (((1,), (1,)), ((), ())), preferred_element_type=jnp.float32)


def group_reduce(x, op):
    lane = lax.broadcasted_iota(jnp.int32, x.shape, 1)
    near = jnp.where(lane % 2 == 0, pltpu.roll(x, 127, 1), pltpu.roll(x, 1, 1))
    x = op(x, near)
    far = jnp.where(lane % 4 < 2, pltpu.roll(x, 126, 1), pltpu.roll(x, 2, 1))
    return op(x, far)


def group_value(scores, legal):
    parts = []
    for half in range(2):
        cols = slice(half * 128, half * 128 + 128)
        masked = jnp.where(legal[:, cols] > 0.0, scores[:, cols], -jnp.inf)
        top = group_reduce(masked, jnp.maximum)
        total = group_reduce(jnp.exp(masked - top), jnp.add)
        parts.append(top + jnp.log(total))
    return jnp.concatenate(parts, axis=1)


def hand_down(value, owner_t):
    a = value.astype(jnp.bfloat16)
    rest = value - a.astype(jnp.float32)
    b = rest.astype(jnp.bfloat16)
    c = (rest - b.astype(jnp.float32)).astype(jnp.bfloat16)
    return dot_t(a, owner_t) + dot_t(b, owner_t) + dot_t(c, owner_t)


def kernel(
    reach_hbm,
    payoff,
    cards_hbm,
    rank_hbm,
    logits_hbm,
    counts_hbm,
    parents_hbm,
    table_hbm,
    onehot_hbm,
    scores,
    own_legal,
    own_owner,
    reach,
    cards,
    rank,
    logits,
    counts,
    parents,
    table,
    onehot,
    load,
    ranks,
    ranks_t,
    out1,
    in1,
    out2,
    in2,
    rows16,
    logit16,
    pay,
    logit_tiles,
    logit_rows,
    total2,
    out5,
    in5,
    out3,
    in3,
    in4,
    shifts,
    legal,
    owners,
    send1,
    recv1,
    send2,
    recv2,
    send3,
    recv3,
    send4,
    recv4,
    send5,
    recv5,
    send_l,
    recv_l,
    know,
):
    board = lax.axis_index("board")
    depth = lax.axis_index("depth")
    x = lax.axis_index("hand")
    z = board // 2
    y_lo = board % 2
    j = y_lo * NL + depth

    def device(to_z, to_j, to_x):
        return (to_z * 2 + to_j // NL, to_j % NL, to_x)

    def along(dz):
        return (z + dz + NZ) % NZ

    def copy(src, dst, send, recv, to):
        return pltpu.make_async_remote_copy(
            src_ref=src, dst_ref=dst, send_sem=send, recv_sem=recv, device_id=to, device_id_type=MESH
        )

    loads = [
        pltpu.make_async_copy(src, dst, load.at[i])
        for i, (src, dst) in enumerate(
            [
                (rank_hbm, rank),
                (cards_hbm, cards),
                (table_hbm, table),
                (onehot_hbm, onehot),
                (reach_hbm, reach),
                (payoff, pay),
                (logits_hbm, logits),
                (counts_hbm, counts),
                (parents_hbm, parents),
            ]
        )
    ]
    for one in loads:
        one.start()

    def hop_x(i):
        return (x + 2 + i + i * (i - 1) // 2) % NX

    barrier = pltpu.get_barrier_semaphore()
    for i in range(NX):
        for other in range(1 if i == NX - 1 else 0, 2):
            to_j = (y_lo + other) % 2 * NL + depth
            pl.semaphore_signal(barrier, inc=1, device_id=device(z, to_j, hop_x(i)), device_id_type=MESH)
    for step in range(1, NL):
        to_j = y_lo * NL + (depth + step) % NL
        pl.semaphore_signal(barrier, inc=1, device_id=device(z, to_j, x), device_id_type=MESH)
    for dz in GREET:
        pl.semaphore_signal(barrier, inc=1, device_id=device(along(dz), j, x), device_id_type=MESH)

    for one in loads[:3]:
        one.wait()

    ranks[...] = jnp.full((NB, HP), NAN, jnp.float32)
    ranks[:, :HANDS] = rank[...].astype(jnp.float32)
    first = table[0:1, :]
    second = table[1:2, :]
    hit = first < 0.0
    for card in range(5):
        one = cards[:, card : card + 1].astype(jnp.float32)
        hit = hit | (first == one) | (second == one)
    ranks[...] = jnp.where(hit, NAN, ranks[...])
    ranks_t[...] = ranks[...].T

    own = pl.ds(pl.multiple_of(x * HX, HX), HX)

    loads[3].wait()
    loads[4].wait()

    def partial(to_x):
        rows = pl.ds(pl.multiple_of(to_x * HX, HX), HX)
        shared = dot_t(onehot[rows, :], onehot[own, :])
        apart = jnp.where(shared > 0.0, 0.0, 1.0)
        minus = -apart
        total = jnp.zeros((HX, SL), jnp.float32)
        for pair in range(NB // 2):
            sides = []
            for b in (2 * pair, 2 * pair + 1):
                mine = ranks_t[rows, b : b + 1]
                theirs = ranks[b : b + 1, own]
                sign = jnp.where(theirs < mine, apart, jnp.where(theirs > mine, minus, 0.0))
                sides.append(sign.astype(jnp.bfloat16))
            total += jnp.dot(
                jnp.concatenate(sides, axis=1),
                reach[2 * HX * pair : 2 * HX * (pair + 1), :],
                preferred_element_type=jnp.float32,
            )
        return jnp.round(total * SCALE).astype(jnp.int32).astype(jnp.int16)

    me1 = x * 2 + y_lo

    def copy1(i, other):
        to_x, to_y = hop_x(i), (y_lo + other) % 2
        return copy(
            out1.at[to_x, to_y],
            in1.at[me1],
            send1.at[i, other],
            recv1.at[me1],
            device(z, to_y * NL + depth, to_x),
        )

    @pl.loop(0, NX)
    def _(i):
        to_x = hop_x(i)
        out1[to_x] = partial(to_x).reshape(2, HY, SL)

        @pl.when(i == 0)
        def _():
            pl.semaphore_wait(barrier, ROW_PEERS + NL - 1 + len(GREET))
            for dz in (2, -2):
                pl.semaphore_signal(
                    know.at[0], inc=1, device_id=device(along(dz), j, x), device_id_type=MESH
                )

        copy1(i, 1).start()

        @pl.when(i < NX - 1)
        def _():
            copy1(i, 0).start()

    pl.semaphore_wait(know.at[0], 2)
    for dz in (4, -4):
        pl.semaphore_signal(know.at[1], inc=1, device_id=device(along(dz), j, x), device_id_type=MESH)
    in1[me1] = out1[x, y_lo]

    for one in loads[5:]:
        one.wait()

    for half in range(2):
        logit_tiles[:, half, :] = logits[:, half * 128 : half * 128 + 128]

    def depth_peer(step):
        return (depth + step) % NL

    def copy_l(step):
        to = depth_peer(step)
        return copy(
            logit_tiles.at[pl.ds(y_lo * HY + z * HZ, HZ)],
            logit_rows.at[depth],
            send_l.at[step],
            recv_l.at[depth],
            device(z, y_lo * NL + to, x),
        )

    for step in range(1, NL):
        copy_l(step).start()
    logit_rows[depth] = logit_tiles[pl.ds(y_lo * HY + z * HZ, HZ)]

    spread = (
        lax.broadcasted_iota(jnp.int32, (SL // ACT, SL), 0)
        == lax.broadcasted_iota(jnp.int32, (SL // ACT, SL), 1) // ACT
    ).astype(jnp.bfloat16)
    lane = lax.broadcasted_iota(jnp.int32, (NL, SL), 1) % ACT
    counts_wide = jnp.dot(
        counts[...].astype(jnp.float32).astype(jnp.bfloat16), spread, preferred_element_type=jnp.float32
    )
    parents_wide = jnp.dot(
        parents[...].astype(jnp.float32).astype(jnp.bfloat16), spread, preferred_element_type=jnp.float32
    )
    legal[...] = jnp.where(lane.astype(jnp.float32) < counts_wide, 1.0, 0.0)
    parents_wide = jnp.where(lane == 0, parents_wide, -1.0)
    seq = lax.broadcasted_iota(jnp.int32, (SL, SL), 0).astype(jnp.float32)
    for level in range(NL):
        owners[level] = jnp.where(seq == parents_wide[level : level + 1, :], 1.0, 0.0).astype(jnp.bfloat16)

    total = in1[me1].astype(jnp.int32)
    for i in range(ROW_PEERS):
        slot = (me1 + 1 + i) % NJ
        copy(
            in1.at[slot], in1.at[slot], send1.at[0, 0], recv1.at[slot], device(z, j, (x + 1) % NX)
        ).wait_recv()
        total += in1[slot].astype(jnp.int32)
    total2[:HY, :] = total.astype(jnp.float32) * (SCALE_PLANE / SCALE)
    total2[HY:, :] = jnp.zeros((8, SL), jnp.float32)
    for to_z in range(NZ):
        rows = jnp.round(total2[to_z * HZ : to_z * HZ + PAD, :])
        out2[to_z] = rows.astype(jnp.int32).astype(jnp.int16)

    pl.semaphore_wait(know.at[1], 2)

    def copy2(i):
        dz = FAR_FIRST[i]
        return copy(
            out2.at[along(dz)], in2.at[i], send2.at[i], recv2.at[i], device(along(dz), j, x)
        )

    for i in range(NZ - 1):
        copy2(i).start()

    rows16[...] = jnp.zeros((PAD, SX), jnp.float32)
    logit16[...] = jnp.zeros((PAD, SX), jnp.float32)
    for step in range(1, NL):
        slot = depth_peer(step)
        copy(
            logit_rows.at[slot], logit_rows.at[slot], send_l.at[0], recv_l.at[slot], device(z, j, (x + 1) % NX)
        ).wait_recv()
    for group in range(8):
        logit16[0:HZ, group * 128 : (group + 1) * 128] = logit_rows[group // 2, :, group % 2, :]

    total = out2[z].astype(jnp.int32)
    for i in range(NZ - 2, -1, -1):
        copy2(i).wait_recv()
        total += in2[i].astype(jnp.int32)
    counter = total.astype(jnp.float32)
    high = counter.astype(jnp.bfloat16).astype(jnp.float32)
    both = jnp.concatenate([high, counter - high], axis=0).astype(jnp.bfloat16)
    partial_gradient = jnp.dot(both, pay[...], preferred_element_type=jnp.float32)
    partial_gradient = (partial_gradient[:PAD] + partial_gradient[PAD:]) * (1.0 / SCALE_PLANE)
    for group in range(8):
        out5[:, group, :] = partial_gradient[:HZ, group * 128 : (group + 1) * 128]

    def copy5(step):
        to = depth_peer(step)
        return copy(
            out5,
            in5.at[step],
            send5.at[step],
            recv5.at[step],
            device(z, y_lo * NL + to, x),
        )

    for step in (2, 1, 3):
        copy5(step).start()
    for step in range(1, NL):
        copy5(step).wait_recv()
    total = out5[...] + in5[1] + in5[2] + in5[3]
    in5[0] = total
    for group in range(8):
        rows16[0:HZ, group * 128 : (group + 1) * 128] = in5[0, :, group, :]
    gradient = rows16[...]

    incoming = jnp.zeros((PAD, SL), jnp.float32)
    for level in range(NL - 1, -1, -1):
        cols = slice(level * SL, (level + 1) * SL)
        shift = gradient[:, cols] + incoming
        out3[level, :, 0, :] = shift[:HZ, :128]
        out3[level, :, 1, :] = shift[:HZ, 128:]
        if level:
            value = group_value(logit16[:, cols] + shift, legal[level : level + 1, :])
            incoming = hand_down(value, owners[level])

    in3[0] = out3[depth]

    def copy3(source, dz):
        slot = PLACES.index(source)
        there = PLACES.index((source - dz + 7) % NZ - 7)
        return copy(in3.at[slot], in3.at[there], send3.at[there], recv3.at[there], device(along(dz), j, x))

    def wait3(source):
        slot = PLACES.index(source)
        copy(in3.at[slot], in3.at[slot], send3.at[slot], recv3.at[slot], device(along(1), j, x)).wait_recv()

    straight = [copy3(0, dz) for dz in (HUB, -HUB) + NEAR]
    onward = [copy3(-HUB, k - HUB) for k in UP]
    onward_down = [copy3(HUB, k + HUB) for k in DOWN]
    for one in straight:
        one.start()
    wait3(-HUB)
    for one in onward:
        one.start()
    wait3(HUB)
    for one in onward_down:
        one.start()

    def copy4(part):
        slots = pl.ds(PARTS[part][0], PARTS[part][1] - PARTS[part][0])
        return copy(
            in3.at[slots],
            in4.at[slots],
            send4.at[part],
            recv4.at[part],
            device(z, (1 - y_lo) * NL + depth, x),
        )

    def place(block, half, slot):
        shifts[pl.ds(half * HY + along(PLACES[slot]) * HZ, HZ)] = block[slot]

    for part, (begin, end) in enumerate(PARTS):
        for slot in range(begin, end):
            if PLACES[slot] not in (0, HUB, -HUB):
                wait3(PLACES[slot])
        copy4(part).start()
        for slot in range(begin, end):
            place(in3, y_lo, slot)
    for part, (begin, end) in enumerate(PARTS):
        copy4(part).wait_recv()
        for slot in range(begin, end):
            place(in4, 1 - y_lo, slot)

    scores[...] = logits[...] + jnp.concatenate([shifts[:, 0, :], shifts[:, 1, :]], axis=1)
    own_legal[...] = jnp.broadcast_to(legal[pl.ds(depth, 1), :], (8, SL))
    own_owner[...] = owners[depth]

    for i in range(NX):
        for other in range(1 if i == NX - 1 else 0, 2):
            copy1(i, other).wait_send()
    for i in range(NZ - 1):
        copy2(i).wait_send()
    for step in range(1, NL):
        copy5(step).wait_send()
        copy_l(step).wait_send()
    for one in straight + onward + onward_down:
        one.wait_send()

    for part in range(len(PARTS)):
        copy4(part).wait_send()


def last_pass(scores, legal, owner, policy_hbm, passed_hbm, policy, passed, stores):
    can = legal[0:1, :]
    copies = []
    for i in range(CHUNKS):
        rows = pl.ds(i * (HX // CHUNKS), HX // CHUNKS)
        value = group_value(scores[rows, :], can)
        policy[rows, :] = jnp.where(can > 0.0, scores[rows, :] - value, 0.0)
        copies.append(pltpu.make_async_copy(policy.at[rows], policy_hbm.at[rows], stores.at[0, i]))
        copies[-1].start()
        passed[rows, :] = hand_down(value, owner[...])
        copies.append(pltpu.make_async_copy(passed.at[rows], passed_hbm.at[rows], stores.at[1, i]))
        copies[-1].start()
    for one in copies:
        one.wait()


def local(reach, payoff, board_cards, hand_rank, logits, action_counts, parent_seq):
    table, onehot = hand_cards()
    vmem = pl.BlockSpec(memory_space=pltpu.VMEM)
    dma = pltpu.SemaphoreType.DMA
    f32, bf16, i16 = jnp.float32, jnp.bfloat16, jnp.int16
    scores, legal, owner = pl.pallas_call(
        kernel,
        name="prox",
        out_shape=(
            jax.ShapeDtypeStruct((HX, SL), f32),
            jax.ShapeDtypeStruct((8, SL), f32),
            jax.ShapeDtypeStruct((SL, SL), bf16),
        ),
        in_specs=[pl.BlockSpec(memory_space=pl.ANY)] * 9,
        out_specs=(vmem, vmem, vmem),
        scratch_shapes=[
            pltpu.VMEM((NB * HX, SL), bf16),
            pltpu.VMEM((NB, 5), jnp.int32),
            pltpu.VMEM((NB, HANDS), jnp.int32),
            pltpu.VMEM((HX, SL), f32),
            pltpu.VMEM((NL, SL // ACT), jnp.int32),
            pltpu.VMEM((NL, SL // ACT), jnp.int32),
            pltpu.VMEM((8, HP), f32),
            pltpu.VMEM((HP, 128), bf16),
            dma((9,)),
            pltpu.VMEM((NB, HP), f32),
            pltpu.VMEM((HP, NB), f32),
            pltpu.VMEM((NX, 2, HY, SL), i16),
            pltpu.VMEM((NJ, HY, SL), i16),
            pltpu.VMEM((NZ, PAD, SL), i16),
            pltpu.VMEM((NZ - 1, PAD, SL), i16),
            pltpu.VMEM((PAD, SX), f32),
            pltpu.VMEM((PAD, SX), f32),
            pltpu.VMEM((SL, SX), bf16),
            pltpu.VMEM((HX, 2, 128), f32),
            pltpu.VMEM((NL, HZ, 2, 128), f32),
            pltpu.VMEM((HY + 8, SL), f32),
            pltpu.VMEM((HZ, 8, 128), f32),
            pltpu.VMEM((NL, HZ, 8, 128), f32),
            pltpu.VMEM((NL, HZ, 2, 128), f32),
            pltpu.VMEM((NZ, HZ, 2, 128), f32),
            pltpu.VMEM((NZ, HZ, 2, 128), f32),
            pltpu.VMEM((HX, 2, 128), f32),
            pltpu.VMEM((NL, SL), f32),
            pltpu.VMEM((NL, SL, SL), bf16),
            dma((NX, 2)),
            dma((NJ,)),
            dma((NZ - 1,)),
            dma((NZ - 1,)),
            dma((NZ,)),
            dma((NZ,)),
            dma((len(PARTS),)),
            dma((len(PARTS),)),
            dma((NL,)),
            dma((NL,)),
            dma((NL,)),
            dma((NL,)),
            pltpu.SemaphoreType.REGULAR((2,)),
        ],
        compiler_params=pltpu.CompilerParams(
            collective_id=0, has_side_effects=True, vmem_limit_bytes=32 * 1024 * 1024
        ),
    )(
        *[
            pltpu.with_memory_space_constraint(operand, pltpu.HBM)
            for operand in (
                reach.reshape(NB * HX, SL),
                payoff,
                board_cards,
                hand_rank,
                logits,
                action_counts,
                parent_seq,
                jnp.asarray(table),
                jnp.asarray(onehot, jnp.bfloat16),
            )
        ]
    )
    hbm = pl.BlockSpec(memory_space=pl.ANY)
    return pl.pallas_call(
        last_pass,
        name="last_pass",
        out_shape=(jax.ShapeDtypeStruct((HX, SL), f32), jax.ShapeDtypeStruct((HX, SL), f32)),
        in_specs=[vmem] * 3,
        out_specs=(hbm, hbm),
        scratch_shapes=[pltpu.VMEM((HX, SL), f32), pltpu.VMEM((HX, SL), f32), dma((2, CHUNKS))],
        compiler_params=pltpu.CompilerParams(vmem_limit_bytes=32 * 1024 * 1024),
    )(scores, legal, owner)


def solution(mesh):
    return jax.shard_map(
        local,
        mesh=mesh,
        in_specs=(
            P("board", "hand", "depth"),
            P("depth", None),
            P("board", None),
            P("board", None),
            P("hand", "depth"),
            P(),
            P(),
        ),
        out_specs=(P("hand", "depth"), P("hand", "depth")),
        check_vma=False,
    )
```

```python
import jax
import jax.numpy as jnp
import numpy as np
from jax import lax
from jax.experimental import pallas as pl
from jax.experimental.pallas import tpu as pltpu
from jax.sharding import PartitionSpec as P

CARDS = 52
HANDS = 1326
ACT = 4
NZ = 16
NX = 4
NL = 4
NJ = 8
HX = 384
HP = NX * HX
HY = HX // 2
HZ = HY // NZ
PAD = 16
SL = 256
SX = NL * SL
NB = 8
BOUND = float(NB * HX)
SCALE = 32767.0 / BOUND
LIVE = 45 * 44 // 2
BOUND_PLANE = float(2 * NB * LIVE)
SCALE_PLANE = 32700.0 / BOUND_PLANE
MESH = pl.DeviceIdType.MESH
NEAR = (1, -1, 2, -2)
UP = (3, 4, 6, 7, 8)
DOWN = (-3, -4, -6, -7)
HUB = 5
FAR_FIRST = (8, 7, -7, 6, -6, 5, -5, 4, -4, 3, -3, 2, -2, 1, -1)
GREET = (1, -1, 2, -2)
PLACES = (0, 1, -1, 2, -2, 5, -5, -3, -4, -6, -7, 3, 4, 6, 7, 8)
PARTS = ((0, 7), (7, 11), (11, 16))
ROW_PEERS = 2 * NX - 1
CHUNKS = 2
NAN = float("nan")


def hand_cards():
    first, second = np.triu_indices(CARDS, 1)
    table = np.full((8, HP), -1.0, np.float32)
    table[0, :HANDS] = first
    table[1, :HANDS] = second
    onehot = np.zeros((HP, 128), np.float32)
    onehot[np.arange(HANDS), first] = 1.0
    onehot[np.arange(HANDS), second] = 1.0
    return table, onehot


def dot_t(a, b):
    return lax.dot_general(a, b, (((1,), (1,)), ((), ())), preferred_element_type=jnp.float32)


def group_reduce(x, op):
    lane = lax.broadcasted_iota(jnp.int32, x.shape, 1)
    near = jnp.where(lane % 2 == 0, pltpu.roll(x, 127, 1), pltpu.roll(x, 1, 1))
    x = op(x, near)
    far = jnp.where(lane % 4 < 2, pltpu.roll(x, 126, 1), pltpu.roll(x, 2, 1))
    return op(x, far)


def group_value(scores, legal):
    parts = []
    for half in range(2):
        cols = slice(half * 128, half * 128 + 128)
        masked = jnp.where(legal[:, cols] > 0.0, scores[:, cols], -jnp.inf)
        top = group_reduce(masked, jnp.maximum)
        total = group_reduce(jnp.exp(masked - top), jnp.add)
        parts.append(top + jnp.log(total))
    return jnp.concatenate(parts, axis=1)


def hand_down(value, owner_t):
    a = value.astype(jnp.bfloat16)
    rest = value - a.astype(jnp.float32)
    b = rest.astype(jnp.bfloat16)
    c = (rest - b.astype(jnp.float32)).astype(jnp.bfloat16)
    return dot_t(a, owner_t) + dot_t(b, owner_t) + dot_t(c, owner_t)


def kernel(
    reach_hbm,
    payoff,
    cards_hbm,
    rank_hbm,
    logits_hbm,
    counts_hbm,
    parents_hbm,
    table_hbm,
    onehot_hbm,
    scores,
    own_policy,
    own_passed,
    own_legal,
    own_owner,
    reach,
    cards,
    rank,
    logits,
    counts,
    parents,
    table,
    onehot,
    load,
    ranks,
    ranks_t,
    out1,
    in1,
    out2,
    in2,
    rows16,
    logit16,
    pay,
    logit_tiles,
    logit_rows,
    total2,
    halves,
    out5,
    in5,
    out3,
    in3,
    in4,
    shifts,
    legal,
    owners,
    send1,
    recv1,
    send2,
    recv2,
    send3,
    recv3,
    send4,
    recv4,
    send5,
    recv5,
    send_l,
    recv_l,
    know,
):
    board = lax.axis_index("board")
    depth = lax.axis_index("depth")
    x = lax.axis_index("hand")
    z = board // 2
    y_lo = board % 2
    j = y_lo * NL + depth

    def device(to_z, to_j, to_x):
        return (to_z * 2 + to_j // NL, to_j % NL, to_x)

    def along(dz):
        return (z + dz + NZ) % NZ

    def copy(src, dst, send, recv, to):
        return pltpu.make_async_remote_copy(
            src_ref=src, dst_ref=dst, send_sem=send, recv_sem=recv, device_id=to, device_id_type=MESH
        )

    def loaded(i, src, dst):
        return pltpu.make_async_copy(src, dst, load.at[i])

    loads = [
        loaded(0, rank_hbm, rank),
        loaded(1, cards_hbm, cards),
        loaded(2, table_hbm, table),
        loaded(3, onehot_hbm, onehot),
    ]
    for b in range(NB):
        rows = pl.ds(b * HX, HX)
        loads.append(loaded(4 + b, reach_hbm.at[rows], reach.at[rows]))
    later = [
        loaded(4 + NB, logits_hbm, logits),
        loaded(5 + NB, counts_hbm, counts),
        loaded(6 + NB, parents_hbm, parents),
        loaded(7 + NB, payoff, pay),
    ]
    for one in loads:
        one.start()

    def hop_x(i):
        return (x + 2 + i + i * (i - 1) // 2) % NX

    barrier = pltpu.get_barrier_semaphore()
    for i in range(NX):
        for other in range(1 if i == NX - 1 else 0, 2):
            to_j = (y_lo + other) % 2 * NL + depth
            pl.semaphore_signal(barrier, inc=1, device_id=device(z, to_j, hop_x(i)), device_id_type=MESH)
    for step in range(1, NL):
        to_j = y_lo * NL + (depth + step) % NL
        pl.semaphore_signal(barrier, inc=1, device_id=device(z, to_j, x), device_id_type=MESH)
    for dz in GREET:
        pl.semaphore_signal(barrier, inc=1, device_id=device(along(dz), j, x), device_id_type=MESH)

    for one in loads[:3]:
        one.wait()

    ranks[...] = jnp.full((NB, HP), NAN, jnp.float32)
    ranks[:, :HANDS] = rank[...].astype(jnp.float32)
    first = table[0:1, :]
    second = table[1:2, :]
    hit = first < 0.0
    for card in range(5):
        one = cards[:, card : card + 1].astype(jnp.float32)
        hit = hit | (first == one) | (second == one)
    ranks[...] = jnp.where(hit, NAN, ranks[...])
    ranks_t[...] = ranks[...].T

    own = pl.ds(pl.multiple_of(x * HX, HX), HX)

    for one in loads[3:]:
        one.wait()
    for one in later:
        one.start()

    def partial(to_x):
        rows = pl.ds(pl.multiple_of(to_x * HX, HX), HX)
        shared = dot_t(onehot[rows, :], onehot[own, :])
        apart = jnp.where(shared > 0.0, 0.0, 1.0)
        minus = -apart
        total = jnp.zeros((HX, SL), jnp.float32)
        for pair in range(NB // 2):
            sides = []
            for b in (2 * pair, 2 * pair + 1):
                mine = ranks_t[rows, b : b + 1]
                theirs = ranks[b : b + 1, own]
                sign = jnp.where(theirs < mine, apart, jnp.where(theirs > mine, minus, 0.0))
                sides.append(sign.astype(jnp.bfloat16))
            total += jnp.dot(
                jnp.concatenate(sides, axis=1),
                reach[2 * HX * pair : 2 * HX * (pair + 1), :],
                preferred_element_type=jnp.float32,
            )
        return jnp.round(total * SCALE).astype(jnp.int32).astype(jnp.int16)

    me1 = x * 2 + y_lo

    def copy1(i, other):
        to_x, to_y = hop_x(i), (y_lo + other) % 2
        return copy(
            out1.at[to_x, to_y],
            in1.at[me1],
            send1.at[i, other],
            recv1.at[me1],
            device(z, to_y * NL + depth, to_x),
        )

    @pl.loop(0, NX)
    def _(i):
        to_x = hop_x(i)
        out1[to_x] = partial(to_x).reshape(2, HY, SL)

        @pl.when(i == 0)
        def _():
            pl.semaphore_wait(barrier, ROW_PEERS + NL - 1 + len(GREET))
            for dz in (2, -2):
                pl.semaphore_signal(
                    know.at[0], inc=1, device_id=device(along(dz), j, x), device_id_type=MESH
                )

        copy1(i, 1).start()

        @pl.when(i < NX - 1)
        def _():
            copy1(i, 0).start()

    pl.semaphore_wait(know.at[0], 2)
    for dz in (4, -4):
        pl.semaphore_signal(know.at[1], inc=1, device_id=device(along(dz), j, x), device_id_type=MESH)
    in1[me1] = out1[x, y_lo]

    for one in later:
        one.wait()

    for half in range(2):
        logit_tiles[:, half, :] = logits[:, half * 128 : half * 128 + 128]

    def depth_peer(step):
        return (depth + step) % NL

    def copy_l(step):
        to = depth_peer(step)
        return copy(
            logit_tiles.at[pl.ds(y_lo * HY + z * HZ, HZ)],
            logit_rows.at[depth],
            send_l.at[step],
            recv_l.at[depth],
            device(z, y_lo * NL + to, x),
        )

    for step in range(1, NL):
        copy_l(step).start()
    logit_rows[depth] = logit_tiles[pl.ds(y_lo * HY + z * HZ, HZ)]

    spread = (
        lax.broadcasted_iota(jnp.int32, (SL // ACT, SL), 0)
        == lax.broadcasted_iota(jnp.int32, (SL // ACT, SL), 1) // ACT
    ).astype(jnp.bfloat16)
    lane = lax.broadcasted_iota(jnp.int32, (NL, SL), 1) % ACT
    counts_wide = jnp.dot(
        counts[...].astype(jnp.float32).astype(jnp.bfloat16), spread, preferred_element_type=jnp.float32
    )
    parents_wide = jnp.dot(
        parents[...].astype(jnp.float32).astype(jnp.bfloat16), spread, preferred_element_type=jnp.float32
    )
    legal[...] = jnp.where(lane.astype(jnp.float32) < counts_wide, 1.0, 0.0)
    parents_wide = jnp.where(lane == 0, parents_wide, -1.0)
    seq = lax.broadcasted_iota(jnp.int32, (SL, SL), 0).astype(jnp.float32)
    for level in range(NL):
        owners[level] = jnp.where(seq == parents_wide[level : level + 1, :], 1.0, 0.0).astype(jnp.bfloat16)

    total = in1[me1].astype(jnp.int32)
    for i in range(ROW_PEERS):
        slot = (me1 + 1 + i) % NJ
        copy(
            in1.at[slot], in1.at[slot], send1.at[0, 0], recv1.at[slot], device(z, j, (x + 1) % NX)
        ).wait_recv()
        total += in1[slot].astype(jnp.int32)
    total2[...] = total.astype(jnp.float32) * (SCALE_PLANE / SCALE)
    for to_z in range(NZ):
        rows = total2[to_z * HZ : (to_z + 1) * HZ, :]
        rows = jnp.round(jnp.concatenate([rows[:, :128], rows[:, 128:]], axis=0))
        out2[to_z] = rows.astype(jnp.int32).astype(jnp.int16)

    pl.semaphore_wait(know.at[1], 2)

    def copy2(i):
        dz = FAR_FIRST[i]
        return copy(
            out2.at[along(dz)], in2.at[i], send2.at[i], recv2.at[i], device(along(dz), j, x)
        )

    for i in range(NZ - 1):
        copy2(i).start()

    rows16[...] = jnp.zeros((PAD, SX), jnp.float32)
    logit16[...] = jnp.zeros((PAD, SX), jnp.float32)
    for step in range(1, NL):
        slot = depth_peer(step)
        copy(
            logit_rows.at[slot], logit_rows.at[slot], send_l.at[0], recv_l.at[slot], device(z, j, (x + 1) % NX)
        ).wait_recv()
    for group in range(8):
        logit16[0:HZ, group * 128 : (group + 1) * 128] = logit_rows[group // 2, :, group % 2, :]

    total = out2[z].astype(jnp.int32)
    for i in range(NZ - 2, -1, -1):
        copy2(i).wait_recv()
        total += in2[i].astype(jnp.int32)
    halves[0 : 2 * HZ, :] = total.astype(jnp.float32)
    halves[2 * HZ :, :] = jnp.zeros((8, 128), jnp.float32)
    counter = jnp.concatenate([halves[0:PAD, :], halves[HZ : HZ + PAD, :]], axis=1)
    high = counter.astype(jnp.bfloat16).astype(jnp.float32)
    both = jnp.concatenate([high, counter - high], axis=0).astype(jnp.bfloat16)
    partial_gradient = jnp.dot(both, pay[...], preferred_element_type=jnp.float32)
    partial_gradient = (partial_gradient[:PAD] + partial_gradient[PAD:]) * (1.0 / SCALE_PLANE)
    for group in range(8):
        out5[:, group, :] = partial_gradient[:HZ, group * 128 : (group + 1) * 128]

    def copy5(step):
        to = depth_peer(step)
        return copy(
            out5,
            in5.at[step],
            send5.at[step],
            recv5.at[step],
            device(z, y_lo * NL + to, x),
        )

    for step in (2, 1, 3):
        copy5(step).start()
    for step in range(1, NL):
        copy5(step).wait_recv()
    total = out5[...] + in5[1] + in5[2] + in5[3]
    in5[0] = total
    for group in range(8):
        rows16[0:HZ, group * 128 : (group + 1) * 128] = in5[0, :, group, :]
    gradient = rows16[...]

    incoming = jnp.zeros((PAD, SL), jnp.float32)
    for level in range(NL - 1, -1, -1):
        cols = slice(level * SL, (level + 1) * SL)
        shift = gradient[:, cols] + incoming
        out3[level, :, 0, :] = shift[:HZ, :128]
        out3[level, :, 1, :] = shift[:HZ, 128:]
        if level:
            value = group_value(logit16[:, cols] + shift, legal[level : level + 1, :])
            incoming = hand_down(value, owners[level])

    in3[0] = out3[depth]

    def copy3(source, dz):
        slot = PLACES.index(source)
        there = PLACES.index((source - dz + 7) % NZ - 7)
        return copy(in3.at[slot], in3.at[there], send3.at[there], recv3.at[there], device(along(dz), j, x))

    def wait3(source):
        slot = PLACES.index(source)
        copy(in3.at[slot], in3.at[slot], send3.at[slot], recv3.at[slot], device(along(1), j, x)).wait_recv()

    straight = [copy3(0, dz) for dz in (HUB, -HUB) + NEAR]
    onward = [copy3(-HUB, k - HUB) for k in UP]
    onward_down = [copy3(HUB, k + HUB) for k in DOWN]
    for one in straight:
        one.start()
    wait3(-HUB)
    for one in onward:
        one.start()
    wait3(HUB)
    for one in onward_down:
        one.start()

    def copy4(part):
        slots = pl.ds(PARTS[part][0], PARTS[part][1] - PARTS[part][0])
        return copy(
            in3.at[slots],
            in4.at[slots],
            send4.at[part],
            recv4.at[part],
            device(z, (1 - y_lo) * NL + depth, x),
        )

    def place(block, half, slot):
        shifts[pl.ds(half * HY + along(PLACES[slot]) * HZ, HZ)] = block[slot]

    for part, (begin, end) in enumerate(PARTS):
        for slot in range(begin, end):
            if PLACES[slot] not in (0, HUB, -HUB):
                wait3(PLACES[slot])
        copy4(part).start()
        for slot in range(begin, end):
            place(in3, y_lo, slot)
    def half_scores(half):
        rows = pl.ds(half * HY, HY)
        here = logits[pl.ds(pl.multiple_of(half * HY, HY), HY), :]
        return here + jnp.concatenate([shifts[rows, 0, :], shifts[rows, 1, :]], axis=1)

    can = legal[pl.ds(depth, 1), :]
    own_legal[...] = jnp.broadcast_to(can, (8, SL))
    own_owner[...] = owners[depth]
    here = half_scores(y_lo)
    value = group_value(here, can)
    own_policy[...] = jnp.where(can > 0.0, here - value, 0.0)
    own_passed[...] = hand_down(value, owners[depth])

    for part, (begin, end) in enumerate(PARTS):
        copy4(part).wait_recv()
        for slot in range(begin, end):
            place(in4, 1 - y_lo, slot)
    scores[...] = half_scores(1 - y_lo)

    for i in range(NX):
        for other in range(1 if i == NX - 1 else 0, 2):
            copy1(i, other).wait_send()
    for i in range(NZ - 1):
        copy2(i).wait_send()
    for step in range(1, NL):
        copy5(step).wait_send()
        copy_l(step).wait_send()
    for one in straight + onward + onward_down:
        one.wait_send()

    for part in range(len(PARTS)):
        copy4(part).wait_send()


def last_pass(scores, own_policy, own_passed, legal, owner, policy_hbm, passed_hbm, policy, passed, stores):
    y_lo = lax.axis_index("board") % 2

    def store(src, dst, half, first, count, sem):
        rows = pl.ds(pl.multiple_of(half * HY + first, 8), count)
        one = pltpu.make_async_copy(src.at[pl.ds(first, count)], dst.at[rows], sem)
        one.start()
        return one

    copies = [
        store(own_policy, policy_hbm, y_lo, 0, HY, stores.at[0, CHUNKS]),
        store(own_passed, passed_hbm, y_lo, 0, HY, stores.at[1, CHUNKS]),
    ]
    can = legal[0:1, :]
    count = HY // CHUNKS
    for i in range(CHUNKS):
        rows = pl.ds(i * count, count)
        value = group_value(scores[rows, :], can)
        policy[rows, :] = jnp.where(can > 0.0, scores[rows, :] - value, 0.0)
        copies.append(store(policy, policy_hbm, 1 - y_lo, i * count, count, stores.at[0, i]))
        passed[rows, :] = hand_down(value, owner[...])
        copies.append(store(passed, passed_hbm, 1 - y_lo, i * count, count, stores.at[1, i]))
    for one in copies:
        one.wait()


def local(reach, payoff, board_cards, hand_rank, logits, action_counts, parent_seq):
    table, onehot = hand_cards()
    vmem = pl.BlockSpec(memory_space=pltpu.VMEM)
    dma = pltpu.SemaphoreType.DMA
    f32, bf16, i16 = jnp.float32, jnp.bfloat16, jnp.int16
    rest = pl.pallas_call(
        kernel,
        name="prox",
        out_shape=(
            jax.ShapeDtypeStruct((HY, SL), f32),
            jax.ShapeDtypeStruct((HY, SL), f32),
            jax.ShapeDtypeStruct((HY, SL), f32),
            jax.ShapeDtypeStruct((8, SL), f32),
            jax.ShapeDtypeStruct((SL, SL), bf16),
        ),
        in_specs=[pl.BlockSpec(memory_space=pl.ANY)] * 9,
        out_specs=(vmem,) * 5,
        scratch_shapes=[
            pltpu.VMEM((NB * HX, SL), bf16),
            pltpu.VMEM((NB, 5), jnp.int32),
            pltpu.VMEM((NB, HANDS), jnp.int32),
            pltpu.VMEM((HX, SL), f32),
            pltpu.VMEM((NL, SL // ACT), jnp.int32),
            pltpu.VMEM((NL, SL // ACT), jnp.int32),
            pltpu.VMEM((8, HP), f32),
            pltpu.VMEM((HP, 128), bf16),
            dma((NB + 8,)),
            pltpu.VMEM((NB, HP), f32),
            pltpu.VMEM((HP, NB), f32),
            pltpu.VMEM((NX, 2, HY, SL), i16),
            pltpu.VMEM((NJ, HY, SL), i16),
            pltpu.VMEM((NZ, 2 * HZ, 128), i16),
            pltpu.VMEM((NZ - 1, 2 * HZ, 128), i16),
            pltpu.VMEM((PAD, SX), f32),
            pltpu.VMEM((PAD, SX), f32),
            pltpu.VMEM((SL, SX), bf16),
            pltpu.VMEM((HX, 2, 128), f32),
            pltpu.VMEM((NL, HZ, 2, 128), f32),
            pltpu.VMEM((HY, SL), f32),
            pltpu.VMEM((2 * HZ + 8, 128), f32),
            pltpu.VMEM((HZ, 8, 128), f32),
            pltpu.VMEM((NL, HZ, 8, 128), f32),
            pltpu.VMEM((NL, HZ, 2, 128), f32),
            pltpu.VMEM((NZ, HZ, 2, 128), f32),
            pltpu.VMEM((NZ, HZ, 2, 128), f32),
            pltpu.VMEM((HX, 2, 128), f32),
            pltpu.VMEM((NL, SL), f32),
            pltpu.VMEM((NL, SL, SL), bf16),
            dma((NX, 2)),
            dma((NJ,)),
            dma((NZ - 1,)),
            dma((NZ - 1,)),
            dma((NZ,)),
            dma((NZ,)),
            dma((len(PARTS),)),
            dma((len(PARTS),)),
            dma((NL,)),
            dma((NL,)),
            dma((NL,)),
            dma((NL,)),
            pltpu.SemaphoreType.REGULAR((2,)),
        ],
        compiler_params=pltpu.CompilerParams(
            collective_id=0, has_side_effects=True, vmem_limit_bytes=32 * 1024 * 1024
        ),
    )(
        *[
            pltpu.with_memory_space_constraint(operand, pltpu.HBM)
            for operand in (
                reach.reshape(NB * HX, SL),
                payoff,
                board_cards,
                hand_rank,
                logits,
                action_counts,
                parent_seq,
                jnp.asarray(table),
                jnp.asarray(onehot, jnp.bfloat16),
            )
        ]
    )
    hbm = pl.BlockSpec(memory_space=pl.ANY)
    return pl.pallas_call(
        last_pass,
        name="last_pass",
        out_shape=(jax.ShapeDtypeStruct((HX, SL), f32), jax.ShapeDtypeStruct((HX, SL), f32)),
        in_specs=[vmem] * 5,
        out_specs=(hbm, hbm),
        scratch_shapes=[pltpu.VMEM((HY, SL), f32), pltpu.VMEM((HY, SL), f32), dma((2, CHUNKS + 1))],
        compiler_params=pltpu.CompilerParams(vmem_limit_bytes=32 * 1024 * 1024),
    )(*rest)


def solution(mesh):
    return jax.shard_map(
        local,
        mesh=mesh,
        in_specs=(
            P("board", "hand", "depth"),
            P("depth", None),
            P("board", None),
            P("board", None),
            P("hand", "depth"),
            P(),
            P(),
        ),
        out_specs=(P("hand", "depth"), P("hand", "depth")),
        check_vma=False,
    )
```

```python
import jax
import jax.numpy as jnp
import numpy as np
from jax import lax
from jax.experimental import pallas as pl
from jax.experimental.pallas import tpu as pltpu
from jax.sharding import PartitionSpec as P

CARDS = 52
HANDS = 1326
ACT = 4
NZ = 16
NX = 4
NL = 4
HX = 384
HP = NX * HX
HY = HX // 2
HH = HY // 2
HZ = HY // NZ
PAD = 16
SL = 256
SX = NL * SL
NB = 8
BOUND = float(2 * NB * HX)
SCALE = 32700.0 / BOUND
LIVE = 45 * 44 // 2
BOUND_PLANE = float(2 * NB * LIVE)
SCALE_PLANE = 32700.0 / BOUND_PLANE
MESH = pl.DeviceIdType.MESH
NEAR = (1, -1, 2, -2)
UP = (3, 4, 6, 7, 8)
DOWN = (-3, -4, -6, -7)
HUB = 5
FAR_FIRST = (8, 7, -7, 6, -6, 5, -5, 4, -4, 3, -3, 2, -2, 1, -1)
GREET = (1, -1, 2, -2)
PLACES = (0, 1, -1, 2, -2, 5, -5, -3, -4, -6, -7, 3, 4, 6, 7, 8)
PARTS = ((0, 7), (7, 11), (11, 16))
ROW_PEERS = 5
CHUNKS = 2
NAN = float("nan")


def hand_cards():
    first, second = np.triu_indices(CARDS, 1)
    table = np.full((8, HP), -1.0, np.float32)
    table[0, :HANDS] = first
    table[1, :HANDS] = second
    onehot = np.zeros((HP, 128), np.float32)
    onehot[np.arange(HANDS), first] = 1.0
    onehot[np.arange(HANDS), second] = 1.0
    return table, onehot


def dot_t(a, b):
    return lax.dot_general(a, b, (((1,), (1,)), ((), ())), preferred_element_type=jnp.float32)


def group_reduce(x, op):
    lane = lax.broadcasted_iota(jnp.int32, x.shape, 1)
    near = jnp.where(lane % 2 == 0, pltpu.roll(x, 127, 1), pltpu.roll(x, 1, 1))
    x = op(x, near)
    far = jnp.where(lane % 4 < 2, pltpu.roll(x, 126, 1), pltpu.roll(x, 2, 1))
    return op(x, far)


def group_value(scores, legal):
    parts = []
    for half in range(2):
        cols = slice(half * 128, half * 128 + 128)
        masked = jnp.where(legal[:, cols] > 0.0, scores[:, cols], -jnp.inf)
        top = group_reduce(masked, jnp.maximum)
        total = group_reduce(jnp.exp(masked - top), jnp.add)
        parts.append(top + jnp.log(total))
    return jnp.concatenate(parts, axis=1)


def hand_down(value, owner_t):
    a = value.astype(jnp.bfloat16)
    rest = value - a.astype(jnp.float32)
    b = rest.astype(jnp.bfloat16)
    c = (rest - b.astype(jnp.float32)).astype(jnp.bfloat16)
    return dot_t(a, owner_t) + dot_t(b, owner_t) + dot_t(c, owner_t)


def kernel(
    reach_hbm,
    payoff,
    cards_hbm,
    rank_hbm,
    logits_hbm,
    counts_hbm,
    parents_hbm,
    table_hbm,
    onehot_hbm,
    scores,
    own_policy,
    own_passed,
    own_legal,
    own_owner,
    reach,
    cards,
    rank,
    logits,
    counts,
    parents,
    table,
    onehot,
    load,
    ranks,
    ranks_t,
    out1,
    relay,
    in_x,
    in_y,
    out2,
    in2,
    rows16,
    logit16,
    pay,
    logit_tiles,
    logit_rows,
    total2,
    halves,
    out5,
    in5,
    out3,
    in3,
    in4,
    shifts,
    legal,
    owners,
    send1,
    recv1,
    send_r,
    recv_r,
    send2,
    recv2,
    send3,
    recv3,
    send4,
    recv4,
    send5,
    recv5,
    send_l,
    recv_l,
    know,
):
    board = lax.axis_index("board")
    depth = lax.axis_index("depth")
    x = lax.axis_index("hand")
    z = board // 2
    y_lo = board % 2
    j = y_lo * NL + depth

    def device(to_z, to_j, to_x):
        return (to_z * 2 + to_j // NL, to_j % NL, to_x)

    def along(dz):
        return (z + dz + NZ) % NZ

    def copy(src, dst, send, recv, to):
        return pltpu.make_async_remote_copy(
            src_ref=src, dst_ref=dst, send_sem=send, recv_sem=recv, device_id=to, device_id_type=MESH
        )

    def loaded(i, src, dst):
        return pltpu.make_async_copy(src, dst, load.at[i])

    loads = [
        loaded(0, rank_hbm, rank),
        loaded(1, cards_hbm, cards),
        loaded(2, table_hbm, table),
        loaded(3, onehot_hbm, onehot),
    ]
    for b in range(NB):
        rows = pl.ds(b * HX, HX)
        loads.append(loaded(4 + b, reach_hbm.at[rows], reach.at[rows]))
    later = [
        loaded(4 + NB, logits_hbm, logits),
        loaded(5 + NB, counts_hbm, counts),
        loaded(6 + NB, parents_hbm, parents),
        loaded(7 + NB, payoff, pay),
    ]
    for one in loads:
        one.start()

    def hop_x(i):
        return (x + 2 + i + i * (i - 1) // 2) % NX

    barrier = pltpu.get_barrier_semaphore()
    for i in (1, 2):
        for other in range(2):
            to_j = (y_lo + other) % 2 * NL + depth
            pl.semaphore_signal(barrier, inc=1, device_id=device(z, to_j, hop_x(i)), device_id_type=MESH)
    to_j = (1 - y_lo) * NL + depth
    pl.semaphore_signal(barrier, inc=1, device_id=device(z, to_j, x), device_id_type=MESH)
    for step in range(1, NL):
        to_j = y_lo * NL + (depth + step) % NL
        pl.semaphore_signal(barrier, inc=1, device_id=device(z, to_j, x), device_id_type=MESH)
    for dz in GREET:
        pl.semaphore_signal(barrier, inc=1, device_id=device(along(dz), j, x), device_id_type=MESH)

    for one in loads[:3]:
        one.wait()

    ranks[...] = jnp.full((NB, HP), NAN, jnp.float32)
    ranks[:, :HANDS] = rank[...].astype(jnp.float32)
    first = table[0:1, :]
    second = table[1:2, :]
    hit = first < 0.0
    for card in range(5):
        one = cards[:, card : card + 1].astype(jnp.float32)
        hit = hit | (first == one) | (second == one)
    ranks[...] = jnp.where(hit, NAN, ranks[...])
    ranks_t[...] = ranks[...].T

    own = pl.ds(pl.multiple_of(x * HX, HX), HX)

    for one in loads[3:]:
        one.wait()
    for one in later:
        one.start()

    def partial(to_x):
        rows = pl.ds(pl.multiple_of(to_x * HX, HX), HX)
        shared = dot_t(onehot[rows, :], onehot[own, :])
        apart = jnp.where(shared > 0.0, 0.0, 1.0)
        minus = -apart
        total = jnp.zeros((HX, SL), jnp.float32)
        for pair in range(NB // 2):
            sides = []
            for b in (2 * pair, 2 * pair + 1):
                mine = ranks_t[rows, b : b + 1]
                theirs = ranks[b : b + 1, own]
                sign = jnp.where(theirs < mine, apart, jnp.where(theirs > mine, minus, 0.0))
                sides.append(sign.astype(jnp.bfloat16))
            total += jnp.dot(
                jnp.concatenate(sides, axis=1),
                reach[2 * HX * pair : 2 * HX * (pair + 1), :],
                preferred_element_type=jnp.float32,
            )
        return jnp.round(total * SCALE).astype(jnp.int32).astype(jnp.int16)

    def half_rows(part):
        return pl.ds(part * HH, HH)

    def copy_r(part):
        return copy(
            out1.at[hop_x(0), pl.ds(0, 2), half_rows(part)],
            relay.at[part],
            send_r.at[part],
            recv_r.at[part],
            device(z, j, hop_x(2 - part)),
        )

    def copy1(i, other, part):
        to_x, to_y, way = hop_x(i), (y_lo + other) % 2, 2 - i
        return copy(
            out1.at[to_x, to_y, half_rows(part)],
            in_x.at[way, y_lo, half_rows(part)],
            send1.at[way, other, part],
            recv1.at[way, y_lo, part],
            device(z, to_y * NL + depth, to_x),
        )

    copy_y = copy(
        out1.at[x, 1 - y_lo], in_y, send_r.at[2], recv_r.at[2], device(z, (1 - y_lo) * NL + depth, x)
    )

    @pl.loop(0, NX)
    def _(i):
        to_x = hop_x(i)
        out1[to_x] = partial(to_x).reshape(2, HY, SL)

        @pl.when(i == 0)
        def _():
            pl.semaphore_wait(barrier, ROW_PEERS + NL - 1 + len(GREET))
            for dz in (2, -2):
                pl.semaphore_signal(
                    know.at[0], inc=1, device_id=device(along(dz), j, x), device_id_type=MESH
                )
            copy_r(0).start()
            copy_r(1).start()

        @pl.when(i == 1)
        def _():
            copy1(1, 1, 0).start()
            copy1(1, 0, 0).start()

        @pl.when(i == 2)
        def _():
            copy1(2, 1, 1).start()
            copy1(2, 0, 1).start()

    copy_y.start()
    for i, part in ((1, 1), (2, 0)):
        copy_r(part).wait_recv()
        to_x = hop_x(i)
        both_rows = slice(part * HH, part * HH + HH)
        here = out1[to_x, :, both_rows, :].astype(jnp.int32)
        out1[to_x, :, both_rows, :] = (here + relay[part].astype(jnp.int32)).astype(jnp.int16)
        copy1(i, 1, part).start()
        copy1(i, 0, part).start()

    pl.semaphore_wait(know.at[0], 2)
    for dz in (4, -4):
        pl.semaphore_signal(know.at[1], inc=1, device_id=device(along(dz), j, x), device_id_type=MESH)
    for one in later:
        one.wait()

    for half in range(2):
        logit_tiles[:, half, :] = logits[:, half * 128 : half * 128 + 128]

    def depth_peer(step):
        return (depth + step) % NL

    def copy_l(step):
        to = depth_peer(step)
        return copy(
            logit_tiles.at[pl.ds(y_lo * HY + z * HZ, HZ)],
            logit_rows.at[depth],
            send_l.at[step],
            recv_l.at[depth],
            device(z, y_lo * NL + to, x),
        )

    for step in range(1, NL):
        copy_l(step).start()
    logit_rows[depth] = logit_tiles[pl.ds(y_lo * HY + z * HZ, HZ)]

    spread = (
        lax.broadcasted_iota(jnp.int32, (SL // ACT, SL), 0)
        == lax.broadcasted_iota(jnp.int32, (SL // ACT, SL), 1) // ACT
    ).astype(jnp.bfloat16)
    lane = lax.broadcasted_iota(jnp.int32, (NL, SL), 1) % ACT
    counts_wide = jnp.dot(
        counts[...].astype(jnp.float32).astype(jnp.bfloat16), spread, preferred_element_type=jnp.float32
    )
    parents_wide = jnp.dot(
        parents[...].astype(jnp.float32).astype(jnp.bfloat16), spread, preferred_element_type=jnp.float32
    )
    legal[...] = jnp.where(lane.astype(jnp.float32) < counts_wide, 1.0, 0.0)
    parents_wide = jnp.where(lane == 0, parents_wide, -1.0)
    seq = lax.broadcasted_iota(jnp.int32, (SL, SL), 0).astype(jnp.float32)
    for level in range(NL):
        owners[level] = jnp.where(seq == parents_wide[level : level + 1, :], 1.0, 0.0).astype(jnp.bfloat16)

    total = out1[x, y_lo].astype(jnp.int32)
    copy_y.wait_recv()
    total += in_y[...].astype(jnp.int32)
    for way in range(2):
        for from_y in range(2):
            for part in range(2):
                rows = in_x.at[way, from_y, half_rows(part)]
                sem = recv1.at[way, from_y, part]
                copy(rows, rows, send1.at[0, 0, 0], sem, device(z, j, hop_x(1))).wait_recv()
            total += in_x[way, from_y].astype(jnp.int32)
    total2[...] = total.astype(jnp.float32) * (SCALE_PLANE / SCALE)
    for to_z in range(NZ):
        rows = total2[to_z * HZ : (to_z + 1) * HZ, :]
        rows = jnp.round(jnp.concatenate([rows[:, :128], rows[:, 128:]], axis=0))
        out2[to_z] = rows.astype(jnp.int32).astype(jnp.int16)

    pl.semaphore_wait(know.at[1], 2)

    def copy2(i):
        dz = FAR_FIRST[i]
        return copy(
            out2.at[along(dz)], in2.at[i], send2.at[i], recv2.at[i], device(along(dz), j, x)
        )

    for i in range(NZ - 1):
        copy2(i).start()

    rows16[...] = jnp.zeros((PAD, SX), jnp.float32)
    logit16[...] = jnp.zeros((PAD, SX), jnp.float32)
    for step in range(1, NL):
        slot = depth_peer(step)
        copy(
            logit_rows.at[slot], logit_rows.at[slot], send_l.at[0], recv_l.at[slot], device(z, j, (x + 1) % NX)
        ).wait_recv()
    for group in range(8):
        logit16[0:HZ, group * 128 : (group + 1) * 128] = logit_rows[group // 2, :, group % 2, :]

    total = out2[z].astype(jnp.int32)
    for i in range(NZ - 2, -1, -1):
        copy2(i).wait_recv()
        total += in2[i].astype(jnp.int32)
    halves[0 : 2 * HZ, :] = total.astype(jnp.float32)
    halves[2 * HZ :, :] = jnp.zeros((8, 128), jnp.float32)
    counter = jnp.concatenate([halves[0:PAD, :], halves[HZ : HZ + PAD, :]], axis=1)
    high = counter.astype(jnp.bfloat16).astype(jnp.float32)
    both = jnp.concatenate([high, counter - high], axis=0).astype(jnp.bfloat16)
    partial_gradient = jnp.dot(both, pay[...], preferred_element_type=jnp.float32)
    partial_gradient = (partial_gradient[:PAD] + partial_gradient[PAD:]) * (1.0 / SCALE_PLANE)
    for group in range(8):
        out5[:, group, :] = partial_gradient[:HZ, group * 128 : (group + 1) * 128]

    def copy5(step):
        to = depth_peer(step)
        return copy(
            out5,
            in5.at[step],
            send5.at[step],
            recv5.at[step],
            device(z, y_lo * NL + to, x),
        )

    for step in (2, 1, 3):
        copy5(step).start()
    for step in range(1, NL):
        copy5(step).wait_recv()
    total = out5[...] + in5[1] + in5[2] + in5[3]
    in5[0] = total
    for group in range(8):
        rows16[0:HZ, group * 128 : (group + 1) * 128] = in5[0, :, group, :]
    gradient = rows16[...]

    incoming = jnp.zeros((PAD, SL), jnp.float32)
    for level in range(NL - 1, -1, -1):
        cols = slice(level * SL, (level + 1) * SL)
        shift = gradient[:, cols] + incoming
        out3[level, :, 0, :] = shift[:HZ, :128]
        out3[level, :, 1, :] = shift[:HZ, 128:]
        if level:
            value = group_value(logit16[:, cols] + shift, legal[level : level + 1, :])
            incoming = hand_down(value, owners[level])

    in3[0] = out3[depth]

    def copy3(source, dz):
        slot = PLACES.index(source)
        there = PLACES.index((source - dz + 7) % NZ - 7)
        return copy(in3.at[slot], in3.at[there], send3.at[there], recv3.at[there], device(along(dz), j, x))

    def wait3(source):
        slot = PLACES.index(source)
        copy(in3.at[slot], in3.at[slot], send3.at[slot], recv3.at[slot], device(along(1), j, x)).wait_recv()

    straight = [copy3(0, dz) for dz in (HUB, -HUB) + NEAR]
    onward = [copy3(-HUB, k - HUB) for k in UP]
    onward_down = [copy3(HUB, k + HUB) for k in DOWN]
    for one in straight:
        one.start()
    wait3(-HUB)
    for one in onward:
        one.start()
    wait3(HUB)
    for one in onward_down:
        one.start()

    def copy4(part):
        slots = pl.ds(PARTS[part][0], PARTS[part][1] - PARTS[part][0])
        return copy(
            in3.at[slots],
            in4.at[slots],
            send4.at[part],
            recv4.at[part],
            device(z, (1 - y_lo) * NL + depth, x),
        )

    def place(block, half, slot):
        shifts[pl.ds(half * HY + along(PLACES[slot]) * HZ, HZ)] = block[slot]

    for part, (begin, end) in enumerate(PARTS):
        for slot in range(begin, end):
            if PLACES[slot] not in (0, HUB, -HUB):
                wait3(PLACES[slot])
        copy4(part).start()
        for slot in range(begin, end):
            place(in3, y_lo, slot)
    def half_scores(half):
        rows = pl.ds(half * HY, HY)
        here = logits[pl.ds(pl.multiple_of(half * HY, HY), HY), :]
        return here + jnp.concatenate([shifts[rows, 0, :], shifts[rows, 1, :]], axis=1)

    can = legal[pl.ds(depth, 1), :]
    own_legal[...] = jnp.broadcast_to(can, (8, SL))
    own_owner[...] = owners[depth]
    here = half_scores(y_lo)
    value = group_value(here, can)
    own_policy[...] = jnp.where(can > 0.0, here - value, 0.0)
    own_passed[...] = hand_down(value, owners[depth])

    for part, (begin, end) in enumerate(PARTS):
        copy4(part).wait_recv()
        for slot in range(begin, end):
            place(in4, 1 - y_lo, slot)
    scores[...] = half_scores(1 - y_lo)

    for part in range(2):
        copy_r(part).wait_send()
        for other in range(2):
            copy1(1, other, part).wait_send()
            copy1(2, other, part).wait_send()
    copy_y.wait_send()
    for i in range(NZ - 1):
        copy2(i).wait_send()
    for step in range(1, NL):
        copy5(step).wait_send()
        copy_l(step).wait_send()
    for one in straight + onward + onward_down:
        one.wait_send()

    for part in range(len(PARTS)):
        copy4(part).wait_send()


def last_pass(scores, own_policy, own_passed, legal, owner, policy_hbm, passed_hbm, policy, passed, stores):
    y_lo = lax.axis_index("board") % 2

    def store(src, dst, half, first, count, sem):
        rows = pl.ds(pl.multiple_of(half * HY + first, 8), count)
        one = pltpu.make_async_copy(src.at[pl.ds(first, count)], dst.at[rows], sem)
        one.start()
        return one

    copies = [
        store(own_policy, policy_hbm, y_lo, 0, HY, stores.at[0, CHUNKS]),
        store(own_passed, passed_hbm, y_lo, 0, HY, stores.at[1, CHUNKS]),
    ]
    can = legal[0:1, :]
    count = HY // CHUNKS
    for i in range(CHUNKS):
        rows = pl.ds(i * count, count)
        value = group_value(scores[rows, :], can)
        policy[rows, :] = jnp.where(can > 0.0, scores[rows, :] - value, 0.0)
        copies.append(store(policy, policy_hbm, 1 - y_lo, i * count, count, stores.at[0, i]))
        passed[rows, :] = hand_down(value, owner[...])
        copies.append(store(passed, passed_hbm, 1 - y_lo, i * count, count, stores.at[1, i]))
    for one in copies:
        one.wait()


def local(reach, payoff, board_cards, hand_rank, logits, action_counts, parent_seq):
    table, onehot = hand_cards()
    vmem = pl.BlockSpec(memory_space=pltpu.VMEM)
    dma = pltpu.SemaphoreType.DMA
    f32, bf16, i16 = jnp.float32, jnp.bfloat16, jnp.int16
    rest = pl.pallas_call(
        kernel,
        name="prox",
        out_shape=(
            jax.ShapeDtypeStruct((HY, SL), f32),
            jax.ShapeDtypeStruct((HY, SL), f32),
            jax.ShapeDtypeStruct((HY, SL), f32),
            jax.ShapeDtypeStruct((8, SL), f32),
            jax.ShapeDtypeStruct((SL, SL), bf16),
        ),
        in_specs=[pl.BlockSpec(memory_space=pl.ANY)] * 9,
        out_specs=(vmem,) * 5,
        scratch_shapes=[
            pltpu.VMEM((NB * HX, SL), bf16),
            pltpu.VMEM((NB, 5), jnp.int32),
            pltpu.VMEM((NB, HANDS), jnp.int32),
            pltpu.VMEM((HX, SL), f32),
            pltpu.VMEM((NL, SL // ACT), jnp.int32),
            pltpu.VMEM((NL, SL // ACT), jnp.int32),
            pltpu.VMEM((8, HP), f32),
            pltpu.VMEM((HP, 128), bf16),
            dma((NB + 8,)),
            pltpu.VMEM((NB, HP), f32),
            pltpu.VMEM((HP, NB), f32),
            pltpu.VMEM((NX, 2, HY, SL), i16),
            pltpu.VMEM((2, 2, HH, SL), i16),
            pltpu.VMEM((2, 2, HY, SL), i16),
            pltpu.VMEM((HY, SL), i16),
            pltpu.VMEM((NZ, 2 * HZ, 128), i16),
            pltpu.VMEM((NZ - 1, 2 * HZ, 128), i16),
            pltpu.VMEM((PAD, SX), f32),
            pltpu.VMEM((PAD, SX), f32),
            pltpu.VMEM((SL, SX), bf16),
            pltpu.VMEM((HX, 2, 128), f32),
            pltpu.VMEM((NL, HZ, 2, 128), f32),
            pltpu.VMEM((HY, SL), f32),
            pltpu.VMEM((2 * HZ + 8, 128), f32),
            pltpu.VMEM((HZ, 8, 128), f32),
            pltpu.VMEM((NL, HZ, 8, 128), f32),
            pltpu.VMEM((NL, HZ, 2, 128), f32),
            pltpu.VMEM((NZ, HZ, 2, 128), f32),
            pltpu.VMEM((NZ, HZ, 2, 128), f32),
            pltpu.VMEM((HX, 2, 128), f32),
            pltpu.VMEM((NL, SL), f32),
            pltpu.VMEM((NL, SL, SL), bf16),
            dma((2, 2, 2)),
            dma((2, 2, 2)),
            dma((3,)),
            dma((3,)),
            dma((NZ - 1,)),
            dma((NZ - 1,)),
            dma((NZ,)),
            dma((NZ,)),
            dma((len(PARTS),)),
            dma((len(PARTS),)),
            dma((NL,)),
            dma((NL,)),
            dma((NL,)),
            dma((NL,)),
            pltpu.SemaphoreType.REGULAR((2,)),
        ],
        compiler_params=pltpu.CompilerParams(
            collective_id=0, has_side_effects=True, vmem_limit_bytes=32 * 1024 * 1024
        ),
    )(
        *[
            pltpu.with_memory_space_constraint(operand, pltpu.HBM)
            for operand in (
                reach.reshape(NB * HX, SL),
                payoff,
                board_cards,
                hand_rank,
                logits,
                action_counts,
                parent_seq,
                jnp.asarray(table),
                jnp.asarray(onehot, jnp.bfloat16),
            )
        ]
    )
    hbm = pl.BlockSpec(memory_space=pl.ANY)
    return pl.pallas_call(
        last_pass,
        name="last_pass",
        out_shape=(jax.ShapeDtypeStruct((HX, SL), f32), jax.ShapeDtypeStruct((HX, SL), f32)),
        in_specs=[vmem] * 5,
        out_specs=(hbm, hbm),
        scratch_shapes=[pltpu.VMEM((HY, SL), f32), pltpu.VMEM((HY, SL), f32), dma((2, CHUNKS + 1))],
        compiler_params=pltpu.CompilerParams(vmem_limit_bytes=32 * 1024 * 1024),
    )(*rest)


def solution(mesh):
    return jax.shard_map(
        local,
        mesh=mesh,
        in_specs=(
            P("board", "hand", "depth"),
            P("depth", None),
            P("board", None),
            P("board", None),
            P("hand", "depth"),
            P(),
            P(),
        ),
        out_specs=(P("hand", "depth"), P("hand", "depth")),
        check_vma=False,
    )
```

```python
import jax
import jax.numpy as jnp
import numpy as np
from jax import lax
from jax.experimental import pallas as pl
from jax.experimental.pallas import tpu as pltpu
from jax.sharding import PartitionSpec as P

CARDS = 52
HANDS = 1326
ACT = 4
NZ = 16
NX = 4
NL = 4
HX = 384
HP = NX * HX
HY = HX // 2
HH = HY // 2
HZ = HY // NZ
PAD = 16
SL = 256
SX = NL * SL
NB = 8
BOUND = float(2 * NB * HX)
SCALE = 32700.0 / BOUND
LIVE = 45 * 44 // 2
BOUND_PLANE = float(2 * NB * LIVE)
SCALE_PLANE = 32700.0 / BOUND_PLANE
MESH = pl.DeviceIdType.MESH
NEAR = (1, -1, 2, -2)
UP = (3, 4, 6, 7, 8)
DOWN = (-3, -4, -6, -7)
HUB = 5
FAR_FIRST = (8, 7, -7, 6, -6, 5, -5, 4, -4, 3, -3, 2, -2, 1, -1)
GREET = (1, -1, 2, -2)
PLACES = (0, 1, -1, 2, -2, 5, -5, -3, -4, -6, -7, 3, 4, 6, 7, 8)
PARTS = ((0, 7), (7, 11), (11, 16))
ROW_PEERS = 5
CHUNKS = 2
NAN = float("nan")


def hand_cards():
    first, second = np.triu_indices(CARDS, 1)
    table = np.full((8, HP), -1.0, np.float32)
    table[0, :HANDS] = first
    table[1, :HANDS] = second
    onehot = np.zeros((HP, 128), np.float32)
    onehot[np.arange(HANDS), first] = 1.0
    onehot[np.arange(HANDS), second] = 1.0
    return table, onehot


def dot_t(a, b):
    return lax.dot_general(a, b, (((1,), (1,)), ((), ())), preferred_element_type=jnp.float32)


def group_reduce(x, op):
    lane = lax.broadcasted_iota(jnp.int32, x.shape, 1)
    near = jnp.where(lane % 2 == 0, pltpu.roll(x, 127, 1), pltpu.roll(x, 1, 1))
    x = op(x, near)
    far = jnp.where(lane % 4 < 2, pltpu.roll(x, 126, 1), pltpu.roll(x, 2, 1))
    return op(x, far)


def group_value(scores, legal):
    parts = []
    for half in range(2):
        cols = slice(half * 128, half * 128 + 128)
        masked = jnp.where(legal[:, cols] > 0.0, scores[:, cols], -jnp.inf)
        top = group_reduce(masked, jnp.maximum)
        total = group_reduce(jnp.exp(masked - top), jnp.add)
        parts.append(top + jnp.log(total))
    return jnp.concatenate(parts, axis=1)


def first_value(scores, legal):
    parts = []
    for half in range(2):
        cols = slice(half * 128, half * 128 + 128)
        slots = [jnp.where(legal[:, cols] > 0.0, scores[:, cols], -jnp.inf)]
        slots += [pltpu.roll(slots[0], 128 - step, 1) for step in range(1, ACT)]
        top = jnp.maximum(jnp.maximum(slots[0], slots[1]), jnp.maximum(slots[2], slots[3]))
        terms = [jnp.exp(slot - top) for slot in slots]
        parts.append(top + jnp.log((terms[0] + terms[1]) + (terms[2] + terms[3])))
    return jnp.concatenate(parts, axis=1)


def hand_down(value, owner_t):
    a = value.astype(jnp.bfloat16)
    rest = value - a.astype(jnp.float32)
    b = rest.astype(jnp.bfloat16)
    c = (rest - b.astype(jnp.float32)).astype(jnp.bfloat16)
    return dot_t(a, owner_t) + dot_t(b, owner_t) + dot_t(c, owner_t)


def kernel(
    reach_hbm,
    payoff,
    cards_hbm,
    rank_hbm,
    logits_hbm,
    counts_hbm,
    parents_hbm,
    table_hbm,
    onehot_hbm,
    scores,
    own_policy,
    own_passed,
    own_legal,
    own_owner,
    reach,
    cards,
    rank,
    logits,
    counts,
    parents,
    table,
    onehot,
    load,
    ranks,
    ranks_t,
    out1,
    relay,
    in_x,
    in_y,
    out2,
    in2,
    rows16,
    logit16,
    pay,
    logit_tiles,
    logit_rows,
    total2,
    halves,
    out5,
    in5,
    out3,
    in3,
    in4,
    shifts,
    legal,
    owners,
    send1,
    recv1,
    send_r,
    recv_r,
    send2,
    recv2,
    send3,
    recv3,
    send4,
    recv4,
    send5,
    recv5,
    send_l,
    recv_l,
    know,
):
    board = lax.axis_index("board")
    depth = lax.axis_index("depth")
    x = lax.axis_index("hand")
    z = board // 2
    y_lo = board % 2
    j = y_lo * NL + depth

    def device(to_z, to_j, to_x):
        return (to_z * 2 + to_j // NL, to_j % NL, to_x)

    def along(dz):
        return (z + dz + NZ) % NZ

    def copy(src, dst, send, recv, to):
        return pltpu.make_async_remote_copy(
            src_ref=src, dst_ref=dst, send_sem=send, recv_sem=recv, device_id=to, device_id_type=MESH
        )

    def loaded(i, src, dst):
        return pltpu.make_async_copy(src, dst, load.at[i])

    loads = [
        loaded(0, rank_hbm, rank),
        loaded(1, cards_hbm, cards),
        loaded(2, table_hbm, table),
        loaded(3, onehot_hbm, onehot),
    ]
    for b in range(NB):
        rows = pl.ds(b * HX, HX)
        loads.append(loaded(4 + b, reach_hbm.at[rows], reach.at[rows]))
    later = [
        loaded(4 + NB, logits_hbm, logits),
        loaded(5 + NB, counts_hbm, counts),
        loaded(6 + NB, parents_hbm, parents),
        loaded(7 + NB, payoff, pay),
    ]
    for one in loads:
        one.start()

    def hop_x(i):
        return (x + 2 + i + i * (i - 1) // 2) % NX

    barrier = pltpu.get_barrier_semaphore()
    for i in (1, 2):
        for other in range(2):
            to_j = (y_lo + other) % 2 * NL + depth
            pl.semaphore_signal(barrier, inc=1, device_id=device(z, to_j, hop_x(i)), device_id_type=MESH)
    to_j = (1 - y_lo) * NL + depth
    pl.semaphore_signal(barrier, inc=1, device_id=device(z, to_j, x), device_id_type=MESH)
    for step in range(1, NL):
        to_j = y_lo * NL + (depth + step) % NL
        pl.semaphore_signal(barrier, inc=1, device_id=device(z, to_j, x), device_id_type=MESH)
    for dz in GREET:
        pl.semaphore_signal(barrier, inc=1, device_id=device(along(dz), j, x), device_id_type=MESH)

    for one in loads[:3]:
        one.wait()

    ranks[...] = jnp.full((NB, HP), NAN, jnp.float32)
    ranks[:, :HANDS] = rank[...].astype(jnp.float32)
    first = table[0:1, :]
    second = table[1:2, :]
    hit = first < 0.0
    for card in range(5):
        one = cards[:, card : card + 1].astype(jnp.float32)
        hit = hit | (first == one) | (second == one)
    left = ranks[...]
    exponent = jnp.floor(left * (1.0 / 128.0))
    ordered = (1.0 + (left - exponent * 128.0) * (1.0 / 128.0)) * 2.0**-29
    for bit in range(6):
        rest = jnp.floor(exponent * 0.5)
        ordered = jnp.where(exponent - 2.0 * rest > 0.5, ordered * 2.0 ** (1 << bit), ordered)
        exponent = rest
    ranks[...] = jnp.where(hit, NAN, ordered)
    ranks_t[...] = ranks[...].T

    own = pl.ds(pl.multiple_of(x * HX, HX), HX)

    for one in loads[3:]:
        one.wait()
    for one in later:
        one.start()

    def partial(to_x):
        rows = pl.ds(pl.multiple_of(to_x * HX, HX), HX)
        shared = dot_t(onehot[rows, :], onehot[own, :])
        apart = jnp.where(shared > 0.0, 0.0, 1.0).astype(jnp.bfloat16)
        minus = -apart
        zero = jnp.zeros((HX, HX), jnp.bfloat16)
        total = jnp.zeros((HX, SL), jnp.float32)
        for pair in range(NB // 2):
            sides = []
            for b in (2 * pair, 2 * pair + 1):
                mine = jnp.broadcast_to(ranks_t[rows, b : b + 1].astype(jnp.bfloat16), (HX, HX))
                theirs = jnp.broadcast_to(ranks[b : b + 1, own].astype(jnp.bfloat16), (HX, HX))
                sides.append(jnp.where(theirs < mine, apart, jnp.where(theirs > mine, minus, zero)))
            total += jnp.dot(
                jnp.concatenate(sides, axis=1),
                reach[2 * HX * pair : 2 * HX * (pair + 1), :],
                preferred_element_type=jnp.float32,
            )
        return jnp.round(total * SCALE).astype(jnp.int32).astype(jnp.int16)

    def half_rows(part):
        return pl.ds(part * HH, HH)

    def copy_r(part):
        return copy(
            out1.at[hop_x(0), pl.ds(0, 2), half_rows(part)],
            relay.at[part],
            send_r.at[part],
            recv_r.at[part],
            device(z, j, hop_x(2 - part)),
        )

    def copy1(i, other, part):
        to_x, to_y, way = hop_x(i), (y_lo + other) % 2, 2 - i
        return copy(
            out1.at[to_x, to_y, half_rows(part)],
            in_x.at[way, y_lo, half_rows(part)],
            send1.at[way, other, part],
            recv1.at[way, y_lo, part],
            device(z, to_y * NL + depth, to_x),
        )

    copy_y = copy(
        out1.at[x, 1 - y_lo], in_y, send_r.at[2], recv_r.at[2], device(z, (1 - y_lo) * NL + depth, x)
    )

    @pl.loop(0, NX)
    def _(i):
        to_x = hop_x(i)
        out1[to_x] = partial(to_x).reshape(2, HY, SL)

        @pl.when(i == 0)
        def _():
            pl.semaphore_wait(barrier, ROW_PEERS + NL - 1 + len(GREET))
            for dz in (2, -2):
                pl.semaphore_signal(
                    know.at[0], inc=1, device_id=device(along(dz), j, x), device_id_type=MESH
                )
            copy_r(0).start()
            copy_r(1).start()

        @pl.when(i == 1)
        def _():
            copy1(1, 1, 0).start()
            copy1(1, 0, 0).start()

        @pl.when(i == 2)
        def _():
            copy1(2, 1, 1).start()
            copy1(2, 0, 1).start()

    copy_y.start()
    for i, part in ((1, 1), (2, 0)):
        copy_r(part).wait_recv()
        to_x = hop_x(i)
        both_rows = slice(part * HH, part * HH + HH)
        here = out1[to_x, :, both_rows, :].astype(jnp.int32)
        out1[to_x, :, both_rows, :] = (here + relay[part].astype(jnp.int32)).astype(jnp.int16)
        copy1(i, 1, part).start()
        copy1(i, 0, part).start()

    pl.semaphore_wait(know.at[0], 2)
    for dz in (4, -4):
        pl.semaphore_signal(know.at[1], inc=1, device_id=device(along(dz), j, x), device_id_type=MESH)
    for one in later:
        one.wait()

    for half in range(2):
        logit_tiles[:, half, :] = logits[:, half * 128 : half * 128 + 128]

    def depth_peer(step):
        return (depth + step) % NL

    def copy_l(step):
        to = depth_peer(step)
        return copy(
            logit_tiles.at[pl.ds(y_lo * HY + z * HZ, HZ)],
            logit_rows.at[depth],
            send_l.at[step],
            recv_l.at[depth],
            device(z, y_lo * NL + to, x),
        )

    for step in range(1, NL):
        copy_l(step).start()
    logit_rows[depth] = logit_tiles[pl.ds(y_lo * HY + z * HZ, HZ)]

    spread = (
        lax.broadcasted_iota(jnp.int32, (SL // ACT, SL), 0)
        == lax.broadcasted_iota(jnp.int32, (SL // ACT, SL), 1) // ACT
    ).astype(jnp.bfloat16)
    lane = lax.broadcasted_iota(jnp.int32, (NL, SL), 1) % ACT
    counts_wide = jnp.dot(
        counts[...].astype(jnp.float32).astype(jnp.bfloat16), spread, preferred_element_type=jnp.float32
    )
    parents_wide = jnp.dot(
        parents[...].astype(jnp.float32).astype(jnp.bfloat16), spread, preferred_element_type=jnp.float32
    )
    legal[...] = jnp.where(lane.astype(jnp.float32) < counts_wide, 1.0, 0.0)
    parents_wide = jnp.where(lane == 0, parents_wide, -1.0)
    seq = lax.broadcasted_iota(jnp.int32, (SL, SL), 0).astype(jnp.float32)
    for level in range(NL):
        owners[level] = jnp.where(seq == parents_wide[level : level + 1, :], 1.0, 0.0).astype(jnp.bfloat16)

    total = out1[x, y_lo].astype(jnp.int32)
    copy_y.wait_recv()
    total += in_y[...].astype(jnp.int32)
    for way in range(2):
        for from_y in range(2):
            for part in range(2):
                rows = in_x.at[way, from_y, half_rows(part)]
                sem = recv1.at[way, from_y, part]
                copy(rows, rows, send1.at[0, 0, 0], sem, device(z, j, hop_x(1))).wait_recv()
            total += in_x[way, from_y].astype(jnp.int32)
    total2[...] = total.astype(jnp.float32) * (SCALE_PLANE / SCALE)
    for to_z in range(NZ):
        rows = total2[to_z * HZ : (to_z + 1) * HZ, :]
        rows = jnp.round(jnp.concatenate([rows[:, :128], rows[:, 128:]], axis=0))
        out2[to_z] = rows.astype(jnp.int32).astype(jnp.int16)

    pl.semaphore_wait(know.at[1], 2)

    def copy2(i):
        dz = FAR_FIRST[i]
        return copy(
            out2.at[along(dz)], in2.at[i], send2.at[i], recv2.at[i], device(along(dz), j, x)
        )

    for i in range(NZ - 1):
        copy2(i).start()

    rows16[...] = jnp.zeros((PAD, SX), jnp.float32)
    logit16[...] = jnp.zeros((PAD, SX), jnp.float32)
    for step in range(1, NL):
        slot = depth_peer(step)
        copy(
            logit_rows.at[slot], logit_rows.at[slot], send_l.at[0], recv_l.at[slot], device(z, j, (x + 1) % NX)
        ).wait_recv()
    for group in range(8):
        logit16[0:HZ, group * 128 : (group + 1) * 128] = logit_rows[group // 2, :, group % 2, :]

    total = out2[z].astype(jnp.int32)
    for i in range(NZ - 2, -1, -1):
        copy2(i).wait_recv()
        total += in2[i].astype(jnp.int32)
    halves[0 : 2 * HZ, :] = total.astype(jnp.float32)
    halves[2 * HZ :, :] = jnp.zeros((8, 128), jnp.float32)
    counter = jnp.concatenate([halves[0:PAD, :], halves[HZ : HZ + PAD, :]], axis=1)
    high = counter.astype(jnp.bfloat16).astype(jnp.float32)
    both = jnp.concatenate([high, counter - high], axis=0).astype(jnp.bfloat16)
    partial_gradient = jnp.dot(both, pay[...], preferred_element_type=jnp.float32)
    partial_gradient = (partial_gradient[:PAD] + partial_gradient[PAD:]) * (1.0 / SCALE_PLANE)
    for group in range(8):
        out5[:, group, :] = partial_gradient[:HZ, group * 128 : (group + 1) * 128]

    def copy5(step):
        to = depth_peer(step)
        return copy(
            out5,
            in5.at[step],
            send5.at[step],
            recv5.at[step],
            device(z, y_lo * NL + to, x),
        )

    for step in (2, 1, 3):
        copy5(step).start()
    for step in range(1, NL):
        copy5(step).wait_recv()
    total = out5[...] + in5[1] + in5[2] + in5[3]
    in5[0] = total
    for group in range(8):
        rows16[0:HZ, group * 128 : (group + 1) * 128] = in5[0, :, group, :]
    gradient = rows16[...]

    incoming = jnp.zeros((PAD, SL), jnp.float32)
    for level in range(NL - 1, -1, -1):
        cols = slice(level * SL, (level + 1) * SL)
        shift = gradient[:, cols] + incoming
        out3[level, :, 0, :] = shift[:HZ, :128]
        out3[level, :, 1, :] = shift[:HZ, 128:]
        if level:
            value = first_value(logit16[:, cols] + shift, legal[level : level + 1, :])
            incoming = hand_down(value, owners[level])

    in3[0] = out3[depth]

    def copy3(source, dz):
        slot = PLACES.index(source)
        there = PLACES.index((source - dz + 7) % NZ - 7)
        return copy(in3.at[slot], in3.at[there], send3.at[there], recv3.at[there], device(along(dz), j, x))

    def wait3(source):
        slot = PLACES.index(source)
        copy(in3.at[slot], in3.at[slot], send3.at[slot], recv3.at[slot], device(along(1), j, x)).wait_recv()

    straight = [copy3(0, dz) for dz in (HUB, -HUB) + NEAR]
    onward = [copy3(-HUB, k - HUB) for k in UP]
    onward_down = [copy3(HUB, k + HUB) for k in DOWN]
    for one in straight:
        one.start()
    wait3(-HUB)
    for one in onward:
        one.start()
    wait3(HUB)
    for one in onward_down:
        one.start()

    def copy4(part):
        slots = pl.ds(PARTS[part][0], PARTS[part][1] - PARTS[part][0])
        return copy(
            in3.at[slots],
            in4.at[slots],
            send4.at[part],
            recv4.at[part],
            device(z, (1 - y_lo) * NL + depth, x),
        )

    def place(block, half, slot):
        shifts[pl.ds(half * HY + along(PLACES[slot]) * HZ, HZ)] = block[slot]

    for part, (begin, end) in enumerate(PARTS):
        for slot in range(begin, end):
            if PLACES[slot] not in (0, HUB, -HUB):
                wait3(PLACES[slot])
        copy4(part).start()
        for slot in range(begin, end):
            place(in3, y_lo, slot)
    def half_scores(half):
        rows = pl.ds(half * HY, HY)
        here = logits[pl.ds(pl.multiple_of(half * HY, HY), HY), :]
        return here + jnp.concatenate([shifts[rows, 0, :], shifts[rows, 1, :]], axis=1)

    can = legal[pl.ds(depth, 1), :]
    own_legal[...] = jnp.broadcast_to(can, (8, SL))
    own_owner[...] = owners[depth]
    here = half_scores(y_lo)
    value = group_value(here, can)
    own_policy[...] = jnp.where(can > 0.0, here - value, 0.0)
    own_passed[...] = hand_down(value, owners[depth])

    for part, (begin, end) in enumerate(PARTS):
        copy4(part).wait_recv()
        for slot in range(begin, end):
            place(in4, 1 - y_lo, slot)
    scores[...] = half_scores(1 - y_lo)

    for part in range(2):
        copy_r(part).wait_send()
        for other in range(2):
            copy1(1, other, part).wait_send()
            copy1(2, other, part).wait_send()
    copy_y.wait_send()
    for i in range(NZ - 1):
        copy2(i).wait_send()
    for step in range(1, NL):
        copy5(step).wait_send()
        copy_l(step).wait_send()
    for one in straight + onward + onward_down:
        one.wait_send()

    for part in range(len(PARTS)):
        copy4(part).wait_send()


def last_pass(scores, own_policy, own_passed, legal, owner, policy_hbm, passed_hbm, policy, passed, stores):
    y_lo = lax.axis_index("board") % 2

    def store(src, dst, half, first, count, sem):
        rows = pl.ds(pl.multiple_of(half * HY + first, 8), count)
        one = pltpu.make_async_copy(src.at[pl.ds(first, count)], dst.at[rows], sem)
        one.start()
        return one

    copies = [
        store(own_policy, policy_hbm, y_lo, 0, HY, stores.at[0, CHUNKS]),
        store(own_passed, passed_hbm, y_lo, 0, HY, stores.at[1, CHUNKS]),
    ]
    can = legal[0:1, :]
    count = HY // CHUNKS
    for i in range(CHUNKS):
        rows = pl.ds(i * count, count)
        value = group_value(scores[rows, :], can)
        policy[rows, :] = jnp.where(can > 0.0, scores[rows, :] - value, 0.0)
        copies.append(store(policy, policy_hbm, 1 - y_lo, i * count, count, stores.at[0, i]))
        passed[rows, :] = hand_down(value, owner[...])
        copies.append(store(passed, passed_hbm, 1 - y_lo, i * count, count, stores.at[1, i]))
    for one in copies:
        one.wait()


def local(reach, payoff, board_cards, hand_rank, logits, action_counts, parent_seq):
    table, onehot = hand_cards()
    vmem = pl.BlockSpec(memory_space=pltpu.VMEM)
    dma = pltpu.SemaphoreType.DMA
    f32, bf16, i16 = jnp.float32, jnp.bfloat16, jnp.int16
    rest = pl.pallas_call(
        kernel,
        name="prox",
        out_shape=(
            jax.ShapeDtypeStruct((HY, SL), f32),
            jax.ShapeDtypeStruct((HY, SL), f32),
            jax.ShapeDtypeStruct((HY, SL), f32),
            jax.ShapeDtypeStruct((8, SL), f32),
            jax.ShapeDtypeStruct((SL, SL), bf16),
        ),
        in_specs=[pl.BlockSpec(memory_space=pl.ANY)] * 9,
        out_specs=(vmem,) * 5,
        scratch_shapes=[
            pltpu.VMEM((NB * HX, SL), bf16),
            pltpu.VMEM((NB, 5), jnp.int32),
            pltpu.VMEM((NB, HANDS), jnp.int32),
            pltpu.VMEM((HX, SL), f32),
            pltpu.VMEM((NL, SL // ACT), jnp.int32),
            pltpu.VMEM((NL, SL // ACT), jnp.int32),
            pltpu.VMEM((8, HP), f32),
            pltpu.VMEM((HP, 128), bf16),
            dma((NB + 8,)),
            pltpu.VMEM((NB, HP), f32),
            pltpu.VMEM((HP, NB), f32),
            pltpu.VMEM((NX, 2, HY, SL), i16),
            pltpu.VMEM((2, 2, HH, SL), i16),
            pltpu.VMEM((2, 2, HY, SL), i16),
            pltpu.VMEM((HY, SL), i16),
            pltpu.VMEM((NZ, 2 * HZ, 128), i16),
            pltpu.VMEM((NZ - 1, 2 * HZ, 128), i16),
            pltpu.VMEM((PAD, SX), f32),
            pltpu.VMEM((PAD, SX), f32),
            pltpu.VMEM((SL, SX), bf16),
            pltpu.VMEM((HX, 2, 128), f32),
            pltpu.VMEM((NL, HZ, 2, 128), f32),
            pltpu.VMEM((HY, SL), f32),
            pltpu.VMEM((2 * HZ + 8, 128), f32),
            pltpu.VMEM((HZ, 8, 128), f32),
            pltpu.VMEM((NL, HZ, 8, 128), f32),
            pltpu.VMEM((NL, HZ, 2, 128), f32),
            pltpu.VMEM((NZ, HZ, 2, 128), f32),
            pltpu.VMEM((NZ, HZ, 2, 128), f32),
            pltpu.VMEM((HX, 2, 128), f32),
            pltpu.VMEM((NL, SL), f32),
            pltpu.VMEM((NL, SL, SL), bf16),
            dma((2, 2, 2)),
            dma((2, 2, 2)),
            dma((3,)),
            dma((3,)),
            dma((NZ - 1,)),
            dma((NZ - 1,)),
            dma((NZ,)),
            dma((NZ,)),
            dma((len(PARTS),)),
            dma((len(PARTS),)),
            dma((NL,)),
            dma((NL,)),
            dma((NL,)),
            dma((NL,)),
            pltpu.SemaphoreType.REGULAR((2,)),
        ],
        compiler_params=pltpu.CompilerParams(
            collective_id=0, has_side_effects=True, vmem_limit_bytes=32 * 1024 * 1024
        ),
    )(
        *[
            pltpu.with_memory_space_constraint(operand, pltpu.HBM)
            for operand in (
                reach.reshape(NB * HX, SL),
                payoff,
                board_cards,
                hand_rank,
                logits,
                action_counts,
                parent_seq,
                jnp.asarray(table),
                jnp.asarray(onehot, jnp.bfloat16),
            )
        ]
    )
    hbm = pl.BlockSpec(memory_space=pl.ANY)
    return pl.pallas_call(
        last_pass,
        name="last_pass",
        out_shape=(jax.ShapeDtypeStruct((HX, SL), f32), jax.ShapeDtypeStruct((HX, SL), f32)),
        in_specs=[vmem] * 5,
        out_specs=(hbm, hbm),
        scratch_shapes=[pltpu.VMEM((HY, SL), f32), pltpu.VMEM((HY, SL), f32), dma((2, CHUNKS + 1))],
        compiler_params=pltpu.CompilerParams(vmem_limit_bytes=32 * 1024 * 1024),
    )(*rest)


def solution(mesh):
    return jax.shard_map(
        local,
        mesh=mesh,
        in_specs=(
            P("board", "hand", "depth"),
            P("depth", None),
            P("board", None),
            P("board", None),
            P("hand", "depth"),
            P(),
            P(),
        ),
        out_specs=(P("hand", "depth"), P("hand", "depth")),
        check_vma=False,
    )
```

```python
import jax
import jax.numpy as jnp
import numpy as np
from jax import lax
from jax.experimental import pallas as pl
from jax.experimental.pallas import tpu as pltpu
from jax.sharding import PartitionSpec as P

CARDS = 52
HANDS = 1326
ACT = 4
NZ = 16
NX = 4
NL = 4
HX = 384
HP = NX * HX
HY = HX // 2
HH = HY // 2
HZ = HY // NZ
PAD = 16
SL = 256
SX = NL * SL
NB = 8
BOUND = float(2 * NB * HX)
SCALE = 32700.0 / BOUND
LIVE = 45 * 44 // 2
BOUND_PLANE = float(2 * NB * LIVE)
SCALE_PLANE = 32700.0 / BOUND_PLANE
MESH = pl.DeviceIdType.MESH
NEAR = (1, -1, 2, -2)
UP = (3, 4, 6, 7, 8)
DOWN = (-3, -4, -6, -7)
HUB = 5
FAR_FIRST = (8, 7, -7, 6, -6, 5, -5, 4, -4, 3, -3, 2, -2, 1, -1)
GREET = (1, -1, 2, -2)
PLACES = (0, 1, -1, 2, -2, 5, -5, -3, -4, -6, -7, 3, 4, 6, 7, 8)
PARTS = ((0, 7), (7, 11), (11, 16))
ROW_PEERS = 5
CHUNKS = 2
NAN = float("nan")


def hand_cards():
    first, second = np.triu_indices(CARDS, 1)
    table = np.full((8, HP), -1.0, np.float32)
    table[0, :HANDS] = first
    table[1, :HANDS] = second
    onehot = np.zeros((HP, 128), np.float32)
    onehot[np.arange(HANDS), first] = 1.0
    onehot[np.arange(HANDS), second] = 1.0
    return table, onehot


def dot_t(a, b):
    return lax.dot_general(a, b, (((1,), (1,)), ((), ())), preferred_element_type=jnp.float32)


def group_reduce(x, op):
    lane = lax.broadcasted_iota(jnp.int32, x.shape, 1)
    near = jnp.where(lane % 2 == 0, pltpu.roll(x, 127, 1), pltpu.roll(x, 1, 1))
    x = op(x, near)
    far = jnp.where(lane % 4 < 2, pltpu.roll(x, 126, 1), pltpu.roll(x, 2, 1))
    return op(x, far)


def group_value(scores, legal):
    parts = []
    for half in range(2):
        cols = slice(half * 128, half * 128 + 128)
        masked = jnp.where(legal[:, cols] > 0.0, scores[:, cols], -jnp.inf)
        top = group_reduce(masked, jnp.maximum)
        total = group_reduce(jnp.exp(masked - top), jnp.add)
        parts.append(top + jnp.log(total))
    return jnp.concatenate(parts, axis=1)


def first_value(scores, legal):
    parts = []
    for half in range(2):
        cols = slice(half * 128, half * 128 + 128)
        slots = [jnp.where(legal[:, cols] > 0.0, scores[:, cols], -jnp.inf)]
        slots += [pltpu.roll(slots[0], 128 - step, 1) for step in range(1, ACT)]
        top = jnp.maximum(jnp.maximum(slots[0], slots[1]), jnp.maximum(slots[2], slots[3]))
        terms = [jnp.exp(slot - top) for slot in slots]
        parts.append(top + jnp.log((terms[0] + terms[1]) + (terms[2] + terms[3])))
    return jnp.concatenate(parts, axis=1)


def hand_down(value, owner_t):
    a = value.astype(jnp.bfloat16)
    rest = value - a.astype(jnp.float32)
    b = rest.astype(jnp.bfloat16)
    c = (rest - b.astype(jnp.float32)).astype(jnp.bfloat16)
    if value.shape[0] > 2 * PAD:
        return dot_t(a, owner_t) + dot_t(b, owner_t) + dot_t(c, owner_t)
    all_parts = dot_t(jnp.concatenate([a, b, c], axis=0), owner_t)
    return all_parts[:PAD] + all_parts[PAD : 2 * PAD] + all_parts[2 * PAD :]


def kernel(
    reach_hbm,
    payoff,
    cards_hbm,
    rank_hbm,
    logits_hbm,
    counts_hbm,
    parents_hbm,
    table_hbm,
    onehot_hbm,
    scores,
    own_policy,
    own_passed,
    own_legal,
    own_owner,
    reach,
    cards,
    rank,
    logits,
    counts,
    parents,
    table,
    onehot,
    load,
    ranks,
    ranks_t,
    out1,
    relay,
    in_x,
    in_y,
    out2,
    in2,
    rows16,
    logit16,
    pay,
    logit_tiles,
    logit_rows,
    total2,
    halves,
    out5,
    in5,
    out3,
    in3,
    in4,
    shifts,
    legal,
    owners,
    send1,
    recv1,
    send_r,
    recv_r,
    send2,
    recv2,
    send3,
    recv3,
    send4,
    recv4,
    send5,
    recv5,
    send_l,
    recv_l,
    know,
):
    board = lax.axis_index("board")
    depth = lax.axis_index("depth")
    x = lax.axis_index("hand")
    z = board // 2
    y_lo = board % 2
    j = y_lo * NL + depth

    def device(to_z, to_j, to_x):
        return (to_z * 2 + to_j // NL, to_j % NL, to_x)

    def along(dz):
        return (z + dz + NZ) % NZ

    def copy(src, dst, send, recv, to):
        return pltpu.make_async_remote_copy(
            src_ref=src, dst_ref=dst, send_sem=send, recv_sem=recv, device_id=to, device_id_type=MESH
        )

    def loaded(i, src, dst):
        return pltpu.make_async_copy(src, dst, load.at[i])

    loads = [
        loaded(0, rank_hbm, rank),
        loaded(1, cards_hbm, cards),
        loaded(2, table_hbm, table),
        loaded(3, onehot_hbm, onehot),
    ]
    for b in range(NB):
        rows = pl.ds(b * HX, HX)
        loads.append(loaded(4 + b, reach_hbm.at[rows], reach.at[rows]))
    later = [
        loaded(4 + NB, logits_hbm, logits),
        loaded(5 + NB, counts_hbm, counts),
        loaded(6 + NB, parents_hbm, parents),
        loaded(7 + NB, payoff, pay),
    ]
    for one in loads:
        one.start()

    def hop_x(i):
        return (x + 2 + i + i * (i - 1) // 2) % NX

    barrier = pltpu.get_barrier_semaphore()
    for i in (1, 2):
        for other in range(2):
            to_j = (y_lo + other) % 2 * NL + depth
            pl.semaphore_signal(barrier, inc=1, device_id=device(z, to_j, hop_x(i)), device_id_type=MESH)
    to_j = (1 - y_lo) * NL + depth
    pl.semaphore_signal(barrier, inc=1, device_id=device(z, to_j, x), device_id_type=MESH)
    for step in range(1, NL):
        to_j = y_lo * NL + (depth + step) % NL
        pl.semaphore_signal(barrier, inc=1, device_id=device(z, to_j, x), device_id_type=MESH)
    for dz in GREET:
        pl.semaphore_signal(barrier, inc=1, device_id=device(along(dz), j, x), device_id_type=MESH)

    for one in loads[:3]:
        one.wait()

    ranks[...] = jnp.full((NB, HP), NAN, jnp.float32)
    ranks[:, :HANDS] = rank[...].astype(jnp.float32)
    first = table[0:1, :]
    second = table[1:2, :]
    hit = first < 0.0
    for card in range(5):
        one = cards[:, card : card + 1].astype(jnp.float32)
        hit = hit | (first == one) | (second == one)
    left = ranks[...]
    exponent = jnp.floor(left * (1.0 / 128.0))
    ordered = (1.0 + (left - exponent * 128.0) * (1.0 / 128.0)) * 2.0**-29
    for bit in range(6):
        rest = jnp.floor(exponent * 0.5)
        ordered = jnp.where(exponent - 2.0 * rest > 0.5, ordered * 2.0 ** (1 << bit), ordered)
        exponent = rest
    ranks[...] = jnp.where(hit, NAN, ordered)
    ranks_t[...] = ranks[...].T

    own = pl.ds(pl.multiple_of(x * HX, HX), HX)

    for one in loads[3:]:
        one.wait()
    for one in later:
        one.start()

    def partial(to_x):
        rows = pl.ds(pl.multiple_of(to_x * HX, HX), HX)
        shared = dot_t(onehot[rows, :], onehot[own, :])
        apart = jnp.where(shared > 0.0, 0.0, 1.0).astype(jnp.bfloat16)
        minus = -apart
        zero = jnp.zeros((HX, HX), jnp.bfloat16)
        total = jnp.zeros((HX, SL), jnp.float32)
        for pair in range(NB // 2):
            sides = []
            for b in (2 * pair, 2 * pair + 1):
                mine = jnp.broadcast_to(ranks_t[rows, b : b + 1].astype(jnp.bfloat16), (HX, HX))
                theirs = jnp.broadcast_to(ranks[b : b + 1, own].astype(jnp.bfloat16), (HX, HX))
                sides.append(jnp.where(theirs < mine, apart, jnp.where(theirs > mine, minus, zero)))
            total += jnp.dot(
                jnp.concatenate(sides, axis=1),
                reach[2 * HX * pair : 2 * HX * (pair + 1), :],
                preferred_element_type=jnp.float32,
            )
        return jnp.round(total * SCALE).astype(jnp.int32).astype(jnp.int16)

    def half_rows(part):
        return pl.ds(part * HH, HH)

    def copy_r(part):
        return copy(
            out1.at[hop_x(0), pl.ds(0, 2), half_rows(part)],
            relay.at[part],
            send_r.at[part],
            recv_r.at[part],
            device(z, j, hop_x(2 - part)),
        )

    def copy1(i, other, part):
        to_x, to_y, way = hop_x(i), (y_lo + other) % 2, 2 - i
        return copy(
            out1.at[to_x, to_y, half_rows(part)],
            in_x.at[way, y_lo, half_rows(part)],
            send1.at[way, other, part],
            recv1.at[way, y_lo, part],
            device(z, to_y * NL + depth, to_x),
        )

    copy_y = copy(
        out1.at[x, 1 - y_lo], in_y, send_r.at[2], recv_r.at[2], device(z, (1 - y_lo) * NL + depth, x)
    )

    @pl.loop(0, NX)
    def _(i):
        to_x = hop_x(i)
        out1[to_x] = partial(to_x).reshape(2, HY, SL)

        @pl.when(i == 0)
        def _():
            pl.semaphore_wait(barrier, ROW_PEERS + NL - 1 + len(GREET))
            for dz in (2, -2):
                pl.semaphore_signal(
                    know.at[0], inc=1, device_id=device(along(dz), j, x), device_id_type=MESH
                )
            copy_r(0).start()
            copy_r(1).start()

        @pl.when(i == 1)
        def _():
            copy1(1, 1, 0).start()
            copy1(1, 0, 0).start()

        @pl.when(i == 2)
        def _():
            copy1(2, 1, 1).start()
            copy1(2, 0, 1).start()

    copy_y.start()
    for i, part in ((1, 1), (2, 0)):
        copy_r(part).wait_recv()
        to_x = hop_x(i)
        both_rows = slice(part * HH, part * HH + HH)
        here = out1[to_x, :, both_rows, :].astype(jnp.int32)
        out1[to_x, :, both_rows, :] = (here + relay[part].astype(jnp.int32)).astype(jnp.int16)
        copy1(i, 1, part).start()
        copy1(i, 0, part).start()

    pl.semaphore_wait(know.at[0], 2)
    for dz in (4, -4):
        pl.semaphore_signal(know.at[1], inc=1, device_id=device(along(dz), j, x), device_id_type=MESH)
    for one in later:
        one.wait()

    for half in range(2):
        logit_tiles[:, half, :] = logits[:, half * 128 : half * 128 + 128]

    def depth_peer(step):
        return (depth + step) % NL

    def copy_l(step):
        to = depth_peer(step)
        return copy(
            logit_tiles.at[pl.ds(y_lo * HY + z * HZ, HZ)],
            logit_rows.at[depth],
            send_l.at[step],
            recv_l.at[depth],
            device(z, y_lo * NL + to, x),
        )

    for step in range(1, NL):
        copy_l(step).start()
    logit_rows[depth] = logit_tiles[pl.ds(y_lo * HY + z * HZ, HZ)]

    spread = (
        lax.broadcasted_iota(jnp.int32, (SL // ACT, SL), 0)
        == lax.broadcasted_iota(jnp.int32, (SL // ACT, SL), 1) // ACT
    ).astype(jnp.bfloat16)
    lane = lax.broadcasted_iota(jnp.int32, (NL, SL), 1) % ACT
    counts_wide = jnp.dot(
        counts[...].astype(jnp.float32).astype(jnp.bfloat16), spread, preferred_element_type=jnp.float32
    )
    parents_wide = jnp.dot(
        parents[...].astype(jnp.float32).astype(jnp.bfloat16), spread, preferred_element_type=jnp.float32
    )
    legal[...] = jnp.where(lane.astype(jnp.float32) < counts_wide, 1.0, 0.0)
    parents_wide = jnp.where(lane == 0, parents_wide, -1.0)
    seq = lax.broadcasted_iota(jnp.int32, (SL, SL), 0).astype(jnp.float32)
    for level in range(NL):
        owners[level] = jnp.where(seq == parents_wide[level : level + 1, :], 1.0, 0.0).astype(jnp.bfloat16)

    def plane_rows(way, from_y, part):
        rows = in_x.at[way, from_y, half_rows(part)]
        sem = recv1.at[way, from_y, part]
        copy(rows, rows, send1.at[0, 0, 0], sem, device(z, j, hop_x(1))).wait_recv()
        return in_x[way, from_y, part * HH : part * HH + HH, :].astype(jnp.int32)

    copy_y.wait_recv()
    sums = []
    for part in range(2):
        rows = slice(part * HH, part * HH + HH)
        sums.append(out1[x, y_lo, rows, :].astype(jnp.int32) + in_y[rows, :].astype(jnp.int32))
    for late in range(2):
        for part in range(2):
            for from_y in range(2):
                sums[part] += plane_rows(1 - part if late == 0 else part, from_y, part)
    for part in range(2):
        total2[part * HH : part * HH + HH, :] = sums[part].astype(jnp.float32) * (SCALE_PLANE / SCALE)
    for to_z in range(NZ):
        rows = total2[to_z * HZ : (to_z + 1) * HZ, :]
        rows = jnp.round(jnp.concatenate([rows[:, :128], rows[:, 128:]], axis=0))
        out2[to_z] = rows.astype(jnp.int32).astype(jnp.int16)

    pl.semaphore_wait(know.at[1], 2)

    def copy2(i):
        dz = FAR_FIRST[i]
        return copy(
            out2.at[along(dz)], in2.at[i], send2.at[i], recv2.at[i], device(along(dz), j, x)
        )

    for i in range(NZ - 1):
        copy2(i).start()

    rows16[...] = jnp.zeros((PAD, SX), jnp.float32)
    logit16[...] = jnp.zeros((PAD, SX), jnp.float32)
    for step in range(1, NL):
        slot = depth_peer(step)
        copy(
            logit_rows.at[slot], logit_rows.at[slot], send_l.at[0], recv_l.at[slot], device(z, j, (x + 1) % NX)
        ).wait_recv()
    for group in range(8):
        logit16[0:HZ, group * 128 : (group + 1) * 128] = logit_rows[group // 2, :, group % 2, :]

    total = out2[z].astype(jnp.int32)
    for i in range(NZ - 2, -1, -1):
        copy2(i).wait_recv()
        total += in2[i].astype(jnp.int32)
    halves[0 : 2 * HZ, :] = total.astype(jnp.float32)
    halves[2 * HZ :, :] = jnp.zeros((8, 128), jnp.float32)
    counter = jnp.concatenate([halves[0:PAD, :], halves[HZ : HZ + PAD, :]], axis=1)
    high = counter.astype(jnp.bfloat16).astype(jnp.float32)
    both = jnp.concatenate([high, counter - high], axis=0).astype(jnp.bfloat16)

    def copy5(pair, step):
        return copy(
            out5.at[pair],
            in5.at[step, pair],
            send5.at[pair, step],
            recv5.at[pair, step],
            device(z, y_lo * NL + depth_peer(step), x),
        )

    for pair in (1, 0):
        cols = slice(pair * 2 * SL, (pair + 1) * 2 * SL)
        part = jnp.dot(both, pay[:, cols], preferred_element_type=jnp.float32)
        part = (part[:PAD] + part[PAD:]) * (1.0 / SCALE_PLANE)
        for group in range(4):
            out5[pair, :, group, :] = part[:HZ, group * 128 : (group + 1) * 128]
        for step in (2, 1, 3):
            copy5(pair, step).start()

    incoming = jnp.zeros((PAD, SL), jnp.float32)
    for level in range(NL - 1, -1, -1):
        cols = slice(level * SL, (level + 1) * SL)
        if level % 2:
            pair = level // 2
            for step in range(1, NL):
                copy5(pair, step).wait_recv()
            in5[0, pair] = out5[pair] + in5[1, pair] + in5[2, pair] + in5[3, pair]
            for group in range(4):
                at = pair * 2 * SL + group * 128
                rows16[0:HZ, at : at + 128] = in5[0, pair, :, group, :]
        shift = rows16[:, cols] + incoming
        out3[level, :, 0, :] = shift[:HZ, :128]
        out3[level, :, 1, :] = shift[:HZ, 128:]
        if level:
            value = first_value(logit16[:, cols] + shift, legal[level : level + 1, :])
            incoming = hand_down(value, owners[level])

    in3[0] = out3[depth]

    def copy3(source, dz):
        slot = PLACES.index(source)
        there = PLACES.index((source - dz + 7) % NZ - 7)
        return copy(in3.at[slot], in3.at[there], send3.at[there], recv3.at[there], device(along(dz), j, x))

    def wait3(source):
        slot = PLACES.index(source)
        copy(in3.at[slot], in3.at[slot], send3.at[slot], recv3.at[slot], device(along(1), j, x)).wait_recv()

    straight = [copy3(0, dz) for dz in (HUB, -HUB) + NEAR]
    onward = [copy3(-HUB, k - HUB) for k in UP]
    onward_down = [copy3(HUB, k + HUB) for k in DOWN]
    for one in straight:
        one.start()
    wait3(-HUB)
    for one in onward:
        one.start()
    wait3(HUB)
    for one in onward_down:
        one.start()

    def copy4(part):
        slots = pl.ds(PARTS[part][0], PARTS[part][1] - PARTS[part][0])
        return copy(
            in3.at[slots],
            in4.at[slots],
            send4.at[part],
            recv4.at[part],
            device(z, (1 - y_lo) * NL + depth, x),
        )

    def place(block, half, slot):
        shifts[pl.ds(half * HY + along(PLACES[slot]) * HZ, HZ)] = block[slot]

    for part, (begin, end) in enumerate(PARTS):
        for slot in range(begin, end):
            if PLACES[slot] not in (0, HUB, -HUB):
                wait3(PLACES[slot])
        copy4(part).start()
        for slot in range(begin, end):
            place(in3, y_lo, slot)
    def half_scores(half):
        rows = pl.ds(half * HY, HY)
        here = logits[pl.ds(pl.multiple_of(half * HY, HY), HY), :]
        return here + jnp.concatenate([shifts[rows, 0, :], shifts[rows, 1, :]], axis=1)

    can = legal[pl.ds(depth, 1), :]
    own_legal[...] = jnp.broadcast_to(can, (8, SL))
    own_owner[...] = owners[depth]
    here = half_scores(y_lo)
    value = group_value(here, can)
    own_policy[...] = jnp.where(can > 0.0, here - value, 0.0)
    own_passed[...] = hand_down(value, owners[depth])

    for part, (begin, end) in enumerate(PARTS):
        copy4(part).wait_recv()
        for slot in range(begin, end):
            place(in4, 1 - y_lo, slot)
    scores[...] = half_scores(1 - y_lo)

    for part in range(2):
        copy_r(part).wait_send()
        for other in range(2):
            copy1(1, other, part).wait_send()
            copy1(2, other, part).wait_send()
    copy_y.wait_send()
    for i in range(NZ - 1):
        copy2(i).wait_send()
    for step in range(1, NL):
        copy5(0, step).wait_send()
        copy5(1, step).wait_send()
        copy_l(step).wait_send()
    for one in straight + onward + onward_down:
        one.wait_send()

    for part in range(len(PARTS)):
        copy4(part).wait_send()


def last_pass(scores, own_policy, own_passed, legal, owner, policy_hbm, passed_hbm, policy, passed, stores):
    y_lo = lax.axis_index("board") % 2

    def store(src, dst, half, first, count, sem):
        rows = pl.ds(pl.multiple_of(half * HY + first, 8), count)
        one = pltpu.make_async_copy(src.at[pl.ds(first, count)], dst.at[rows], sem)
        one.start()
        return one

    copies = [
        store(own_policy, policy_hbm, y_lo, 0, HY, stores.at[0, CHUNKS]),
        store(own_passed, passed_hbm, y_lo, 0, HY, stores.at[1, CHUNKS]),
    ]
    can = legal[0:1, :]
    count = HY // CHUNKS
    for i in range(CHUNKS):
        rows = pl.ds(i * count, count)
        value = group_value(scores[rows, :], can)
        policy[rows, :] = jnp.where(can > 0.0, scores[rows, :] - value, 0.0)
        copies.append(store(policy, policy_hbm, 1 - y_lo, i * count, count, stores.at[0, i]))
        passed[rows, :] = hand_down(value, owner[...])
        copies.append(store(passed, passed_hbm, 1 - y_lo, i * count, count, stores.at[1, i]))
    for one in copies:
        one.wait()


def local(reach, payoff, board_cards, hand_rank, logits, action_counts, parent_seq):
    table, onehot = hand_cards()
    vmem = pl.BlockSpec(memory_space=pltpu.VMEM)
    dma = pltpu.SemaphoreType.DMA
    f32, bf16, i16 = jnp.float32, jnp.bfloat16, jnp.int16
    rest = pl.pallas_call(
        kernel,
        name="prox",
        out_shape=(
            jax.ShapeDtypeStruct((HY, SL), f32),
            jax.ShapeDtypeStruct((HY, SL), f32),
            jax.ShapeDtypeStruct((HY, SL), f32),
            jax.ShapeDtypeStruct((8, SL), f32),
            jax.ShapeDtypeStruct((SL, SL), bf16),
        ),
        in_specs=[pl.BlockSpec(memory_space=pl.ANY)] * 9,
        out_specs=(vmem,) * 5,
        scratch_shapes=[
            pltpu.VMEM((NB * HX, SL), bf16),
            pltpu.VMEM((NB, 5), jnp.int32),
            pltpu.VMEM((NB, HANDS), jnp.int32),
            pltpu.VMEM((HX, SL), f32),
            pltpu.VMEM((NL, SL // ACT), jnp.int32),
            pltpu.VMEM((NL, SL // ACT), jnp.int32),
            pltpu.VMEM((8, HP), f32),
            pltpu.VMEM((HP, 128), bf16),
            dma((NB + 8,)),
            pltpu.VMEM((NB, HP), f32),
            pltpu.VMEM((HP, NB), f32),
            pltpu.VMEM((NX, 2, HY, SL), i16),
            pltpu.VMEM((2, 2, HH, SL), i16),
            pltpu.VMEM((2, 2, HY, SL), i16),
            pltpu.VMEM((HY, SL), i16),
            pltpu.VMEM((NZ, 2 * HZ, 128), i16),
            pltpu.VMEM((NZ - 1, 2 * HZ, 128), i16),
            pltpu.VMEM((PAD, SX), f32),
            pltpu.VMEM((PAD, SX), f32),
            pltpu.VMEM((SL, SX), bf16),
            pltpu.VMEM((HX, 2, 128), f32),
            pltpu.VMEM((NL, HZ, 2, 128), f32),
            pltpu.VMEM((HY, SL), f32),
            pltpu.VMEM((2 * HZ + 8, 128), f32),
            pltpu.VMEM((2, HZ, 4, 128), f32),
            pltpu.VMEM((NL, 2, HZ, 4, 128), f32),
            pltpu.VMEM((NL, HZ, 2, 128), f32),
            pltpu.VMEM((NZ, HZ, 2, 128), f32),
            pltpu.VMEM((NZ, HZ, 2, 128), f32),
            pltpu.VMEM((HX, 2, 128), f32),
            pltpu.VMEM((NL, SL), f32),
            pltpu.VMEM((NL, SL, SL), bf16),
            dma((2, 2, 2)),
            dma((2, 2, 2)),
            dma((3,)),
            dma((3,)),
            dma((NZ - 1,)),
            dma((NZ - 1,)),
            dma((NZ,)),
            dma((NZ,)),
            dma((len(PARTS),)),
            dma((len(PARTS),)),
            dma((2, NL)),
            dma((2, NL)),
            dma((NL,)),
            dma((NL,)),
            pltpu.SemaphoreType.REGULAR((2,)),
        ],
        compiler_params=pltpu.CompilerParams(
            collective_id=0, has_side_effects=True, vmem_limit_bytes=32 * 1024 * 1024
        ),
    )(
        *[
            pltpu.with_memory_space_constraint(operand, pltpu.HBM)
            for operand in (
                reach.reshape(NB * HX, SL),
                payoff,
                board_cards,
                hand_rank,
                logits,
                action_counts,
                parent_seq,
                jnp.asarray(table),
                jnp.asarray(onehot, jnp.bfloat16),
            )
        ]
    )
    hbm = pl.BlockSpec(memory_space=pl.ANY)
    return pl.pallas_call(
        last_pass,
        name="last_pass",
        out_shape=(jax.ShapeDtypeStruct((HX, SL), f32), jax.ShapeDtypeStruct((HX, SL), f32)),
        in_specs=[vmem] * 5,
        out_specs=(hbm, hbm),
        scratch_shapes=[pltpu.VMEM((HY, SL), f32), pltpu.VMEM((HY, SL), f32), dma((2, CHUNKS + 1))],
        compiler_params=pltpu.CompilerParams(vmem_limit_bytes=32 * 1024 * 1024),
    )(*rest)


def solution(mesh):
    return jax.shard_map(
        local,
        mesh=mesh,
        in_specs=(
            P("board", "hand", "depth"),
            P("depth", None),
            P("board", None),
            P("board", None),
            P("hand", "depth"),
            P(),
            P(),
        ),
        out_specs=(P("hand", "depth"), P("hand", "depth")),
        check_vma=False,
    )
```

```python
import jax
import jax.numpy as jnp
import numpy as np
from jax import lax
from jax.experimental import pallas as pl
from jax.experimental.pallas import tpu as pltpu
from jax.sharding import PartitionSpec as P

CARDS = 52
HANDS = 1326
ACT = 4
NZ = 16
NX = 4
NL = 4
HX = 384
HP = NX * HX
HY = HX // 2
HH = HY // 2
HZ = HY // NZ
PAD = 16
SL = 256
SX = NL * SL
NB = 8
BOUND = float(2 * NB * HX)
SCALE = 32700.0 / BOUND
LIVE = 45 * 44 // 2
BOUND_PLANE = float(2 * NB * LIVE)
SCALE_PLANE = 32700.0 / BOUND_PLANE
MESH = pl.DeviceIdType.MESH
NEAR = (1, -1, 2, -2)
UP = (3, 4, 6, 7, 8)
DOWN = (-3, -4, -6, -7)
HUB = 5
FAR_FIRST = (8, 7, -7, 6, -6, 5, -5, 4, -4, 3, -3, 2, -2, 1, -1)
GREET = (1, -1, 2, -2)
PLACES = (0, 1, -1, 2, -2, 5, -5, -3, -4, -6, -7, 3, 4, 6, 7, 8)
PARTS = ((0, 7), (7, 11), (11, 16))
ROW_PEERS = 5
CHUNKS = 2
NAN = float("nan")


def hand_cards():
    first, second = np.triu_indices(CARDS, 1)
    table = np.full((8, HP), -1.0, np.float32)
    table[0, :HANDS] = first
    table[1, :HANDS] = second
    onehot = np.zeros((HP, 128), np.float32)
    onehot[np.arange(HANDS), first] = 1.0
    onehot[np.arange(HANDS), second] = 1.0
    return table, onehot


def dot_t(a, b):
    return lax.dot_general(a, b, (((1,), (1,)), ((), ())), preferred_element_type=jnp.float32)


def group_reduce(x, op):
    lane = lax.broadcasted_iota(jnp.int32, x.shape, 1)
    near = jnp.where(lane % 2 == 0, pltpu.roll(x, 127, 1), pltpu.roll(x, 1, 1))
    x = op(x, near)
    far = jnp.where(lane % 4 < 2, pltpu.roll(x, 126, 1), pltpu.roll(x, 2, 1))
    return op(x, far)


def group_value(scores, legal):
    parts = []
    for half in range(2):
        cols = slice(half * 128, half * 128 + 128)
        masked = jnp.where(legal[:, cols] > 0.0, scores[:, cols], -jnp.inf)
        top = group_reduce(masked, jnp.maximum)
        total = group_reduce(jnp.exp(masked - top), jnp.add)
        parts.append(top + jnp.log(total))
    return jnp.concatenate(parts, axis=1)


def first_value(scores, legal):
    parts = []
    for half in range(2):
        cols = slice(half * 128, half * 128 + 128)
        slots = [jnp.where(legal[:, cols] > 0.0, scores[:, cols], -jnp.inf)]
        slots += [pltpu.roll(slots[0], 128 - step, 1) for step in range(1, ACT)]
        top = jnp.maximum(jnp.maximum(slots[0], slots[1]), jnp.maximum(slots[2], slots[3]))
        terms = [jnp.exp(slot - top) for slot in slots]
        parts.append(top + jnp.log((terms[0] + terms[1]) + (terms[2] + terms[3])))
    return jnp.concatenate(parts, axis=1)


def hand_down(value, owner_t):
    a = value.astype(jnp.bfloat16)
    rest = value - a.astype(jnp.float32)
    b = rest.astype(jnp.bfloat16)
    c = (rest - b.astype(jnp.float32)).astype(jnp.bfloat16)
    if value.shape[0] > 2 * PAD:
        return dot_t(a, owner_t) + dot_t(b, owner_t) + dot_t(c, owner_t)
    all_parts = dot_t(jnp.concatenate([a, b, c], axis=0), owner_t)
    return all_parts[:PAD] + all_parts[PAD : 2 * PAD] + all_parts[2 * PAD :]


def kernel(
    reach_hbm,
    payoff,
    cards_hbm,
    rank_hbm,
    logits_hbm,
    counts_hbm,
    parents_hbm,
    table_hbm,
    onehot_hbm,
    scores,
    own_policy,
    own_passed,
    own_legal,
    own_owner,
    reach,
    cards,
    rank,
    logits,
    counts,
    parents,
    table,
    onehot,
    load,
    ranks,
    ranks_t,
    out1,
    relay,
    in_x,
    in_y,
    out2,
    in2,
    rows16,
    logit16,
    pay,
    logit_tiles,
    logit_rows,
    total2,
    out5,
    in5,
    out3,
    in3,
    in4,
    shifts,
    legal,
    owners,
    send1,
    recv1,
    send_r,
    recv_r,
    send2,
    recv2,
    send3,
    recv3,
    send4,
    recv4,
    send5,
    recv5,
    send_l,
    recv_l,
    know,
):
    board = lax.axis_index("board")
    depth = lax.axis_index("depth")
    x = lax.axis_index("hand")
    z = board // 2
    y_lo = board % 2
    j = y_lo * NL + depth

    def device(to_z, to_j, to_x):
        return (to_z * 2 + to_j // NL, to_j % NL, to_x)

    def along(dz):
        return (z + dz + NZ) % NZ

    def copy(src, dst, send, recv, to):
        return pltpu.make_async_remote_copy(
            src_ref=src, dst_ref=dst, send_sem=send, recv_sem=recv, device_id=to, device_id_type=MESH
        )

    def loaded(i, src, dst):
        return pltpu.make_async_copy(src, dst, load.at[i])

    loads = [
        loaded(0, rank_hbm, rank),
        loaded(1, cards_hbm, cards),
        loaded(2, table_hbm, table),
        loaded(3, onehot_hbm, onehot),
    ]
    for b in range(NB):
        rows = pl.ds(b * HX, HX)
        loads.append(loaded(4 + b, reach_hbm.at[rows], reach.at[rows]))
    later = [
        loaded(4 + NB, logits_hbm, logits),
        loaded(5 + NB, counts_hbm, counts),
        loaded(6 + NB, parents_hbm, parents),
        loaded(7 + NB, payoff, pay),
    ]
    for one in loads:
        one.start()

    def hop_x(i):
        return (x + 2 + i + i * (i - 1) // 2) % NX

    barrier = pltpu.get_barrier_semaphore()
    for i in (1, 2):
        for other in range(2):
            to_j = (y_lo + other) % 2 * NL + depth
            pl.semaphore_signal(barrier, inc=1, device_id=device(z, to_j, hop_x(i)), device_id_type=MESH)
    to_j = (1 - y_lo) * NL + depth
    pl.semaphore_signal(barrier, inc=1, device_id=device(z, to_j, x), device_id_type=MESH)
    for step in range(1, NL):
        to_j = y_lo * NL + (depth + step) % NL
        pl.semaphore_signal(barrier, inc=1, device_id=device(z, to_j, x), device_id_type=MESH)
    for dz in GREET:
        pl.semaphore_signal(barrier, inc=1, device_id=device(along(dz), j, x), device_id_type=MESH)

    for one in loads[:3]:
        one.wait()

    ranks[...] = jnp.full((NB, HP), NAN, jnp.float32)
    ranks[:, :HANDS] = rank[...].astype(jnp.float32)
    first = table[0:1, :]
    second = table[1:2, :]
    hit = first < 0.0
    for card in range(5):
        one = cards[:, card : card + 1].astype(jnp.float32)
        hit = hit | (first == one) | (second == one)
    left = ranks[...]
    exponent = jnp.floor(left * (1.0 / 128.0))
    ordered = (1.0 + (left - exponent * 128.0) * (1.0 / 128.0)) * 2.0**-29
    for bit in range(6):
        rest = jnp.floor(exponent * 0.5)
        ordered = jnp.where(exponent - 2.0 * rest > 0.5, ordered * 2.0 ** (1 << bit), ordered)
        exponent = rest
    ranks[...] = jnp.where(hit, NAN, ordered)
    ranks_t[...] = ranks[...].T

    own = pl.ds(pl.multiple_of(x * HX, HX), HX)

    for one in loads[3:]:
        one.wait()
    for one in later:
        one.start()

    def partial(to_x):
        rows = pl.ds(pl.multiple_of(to_x * HX, HX), HX)
        shared = dot_t(onehot[rows, :], onehot[own, :])
        apart = jnp.where(shared > 0.0, 0.0, 1.0).astype(jnp.bfloat16)
        minus = -apart
        zero = jnp.zeros((HX, HX), jnp.bfloat16)
        total = jnp.zeros((HX, SL), jnp.float32)
        for pair in range(NB // 2):
            sides = []
            for b in (2 * pair, 2 * pair + 1):
                mine = jnp.broadcast_to(ranks_t[rows, b : b + 1].astype(jnp.bfloat16), (HX, HX))
                theirs = jnp.broadcast_to(ranks[b : b + 1, own].astype(jnp.bfloat16), (HX, HX))
                sides.append(jnp.where(theirs < mine, apart, jnp.where(theirs > mine, minus, zero)))
            total += jnp.dot(
                jnp.concatenate(sides, axis=1),
                reach[2 * HX * pair : 2 * HX * (pair + 1), :],
                preferred_element_type=jnp.float32,
            )
        return jnp.round(total * SCALE).astype(jnp.int32).astype(jnp.int16)

    def half_rows(part):
        return pl.ds(part * HH, HH)

    def copy_r(part):
        return copy(
            out1.at[hop_x(0), pl.ds(0, 2), half_rows(part)],
            relay.at[part],
            send_r.at[part],
            recv_r.at[part],
            device(z, j, hop_x(2 - part)),
        )

    def copy1(i, other, part):
        to_x, to_y, way = hop_x(i), (y_lo + other) % 2, 2 - i
        return copy(
            out1.at[to_x, to_y, half_rows(part)],
            in_x.at[way, y_lo, half_rows(part)],
            send1.at[way, other, part],
            recv1.at[way, y_lo, part],
            device(z, to_y * NL + depth, to_x),
        )

    copy_y = copy(
        out1.at[x, 1 - y_lo], in_y, send_r.at[2], recv_r.at[2], device(z, (1 - y_lo) * NL + depth, x)
    )

    @pl.loop(0, NX)
    def _(i):
        to_x = hop_x(i)
        out1[to_x] = partial(to_x).reshape(2, HY, SL)

        @pl.when(i == 0)
        def _():
            pl.semaphore_wait(barrier, ROW_PEERS + NL - 1 + len(GREET))
            for dz in (2, -2):
                pl.semaphore_signal(
                    know.at[0], inc=1, device_id=device(along(dz), j, x), device_id_type=MESH
                )
            copy_r(0).start()
            copy_r(1).start()

        @pl.when(i == 1)
        def _():
            copy1(1, 1, 0).start()
            copy1(1, 0, 0).start()

        @pl.when(i == 2)
        def _():
            copy1(2, 1, 1).start()
            copy1(2, 0, 1).start()

    copy_y.start()
    for i, part in ((1, 1), (2, 0)):
        copy_r(part).wait_recv()
        to_x = hop_x(i)
        both_rows = slice(part * HH, part * HH + HH)
        here = out1[to_x, :, both_rows, :].astype(jnp.int32)
        out1[to_x, :, both_rows, :] = (here + relay[part].astype(jnp.int32)).astype(jnp.int16)
        copy1(i, 1, part).start()
        copy1(i, 0, part).start()

    pl.semaphore_wait(know.at[0], 2)
    for dz in (4, -4):
        pl.semaphore_signal(know.at[1], inc=1, device_id=device(along(dz), j, x), device_id_type=MESH)
    for one in later:
        one.wait()

    for half in range(2):
        logit_tiles[:, half, :] = logits[:, half * 128 : half * 128 + 128]

    def depth_peer(step):
        return (depth + step) % NL

    def copy_l(step):
        to = depth_peer(step)
        return copy(
            logit_tiles.at[pl.ds(y_lo * HY + z * HZ, HZ)],
            logit_rows.at[depth],
            send_l.at[step],
            recv_l.at[depth],
            device(z, y_lo * NL + to, x),
        )

    for step in range(1, NL):
        copy_l(step).start()
    logit_rows[depth] = logit_tiles[pl.ds(y_lo * HY + z * HZ, HZ)]

    spread = (
        lax.broadcasted_iota(jnp.int32, (SL // ACT, SL), 0)
        == lax.broadcasted_iota(jnp.int32, (SL // ACT, SL), 1) // ACT
    ).astype(jnp.bfloat16)
    lane = lax.broadcasted_iota(jnp.int32, (NL, SL), 1) % ACT
    counts_wide = jnp.dot(
        counts[...].astype(jnp.float32).astype(jnp.bfloat16), spread, preferred_element_type=jnp.float32
    )
    parents_wide = jnp.dot(
        parents[...].astype(jnp.float32).astype(jnp.bfloat16), spread, preferred_element_type=jnp.float32
    )
    legal[...] = jnp.where(lane.astype(jnp.float32) < counts_wide, 1.0, 0.0)
    parents_wide = jnp.where(lane == 0, parents_wide, -1.0)
    seq = lax.broadcasted_iota(jnp.int32, (SL, SL), 0).astype(jnp.float32)
    for level in range(NL):
        owners[level] = jnp.where(seq == parents_wide[level : level + 1, :], 1.0, 0.0).astype(jnp.bfloat16)

    def plane_rows(way, from_y, part):
        rows = in_x.at[way, from_y, half_rows(part)]
        sem = recv1.at[way, from_y, part]
        copy(rows, rows, send1.at[0, 0, 0], sem, device(z, j, hop_x(1))).wait_recv()
        return in_x[way, from_y, part * HH : part * HH + HH, :].astype(jnp.int32)

    copy_y.wait_recv()
    sums = []
    for part in range(2):
        rows = slice(part * HH, part * HH + HH)
        sums.append(out1[x, y_lo, rows, :].astype(jnp.int32) + in_y[rows, :].astype(jnp.int32))
    for late in range(2):
        for part in range(2):
            for from_y in range(2):
                sums[part] += plane_rows(1 - part if late == 0 else part, from_y, part)
    total2[HY:, :] = jnp.zeros((8, SL), jnp.float32)
    for part in range(2):
        total2[part * HH : part * HH + HH, :] = sums[part].astype(jnp.float32) * (SCALE_PLANE / SCALE)
    for to_z in range(NZ):
        rows = jnp.round(total2[to_z * HZ : to_z * HZ + PAD, :])
        out2[to_z] = rows.astype(jnp.int32).astype(jnp.int16)

    pl.semaphore_wait(know.at[1], 2)

    def copy2(i):
        dz = FAR_FIRST[i]
        return copy(
            out2.at[along(dz)], in2.at[i], send2.at[i], recv2.at[i], device(along(dz), j, x)
        )

    for i in range(NZ - 1):
        copy2(i).start()

    rows16[...] = jnp.zeros((PAD, SX), jnp.float32)
    logit16[...] = jnp.zeros((PAD, SX), jnp.float32)
    for step in range(1, NL):
        slot = depth_peer(step)
        copy(
            logit_rows.at[slot], logit_rows.at[slot], send_l.at[0], recv_l.at[slot], device(z, j, (x + 1) % NX)
        ).wait_recv()
    for group in range(8):
        logit16[0:HZ, group * 128 : (group + 1) * 128] = logit_rows[group // 2, :, group % 2, :]

    total = out2[z].astype(jnp.int32)
    for i in range(NZ - 2, -1, -1):
        copy2(i).wait_recv()
        total += in2[i].astype(jnp.int32)
    counter = total.astype(jnp.float32)
    high = counter.astype(jnp.bfloat16).astype(jnp.float32)
    both = jnp.concatenate([high, counter - high], axis=0).astype(jnp.bfloat16)

    def copy5(pair, step):
        return copy(
            out5.at[pair],
            in5.at[step, pair],
            send5.at[pair, step],
            recv5.at[pair, step],
            device(z, y_lo * NL + depth_peer(step), x),
        )

    for pair in (1, 0):
        cols = slice(pair * 2 * SL, (pair + 1) * 2 * SL)
        part = jnp.dot(both, pay[:, cols], preferred_element_type=jnp.float32)
        part = (part[:PAD] + part[PAD:]) * (1.0 / SCALE_PLANE)
        for group in range(4):
            out5[pair, :, group, :] = part[:HZ, group * 128 : (group + 1) * 128]
        for step in (2, 1, 3):
            copy5(pair, step).start()

    incoming = jnp.zeros((PAD, SL), jnp.float32)
    for level in range(NL - 1, -1, -1):
        cols = slice(level * SL, (level + 1) * SL)
        if level % 2:
            pair = level // 2
            for step in range(1, NL):
                copy5(pair, step).wait_recv()
            in5[0, pair] = out5[pair] + in5[1, pair] + in5[2, pair] + in5[3, pair]
            for group in range(4):
                at = pair * 2 * SL + group * 128
                rows16[0:HZ, at : at + 128] = in5[0, pair, :, group, :]
        shift = rows16[:, cols] + incoming
        out3[level, :, 0, :] = shift[:HZ, :128]
        out3[level, :, 1, :] = shift[:HZ, 128:]
        if level:
            value = first_value(logit16[:, cols] + shift, legal[level : level + 1, :])
            incoming = hand_down(value, owners[level])

    in3[0] = out3[depth]

    def copy3(source, dz):
        slot = PLACES.index(source)
        there = PLACES.index((source - dz + 7) % NZ - 7)
        return copy(in3.at[slot], in3.at[there], send3.at[there], recv3.at[there], device(along(dz), j, x))

    def wait3(source):
        slot = PLACES.index(source)
        copy(in3.at[slot], in3.at[slot], send3.at[slot], recv3.at[slot], device(along(1), j, x)).wait_recv()

    straight = [copy3(0, dz) for dz in (HUB, -HUB) + NEAR]
    onward = [copy3(-HUB, k - HUB) for k in UP]
    onward_down = [copy3(HUB, k + HUB) for k in DOWN]
    for one in straight:
        one.start()
    wait3(-HUB)
    for one in onward:
        one.start()
    wait3(HUB)
    for one in onward_down:
        one.start()

    def copy4(part):
        slots = pl.ds(PARTS[part][0], PARTS[part][1] - PARTS[part][0])
        return copy(
            in3.at[slots],
            in4.at[slots],
            send4.at[part],
            recv4.at[part],
            device(z, (1 - y_lo) * NL + depth, x),
        )

    def place(block, half, slot):
        shifts[pl.ds(half * HY + along(PLACES[slot]) * HZ, HZ)] = block[slot]

    for part, (begin, end) in enumerate(PARTS):
        for slot in range(begin, end):
            if PLACES[slot] not in (0, HUB, -HUB):
                wait3(PLACES[slot])
        copy4(part).start()
        for slot in range(begin, end):
            place(in3, y_lo, slot)
    def half_scores(half):
        rows = pl.ds(half * HY, HY)
        here = logits[pl.ds(pl.multiple_of(half * HY, HY), HY), :]
        return here + jnp.concatenate([shifts[rows, 0, :], shifts[rows, 1, :]], axis=1)

    can = legal[pl.ds(depth, 1), :]
    own_legal[...] = jnp.broadcast_to(can, (8, SL))
    own_owner[...] = owners[depth]
    here = half_scores(y_lo)
    value = group_value(here, can)
    own_policy[...] = jnp.where(can > 0.0, here - value, 0.0)
    own_passed[...] = hand_down(value, owners[depth])

    for part, (begin, end) in enumerate(PARTS):
        copy4(part).wait_recv()
        for slot in range(begin, end):
            place(in4, 1 - y_lo, slot)
    scores[...] = half_scores(1 - y_lo)

    for part in range(2):
        copy_r(part).wait_send()
        for other in range(2):
            copy1(1, other, part).wait_send()
            copy1(2, other, part).wait_send()
    copy_y.wait_send()
    for i in range(NZ - 1):
        copy2(i).wait_send()
    for step in range(1, NL):
        copy5(0, step).wait_send()
        copy5(1, step).wait_send()
        copy_l(step).wait_send()
    for one in straight + onward + onward_down:
        one.wait_send()

    for part in range(len(PARTS)):
        copy4(part).wait_send()


def last_pass(scores, own_policy, own_passed, legal, owner, policy_hbm, passed_hbm, policy, passed, stores):
    y_lo = lax.axis_index("board") % 2

    def store(src, dst, half, first, count, sem):
        rows = pl.ds(pl.multiple_of(half * HY + first, 8), count)
        one = pltpu.make_async_copy(src.at[pl.ds(first, count)], dst.at[rows], sem)
        one.start()
        return one

    copies = [
        store(own_policy, policy_hbm, y_lo, 0, HY, stores.at[0, CHUNKS]),
        store(own_passed, passed_hbm, y_lo, 0, HY, stores.at[1, CHUNKS]),
    ]
    can = legal[0:1, :]
    count = HY // CHUNKS
    for i in range(CHUNKS):
        rows = pl.ds(i * count, count)
        value = group_value(scores[rows, :], can)
        policy[rows, :] = jnp.where(can > 0.0, scores[rows, :] - value, 0.0)
        copies.append(store(policy, policy_hbm, 1 - y_lo, i * count, count, stores.at[0, i]))
        passed[rows, :] = hand_down(value, owner[...])
        copies.append(store(passed, passed_hbm, 1 - y_lo, i * count, count, stores.at[1, i]))
    for one in copies:
        one.wait()


def local(reach, payoff, board_cards, hand_rank, logits, action_counts, parent_seq):
    table, onehot = hand_cards()
    vmem = pl.BlockSpec(memory_space=pltpu.VMEM)
    dma = pltpu.SemaphoreType.DMA
    f32, bf16, i16 = jnp.float32, jnp.bfloat16, jnp.int16
    rest = pl.pallas_call(
        kernel,
        name="prox",
        out_shape=(
            jax.ShapeDtypeStruct((HY, SL), f32),
            jax.ShapeDtypeStruct((HY, SL), f32),
            jax.ShapeDtypeStruct((HY, SL), f32),
            jax.ShapeDtypeStruct((8, SL), f32),
            jax.ShapeDtypeStruct((SL, SL), bf16),
        ),
        in_specs=[pl.BlockSpec(memory_space=pl.ANY)] * 9,
        out_specs=(vmem,) * 5,
        scratch_shapes=[
            pltpu.VMEM((NB * HX, SL), bf16),
            pltpu.VMEM((NB, 5), jnp.int32),
            pltpu.VMEM((NB, HANDS), jnp.int32),
            pltpu.VMEM((HX, SL), f32),
            pltpu.VMEM((NL, SL // ACT), jnp.int32),
            pltpu.VMEM((NL, SL // ACT), jnp.int32),
            pltpu.VMEM((8, HP), f32),
            pltpu.VMEM((HP, 128), bf16),
            dma((NB + 8,)),
            pltpu.VMEM((NB, HP), f32),
            pltpu.VMEM((HP, NB), f32),
            pltpu.VMEM((NX, 2, HY, SL), i16),
            pltpu.VMEM((2, 2, HH, SL), i16),
            pltpu.VMEM((2, 2, HY, SL), i16),
            pltpu.VMEM((HY, SL), i16),
            pltpu.VMEM((NZ, PAD, SL), i16),
            pltpu.VMEM((NZ - 1, PAD, SL), i16),
            pltpu.VMEM((PAD, SX), f32),
            pltpu.VMEM((PAD, SX), f32),
            pltpu.VMEM((SL, SX), bf16),
            pltpu.VMEM((HX, 2, 128), f32),
            pltpu.VMEM((NL, HZ, 2, 128), f32),
            pltpu.VMEM((HY + 8, SL), f32),
            pltpu.VMEM((2, HZ, 4, 128), f32),
            pltpu.VMEM((NL, 2, HZ, 4, 128), f32),
            pltpu.VMEM((NL, HZ, 2, 128), f32),
            pltpu.VMEM((NZ, HZ, 2, 128), f32),
            pltpu.VMEM((NZ, HZ, 2, 128), f32),
            pltpu.VMEM((HX, 2, 128), f32),
            pltpu.VMEM((NL, SL), f32),
            pltpu.VMEM((NL, SL, SL), bf16),
            dma((2, 2, 2)),
            dma((2, 2, 2)),
            dma((3,)),
            dma((3,)),
            dma((NZ - 1,)),
            dma((NZ - 1,)),
            dma((NZ,)),
            dma((NZ,)),
            dma((len(PARTS),)),
            dma((len(PARTS),)),
            dma((2, NL)),
            dma((2, NL)),
            dma((NL,)),
            dma((NL,)),
            pltpu.SemaphoreType.REGULAR((2,)),
        ],
        compiler_params=pltpu.CompilerParams(
            collective_id=0, has_side_effects=True, vmem_limit_bytes=32 * 1024 * 1024
        ),
    )(
        *[
            pltpu.with_memory_space_constraint(operand, pltpu.HBM)
            for operand in (
                reach.reshape(NB * HX, SL),
                payoff,
                board_cards,
                hand_rank,
                logits,
                action_counts,
                parent_seq,
                jnp.asarray(table),
                jnp.asarray(onehot, jnp.bfloat16),
            )
        ]
    )
    hbm = pl.BlockSpec(memory_space=pl.ANY)
    return pl.pallas_call(
        last_pass,
        name="last_pass",
        out_shape=(jax.ShapeDtypeStruct((HX, SL), f32), jax.ShapeDtypeStruct((HX, SL), f32)),
        in_specs=[vmem] * 5,
        out_specs=(hbm, hbm),
        scratch_shapes=[pltpu.VMEM((HY, SL), f32), pltpu.VMEM((HY, SL), f32), dma((2, CHUNKS + 1))],
        compiler_params=pltpu.CompilerParams(vmem_limit_bytes=32 * 1024 * 1024),
    )(*rest)


def solution(mesh):
    return jax.shard_map(
        local,
        mesh=mesh,
        in_specs=(
            P("board", "hand", "depth"),
            P("depth", None),
            P("board", None),
            P("board", None),
            P("hand", "depth"),
            P(),
            P(),
        ),
        out_specs=(P("hand", "depth"), P("hand", "depth")),
        check_vma=False,
    )
```
